128 devices in a mesh: sec: 2 (over y_hi), row: 32 (over x, y_lo, z), col: 2 (over core).
Axes of the slice: x: 4, y: 4 (y_hi: 2, y_lo: 2; y = y_hi * 2 + y_lo), z: 4, core: 2. Of those that a mesh axis runs over, the one named last changes fastest.
Arguments:
- populations: float32 [19, 2048, 256], P(None, ('sec', 'row', 'col')), may hold values from 0.01 to 0.1
- relaxation: float32 [2048, 256], P(('sec', 'row', 'col')), may hold values from 0.6 to 1.9
- send_lists: int32 [128, 32], P(('sec', 'row', 'col')), may hold values from 0 to 31, as said below
- lift_weight: bfloat16 [320, 81], replicated, may hold values from -0.625 to 0.625
- norm_gain: float32 [320], replicated, may hold values from 0.1 to 1.9
- norm_shift: float32 [320], replicated, may hold values from -3 to 3
- mix_master: float32 [1280, 320], P(('row', 'col')), may hold values from -0.3125 to 0.3125
- mix_first: float32 [1280, 320], P(('row', 'col')), may hold values from -1.5 to 1.5
- mix_second: float32 [1280, 320], P(('row', 'col')), may hold values from 0.1 to 1
- out_weight: bfloat16 [3, 320], replicated, may hold values from -0.3125 to 0.3125
Outputs:
- after: float32 [19, 2048, 256], P(None, ('sec', 'row', 'col'))
- new_master: float32 [1280, 320], P(('row', 'col'))
- new_first: float32 [1280, 320], P(('row', 'col'))
- new_second: float32 [1280, 320], P(('row', 'col'))
The draws below stay inside these ranges and needn't reach their ends.
Inputs may be any that keep to these rules, and one draw needn't show every extreme that they name: `send_lists`: within each sec and col index, a device sends exactly 2 of its 32 bricks to each of 16 distinct trainers along row, and every trainer receives exactly 32 bricks.
All inputs are finite; a program needn't handle non-finite values.
Results may differ from the reference program's by a relative error of at most 0.0003.
The reference program's roundings to bfloat16 on the way count: a program that leaves them out, or rounds other values in their place, can miss the bound.
Values may be sent and summed in bfloat16 or wider, within the bound.
No kernel may reach another device: no remote copies, remote signals or barrier semaphores. Data moves between devices by JAX's collectives and lax.ppermute only.
A program may use at most 64 MiB of HBM per device.

```python
import math
import jax
import jax.numpy as jnp
from jax import lax

BRK_X = 4
BRK_Y = 4
BRK_Z = 8
CY = 16
CZ = 16
CYZ = 256
V = 128
BRICKS = 32
CAP = 2
C = 320
LAYERS = 4
NX = 2048
N_SEC = 2
N_ROW = 32
N_COL = 2
DEVICES = 128


def draw_send_lists(key, part):
    key = jax.random.fold_in(key, 7)
    offsets = []
    for member in range(N_SEC * N_COL):
        chosen = jax.random.permutation(jax.random.fold_in(key, 2 * member), N_ROW)[:BRICKS // CAP]
        shuffle = jax.random.permutation(jax.random.fold_in(key, 2 * member + 1), BRICKS)
        offsets.append(chosen[shuffle // CAP])
    offset_table = jnp.stack(offsets).reshape(N_SEC, 1, N_COL, BRICKS).astype(jnp.int32)
    row_index = jnp.arange(N_ROW, dtype=jnp.int32).reshape(1, N_ROW, 1, 1)
    return ((row_index + offset_table) % N_ROW).astype(jnp.int32).reshape(DEVICES, BRICKS)


def levels(rng, dims, cuts, low, largest):
    level = 1.0
    for dim, shards_of in cuts:
        steps = jax.random.uniform(jax.random.fold_in(jax.random.fold_in(rng, 6), dim), (shards_of,), jnp.float32, low / len(cuts), largest / len(cuts))
        level = level * jnp.repeat(jnp.exp(steps), dims[dim] // shards_of).reshape((-1,) + (1,) * (len(dims) - 1 - dim))
    return level


def normal_values(key, shape, width, reach, pieces=(), held_as=jnp.bfloat16):
    values = jax.random.normal(key, shape, jnp.float32) * width
    if len(pieces) > 0:
        values = levels(key, shape, pieces, -0.22, 0.18) * values
    return jnp.clip(values, min=-reach, max=reach).astype(held_as)


def setup_inputs(seed: int = 0) -> dict:
    seeds = jax.random.split(jax.random.key(seed), 11)
    populations = jnp.clip(0.01 + 0.09 * jax.random.uniform(seeds[0], (19, NX, CYZ), jnp.float32) ** levels(seeds[0], (19, NX, CYZ), ((1, 128),), -0.2, 0.2), 0.01, 0.1)
    relaxation = jnp.clip(jnp.exp(math.log(1.9) - 1.1526795 * jax.random.uniform(seeds[1], (NX, CYZ), jnp.float32) ** levels(seeds[1], (NX, CYZ), ((0, 128),), -0.2, 0.2)), 0.6, 1.9)
    send_lists = draw_send_lists(jax.random.fold_in(seeds[10], 71), 0)
    lift_weight = normal_values(seeds[3], (C, 81), 81 ** -0.5, 0.625)
    norm_gain = jnp.clip(1.0 + 0.18 * jax.random.normal(seeds[4], (C,), jnp.float32), 0.1, 1.9)
    norm_shift = normal_values(seeds[5], (C,), 0.5, 3.0, (), jnp.float32)
    mix_master = normal_values(seeds[6], (LAYERS * C, C), C ** -0.5, 0.3125, ((0, 64),), jnp.float32)
    mix_first = normal_values(seeds[7], (LAYERS * C, C), 0.1, 1.5, ((0, 64),), jnp.float32)
    mix_second = jnp.clip(jnp.exp(math.log(1.0) - 2.3025851 * jax.random.uniform(seeds[8], (LAYERS * C, C), jnp.float32) ** levels(seeds[8], (LAYERS * C, C), ((0, 64),), -0.2, 0.2)), 0.1, 1.0)
    out_weight = normal_values(seeds[9], (3, C), C ** -0.5, 0.3125)
    return dict(populations=populations, relaxation=relaxation, send_lists=send_lists, lift_weight=lift_weight, norm_gain=norm_gain, norm_shift=norm_shift, mix_master=mix_master, mix_first=mix_first, mix_second=mix_second, out_weight=out_weight)


VELOCITIES = ((0, 0, 0), (1, 0, 0), (-1, 0, 0), (0, 1, 0), (0, -1, 0), (0, 0, 1), (0, 0, -1), (1, 1, 0), (-1, -1, 0), (1, -1, 0), (-1, 1, 0), (1, 0, 1), (-1, 0, -1), (1, 0, -1), (-1, 0, 1), (0, 1, 1), (0, -1, -1), (0, 1, -1), (0, -1, 1))
LATTICE_WEIGHTS = (1.0 / 3.0,) + (1.0 / 18.0,) * 6 + (1.0 / 36.0,) * 12

def moments(read):
    density = read[0]
    moment_x = jnp.zeros_like(density)
    moment_y = jnp.zeros_like(density)
    moment_z = jnp.zeros_like(density)
    for index in range(1, 19):
        along_x, along_y, along_z = VELOCITIES[index]
        density = density + read[index]
        moment_x = moment_x + along_x * read[index]
        moment_y = moment_y + along_y * read[index]
        moment_z = moment_z + along_z * read[index]
    return (density, (moment_x / density, moment_y / density, moment_z / density))

def collide(read, density, flow, relaxation):
    speed = flow[0] * flow[0] + flow[1] * flow[1] + flow[2] * flow[2]
    result = []
    for index in range(19):
        along_x, along_y, along_z = VELOCITIES[index]
        project = along_x * flow[0] + along_y * flow[1] + along_z * flow[2]
        balance = LATTICE_WEIGHTS[index] * density * (1.0 + 3.0 * project + 4.5 * project * project - 1.5 * speed)
        result.append(read[index] - relaxation * (read[index] - balance))
    return jnp.stack(result)

def gelu_value(value):
    return 0.5 * value * (1.0 + lax.erf(value * 0.7071067811865476))

def gelu_slope(value):
    return 0.5 * (1.0 + lax.erf(value * 0.7071067811865476)) + value * jnp.exp(-0.5 * value * value) * 0.3989422804014327

def unfold(brick):
    inputs = brick[:3].reshape(3, BRK_X, BRK_Y, BRK_Z)
    padded = jnp.pad(inputs, ((0, 0), (1, 1), (1, 1), (1, 1)))
    taps = []
    for shift_x in range(3):
        for shift_y in range(3):
            for shift_z in range(3):
                taps.append(padded[:, shift_x:shift_x + BRK_X, shift_y:shift_y + BRK_Y, shift_z:shift_z + BRK_Z])
    return jnp.stack(taps, axis=1).reshape(81, V)

def brick_sums(brick, lift_weight):
    lifted = jnp.dot(lift_weight, unfold(brick), preferred_element_type=jnp.float32)
    return jnp.stack([lax.optimization_barrier(jnp.sum(lifted, axis=1)), lax.optimization_barrier(jnp.sum(lifted * lifted, axis=1))])

def normalizers(totals):
    count = BRICKS * V
    mean = totals[..., 0, :] / count
    spread = totals[..., 1, :] / count - mean * mean
    return (mean, lax.rsqrt(spread + 1e-05))

def train_bricks(bricks, means, scales, lift_weight, norm_gain, norm_shift, mixing, out_weight):
    layers = mixing.shape[0]

    def one_brick(total, inputs):
        brick, mean, scale = inputs
        lifted = jnp.dot(lift_weight, unfold(brick), preferred_element_type=jnp.float32)
        normed = (lifted - mean[:, None]) * (scale * norm_gain)[:, None] + norm_shift[:, None]
        current = gelu_value(normed).astype(jnp.bfloat16)
        states = []
        befores = []
        for layer in range(layers):
            mixed = jnp.dot(mixing[layer], current, preferred_element_type=jnp.float32)
            states.append(current)
            befores.append(mixed)
            current = (current.astype(jnp.float32) + gelu_value(mixed)).astype(jnp.bfloat16)
        output = jnp.dot(out_weight, current, preferred_element_type=jnp.float32)
        target = brick[3:].astype(jnp.float32)
        delta = ((output - target) * (2.0 / (3.0 * V))).astype(jnp.bfloat16)
        back = lax.dot_general(out_weight, delta, (((0,), (0,)), ((), ())), preferred_element_type=jnp.float32)
        terms = [None] * layers
        for layer in range(layers - 1, -1, -1):
            inner = (back * gelu_slope(befores[layer])).astype(jnp.bfloat16)
            terms[layer] = lax.dot_general(inner, states[layer], (((1,), (1,)), ((), ())), preferred_element_type=jnp.float32)
            if layer > 0:
                back = back + lax.dot_general(mixing[layer], inner, (((0,), (0,)), ((), ())), preferred_element_type=jnp.float32)
        return (total + jnp.stack(terms), None)
    start = jnp.zeros(mixing.shape, jnp.float32)
    total, unused = lax.scan(one_brick, start, (bricks, means, scales))
    return total

def adamw(master, gradient, first, second):
    first_next = 0.9 * first + 0.1 * gradient
    second_next = 0.999 * second + 0.001 * gradient * gradient
    ratio = first_next / (1.0 - 0.9 ** 10) / (jnp.sqrt(second_next / (1.0 - 0.999 ** 10)) + 1e-08)
    return (master - 0.01 * (ratio + 0.1 * master), first_next, second_next)

def reference(populations, relaxation, send_lists, lift_weight, norm_gain, norm_shift, mix_master, mix_first, mix_second, out_weight):
    grid = populations.reshape(19, NX, CY, CZ)
    read = jnp.stack([jnp.roll(grid[index], VELOCITIES[index], (0, 1, 2)).reshape(NX, CYZ) for index in range(19)])
    density, flow = moments(read)
    after = collide(read, density, flow, relaxation)
    old_density, old_flow = moments(populations)
    field = jnp.stack(list(old_flow) + list(flow)).astype(jnp.bfloat16)
    bricks = field.reshape(6, DEVICES, 4, BRK_X, 4, BRK_Y, 2, BRK_Z).transpose(1, 2, 4, 6, 0, 3, 5, 7).reshape(DEVICES, BRICKS, 6, V)
    sums = lax.map(lambda group: lax.map(lambda single: brick_sums(single, lift_weight), group), bricks)
    device = jnp.arange(DEVICES, dtype=jnp.int32)
    section = device // (N_ROW * N_COL)
    column = device % N_COL
    trainer = ((section[:, None] * N_ROW + send_lists) * N_COL + column[:, None]).astype(jnp.int32)
    totals = jax.ops.segment_sum(sums.reshape(DEVICES * BRICKS, 2, C), trainer.reshape(-1), num_segments=DEVICES)
    means, scales = normalizers(totals[trainer])
    mixing = mix_master.astype(jnp.bfloat16).reshape(LAYERS, C, C)

    def accumulate(total, inputs):
        group, mean, scale = inputs
        return (total + train_bricks(group, mean, scale, lift_weight, norm_gain, norm_shift, mixing, out_weight), None)
    gradient, unused = lax.scan(accumulate, jnp.zeros((LAYERS, C, C), jnp.float32), (bricks, means, scales))
    new_master, new_first, new_second = adamw(mix_master, gradient.reshape(LAYERS * C, C), mix_first, mix_second)
    return (after, new_master, new_first, new_second)
```

```python
import functools

import jax
import jax.numpy as jnp
from jax import lax
from jax.experimental import pallas as pl
from jax.experimental.pallas import tpu as pltpu
from jax.sharding import PartitionSpec as P

BF = jnp.bfloat16
F4 = jnp.float32
I4 = jnp.int32
C = 320
CELLS = 4096
PIECE = 24
MIB = 1024 * 1024

VELOCITIES = (
    (0, 0, 0),
    (1, 0, 0),
    (-1, 0, 0),
    (0, 1, 0),
    (0, -1, 0),
    (0, 0, 1),
    (0, 0, -1),
    (1, 1, 0),
    (-1, -1, 0),
    (1, -1, 0),
    (-1, 1, 0),
    (1, 0, 1),
    (-1, 0, -1),
    (1, 0, -1),
    (-1, 0, 1),
    (0, 1, 1),
    (0, -1, -1),
    (0, 1, -1),
    (0, -1, 1),
)
LATTICE_WEIGHTS = (1.0 / 3.0,) + (1.0 / 18.0,) * 6 + (1.0 / 36.0,) * 12

TAIL_P = 0.3275911 * 0.7071067811865476
TAIL_A = (
    0.5 * 0.254829592,
    0.5 * -0.284496736,
    0.5 * 1.421413741,
    0.5 * -1.453152027,
    0.5 * 1.061405429,
)
EXP_SCALE = -0.5 * 1.4426950408889634


def iota(shape, dim):
    return lax.broadcasted_iota(I4, shape, dim)


def gelu_parts(z):
    size = jnp.abs(z)
    t = pl.reciprocal(1.0 + TAIL_P * size, approx=True)
    bell = jnp.exp2(z * z * EXP_SCALE)
    poly = (((TAIL_A[4] * t + TAIL_A[3]) * t + TAIL_A[2]) * t + TAIL_A[1]) * t + TAIL_A[0]
    return size, bell, poly * t * bell


def gelu_value(z):
    size, bell, tail = gelu_parts(z)
    return jnp.maximum(z, 0.0) - size * tail


def gelu_both(z):
    size, bell, tail = gelu_parts(z)
    value = jnp.maximum(z, 0.0) - size * tail
    below = tail - (size * 0.3989422804014327) * bell
    return value, jnp.where(z >= 0.0, 1.0 - below, below)


def moments(read):
    density = read[0]
    moment = [None, None, None]
    for index in range(1, 19):
        density = density + read[index]
        for axis in range(3):
            along = VELOCITIES[index][axis]
            if along:
                term = read[index] if along > 0 else -read[index]
                moment[axis] = term if moment[axis] is None else moment[axis] + term
    return density, [moment[axis] / density for axis in range(3)]


def brick_rows(fields):
    stacked = jnp.concatenate(fields, axis=0).astype(BF)
    lane = iota((256, 256), 1)
    source = (lane & 0xC0) | (((lane >> 3) & 3) << 4) | (((lane >> 5) & 1) << 3) | (lane & 7)
    lanes = (iota((256, 256), 0) == source).astype(F4).astype(BF)
    row = iota((128, 96), 0)
    wanted = ((row >> 2) & 7) * 16 + (row & 3) * 4 + (row >> 5)
    rows = (iota((128, 96), 1) == wanted).astype(F4).astype(BF)
    moved = jnp.dot(stacked, lanes, preferred_element_type=F4).astype(BF)
    moved = jnp.dot(rows, moved, preferred_element_type=F4)
    part = iota((32, 128), 1) >> 5
    flag = (iota((32, 128), 0) >> 2) == 6
    groups = []
    for group in range(8):
        tile, place = group // 4, group % 4
        total = None
        for low in range(4):
            piece = moved[low * 32 : (low + 1) * 32, tile * 128 : (tile + 1) * 128]
            turn = (low - place) * 32 % 128
            if turn:
                piece = pltpu.roll(piece, turn, 1)
            total = piece if total is None else jnp.where(part == low, piece, total)
        groups.append(jnp.where(flag, 1.0, total))
    return jnp.concatenate(groups, axis=0).astype(BF)


def route_rows(targets):
    across = jnp.broadcast_to(targets, (32, 32)).astype(F4)
    first, second = iota((32, 32), 0), iota((32, 32), 1)
    down = jnp.sum(jnp.where(first == second, across, 0.0), axis=1, keepdims=True)
    earlier = (down == across) & (first < second)
    rank = jnp.sum(jnp.where(earlier, 1.0, 0.0), axis=0, keepdims=True)
    code = (2.0 * across[0:16] + rank).astype(BF)
    lane = iota((32, 256), 1)
    spread = (iota((32, 256), 0) == 8 * (lane & 3) + (lane >> 5)).astype(F4).astype(BF)
    code = jnp.dot(code, spread, preferred_element_type=F4)[0:1].astype(I4)
    key = code * 8 + ((iota((1, 256), 1) >> 2) & 7)
    return (iota((512, 256), 0) == key).astype(F4).astype(BF)


def lattice_kernel(pop_ref, before_ref, behind_ref, relax_ref, lists_ref, after_ref, out_ref):
    row = iota((16, 256), 0)
    depth = iota((16, 256), 1) & 15
    read = []
    for index in range(19):
        along_x, along_y, along_z = VELOCITIES[index]
        plane = pop_ref[index]
        if along_x > 0:
            plane = jnp.where(row == 0, before_ref[index - 1 : index], pltpu.roll(plane, 1, 0))
        elif along_x < 0:
            plane = jnp.where(row == 15, behind_ref[index - 1 : index], pltpu.roll(plane, 15, 0))
        if along_y:
            plane = pltpu.roll(plane, along_y * 16 % 256, 1)
        if along_z > 0:
            plane = jnp.where(depth == 0, pltpu.roll(plane, 241, 1), pltpu.roll(plane, 1, 1))
        elif along_z < 0:
            plane = jnp.where(depth == 15, pltpu.roll(plane, 15, 1), pltpu.roll(plane, 255, 1))
        read.append(plane)
    density, flow = moments(read)
    speed = flow[0] * flow[0] + flow[1] * flow[1] + flow[2] * flow[2]
    relaxation = relax_ref[...]
    for index in range(19):
        project = None
        for axis in range(3):
            along = VELOCITIES[index][axis]
            if along:
                term = flow[axis] if along > 0 else -flow[axis]
                project = term if project is None else project + term
        if project is None:
            shape = 1.0 - 1.5 * speed
        else:
            shape = 1.0 + 3.0 * project + 4.5 * project * project - 1.5 * speed
        balance = LATTICE_WEIGHTS[index] * density * shape
        after_ref[index] = read[index] - relaxation * (read[index] - balance)
    unused, old_flow = moments([pop_ref[index] for index in range(19)])
    bricks = brick_rows(old_flow + flow)
    select = route_rows(lists_ref[...])
    out_ref[...] = jnp.dot(select, bricks, preferred_element_type=F4).astype(BF)


def lattice(populations, before, behind, relaxation, lists):
    return pl.pallas_call(
        lattice_kernel,
        out_shape=(
            jax.ShapeDtypeStruct((19, 16, 256), F4),
            jax.ShapeDtypeStruct((512, 128), BF),
        ),
        name="lattice",
        compiler_params=pltpu.CompilerParams(vmem_limit_bytes=24 * MIB),
    )(populations, before, behind, relaxation, lists)


def lift_kernel(arrived_ref, lift_ref, gain_ref, shift_ref, h_ref, target_ref, taps, lifted):
    arrived = arrived_ref[...]
    flags = (iota((32, 512), 1) == iota((32, 512), 0) * 16 + 6).astype(F4).astype(BF)
    flags = jnp.dot(flags, arrived, preferred_element_type=F4).astype(BF)
    source = iota((32, 512), 1) >> 4
    ahead = (iota((32, 512), 0) < source).astype(F4).astype(BF)
    same = (iota((32, 512), 0) == source).astype(F4).astype(BF)
    dims = (((0,), (0,)), ((), ()))
    place = lax.dot_general(flags, ahead, dims, preferred_element_type=F4)[0:1].astype(I4)
    live = lax.dot_general(flags, same, dims, preferred_element_type=F4)[0:1]
    lane = iota((1, 512), 1)
    key = jnp.where(live > 0.5, place * 16 + (lane & 15), -1)
    pick = (iota((256, 512), 0) == key).astype(F4).astype(BF)
    held = jnp.dot(pick, arrived, preferred_element_type=F4)
    for brick in range(32):
        target_ref[0:8, brick * 128 : (brick + 1) * 128] = held[brick * 8 : (brick + 1) * 8]
    target_ref[8:16, :] = jnp.zeros((8, CELLS), F4)
    cell = iota((8, 128), 1)
    cell_x, cell_y, cell_z = cell >> 5, (cell >> 3) & 3, cell & 7
    shifts = [(x, y, z) for x in (-1, 0, 1) for y in (-1, 0, 1) for z in (-1, 0, 1)]
    masks = []
    for x, y, z in shifts:
        inside = (cell_x + x >= 0) & (cell_x + x < 4) & (cell_y + y >= 0) & (cell_y + y < 4)
        masks.append(inside & (cell_z + z >= 0) & (cell_z + z < 8))
    for pair in range(14):
        for brick in range(32):
            own = held[brick * 8 : (brick + 1) * 8]
            halves = []
            for tap in (2 * pair, 2 * pair + 1):
                if tap == 27:
                    halves.append(jnp.zeros((8, 128), F4))
                    continue
                x, y, z = shifts[tap]
                turn = -(x * 32 + y * 8 + z) % 128
                moved = pltpu.roll(own, turn, 1) if turn else own
                halves.append(jnp.where(masks[tap], moved, 0.0))
            taps[pair * 16 : (pair + 1) * 16, brick * 128 : (brick + 1) * 128] = jnp.concatenate(
                halves, axis=0
            ).astype(BF)
    column = iota((81, 224), 1)
    feature = (column & 7) * 27 + (column >> 3)
    valid = ((column & 7) < 3) & (column < 216)
    spread = jnp.where(valid & (iota((81, 224), 0) == feature), 1.0, 0.0).astype(BF)
    weight = jnp.dot(lift_ref[...], spread, preferred_element_type=F4).astype(BF)
    for start in range(0, CELLS, 512):
        part = slice(start, start + 512)
        lifted[:, part] = jnp.dot(weight, taps[:, part], preferred_element_type=F4)

    @pl.loop(0, C // 16)
    def _(block):
        rows = pl.ds(pl.multiple_of(block * 16, 16), 16)
        total = jnp.zeros((16, 128), F4)
        square = jnp.zeros((16, 128), F4)
        for start in range(0, CELLS, 128):
            value = lifted[rows, start : start + 128]
            total = total + value
            square = square + value * value
        mean = jnp.sum(total, axis=1, keepdims=True) / CELLS
        spread = jnp.sum(square, axis=1, keepdims=True) / CELLS - mean * mean
        scale = lax.rsqrt(spread + 1e-05) * gain_ref[rows, :]
        shift = shift_ref[rows, :]
        for start in range(0, CELLS, 256):
            part = slice(start, start + 256)
            normed = (lifted[rows, part] - mean) * scale + shift
            h_ref[rows, part] = gelu_value(normed).astype(BF)


def lift(arrived, lift_weight, gain, shift):
    return pl.pallas_call(
        lift_kernel,
        out_shape=(
            jax.ShapeDtypeStruct((C, CELLS), BF),
            jax.ShapeDtypeStruct((16, CELLS), F4),
        ),
        scratch_shapes=[pltpu.VMEM((224, CELLS), BF), pltpu.VMEM((C, CELLS), F4)],
        name="lift",
        compiler_params=pltpu.CompilerParams(vmem_limit_bytes=40 * MIB),
    )(arrived, lift_weight, gain, shift)


def train_kernel(
    steps,
    layers,
    col_ref,
    h_ref,
    target_ref,
    mix_ref,
    out_ref,
    send_ref,
    keep_ref,
    mix_back,
    states,
    slopes,
    ahead,
    back,
    inner,
    total,
):
    step = pl.program_id(0)
    cells = h_ref.shape[1]
    parts = [slice(start, start + 256) for start in range(0, cells, 256)]

    @pl.when(step == 0)
    def _():
        total[...] = jnp.zeros_like(total)
        same = (iota((C, C), 0) == iota((C, C), 1)).astype(F4).astype(BF)
        for layer in range(1, layers):
            rows = slice(layer * C, (layer + 1) * C)
            mix_back[rows, :] = lax.dot_general(
                mix_ref[rows, :], same, (((0,), (0,)), ((), ())), preferred_element_type=F4
            ).astype(BF)

    def state(layer):
        return h_ref if layer == 0 else states.at[layer - 1]

    for layer in range(layers):
        for part in parts:
            ahead[:, part] = jnp.dot(
                mix_ref[layer * C : (layer + 1) * C, :],
                state(layer)[:, part],
                preferred_element_type=F4,
            )
        for part in parts:
            for start in range(0, C, 16):
                rows = slice(start, start + 16)
                value, slope = gelu_both(ahead[rows, part])
                slopes[layer, rows, part] = slope
                states[layer, rows, part] = (state(layer)[rows, part].astype(F4) + value).astype(BF)
    for part in parts:
        output = jnp.dot(out_ref[...], states[layers - 1, :, part], preferred_element_type=F4)
        delta = ((output - target_ref[:, part]) * (2.0 / 384.0)).astype(BF)
        back[:, part] = lax.dot_general(
            out_ref[...], delta, (((0,), (0,)), ((), ())), preferred_element_type=F4
        )
    for layer in range(layers - 1, -1, -1):
        rows_of = slice(layer * C, (layer + 1) * C)
        for part in parts:
            for start in range(0, C, 16):
                rows = slice(start, start + 16)
                inner[layer, rows, part] = (back[rows, part] * slopes[layer, rows, part]).astype(BF)
        if layer > 0:
            for part in parts:
                back[:, part] += jnp.dot(
                    mix_back[rows_of, :], inner[layer, :, part], preferred_element_type=F4
                )
        total[rows_of, :] += lax.dot_general(
            inner[layer], state(layer)[...], (((1,), (1,)), ((), ())), preferred_element_type=F4
        )

    @pl.when(step == steps - 1)
    def _():
        col = col_ref[0]
        for piece in range(32):
            own = pl.multiple_of(piece * 40 + 16 * col, 8)
            other = pl.multiple_of(piece * 40 + 16 * (1 - col), 8)
            rows = slice(piece * PIECE, (piece + 1) * PIECE)
            keep_ref[rows, :] = total[pl.ds(own, PIECE), :]
            send_ref[rows, :] = total[pl.ds(other, PIECE), :]


def train(col, h, target, mixing, out_weight):
    cells = 1024
    steps = CELLS // cells
    layers = mixing.shape[0] // C
    return pl.pallas_call(
        functools.partial(train_kernel, steps, layers),
        grid=(steps,),
        in_specs=[
            pl.BlockSpec(memory_space=pltpu.SMEM),
            pl.BlockSpec((C, cells), lambda i: (0, i)),
            pl.BlockSpec((16, cells), lambda i: (0, i)),
            pl.BlockSpec((layers * C, C), lambda i: (0, 0)),
            pl.BlockSpec((16, C), lambda i: (0, 0)),
        ],
        out_specs=(
            pl.BlockSpec((32 * PIECE, C), lambda i: (0, 0)),
            pl.BlockSpec((32 * PIECE, C), lambda i: (0, 0)),
        ),
        out_shape=(
            jax.ShapeDtypeStruct((32 * PIECE, C), F4),
            jax.ShapeDtypeStruct((32 * PIECE, C), F4),
        ),
        scratch_shapes=[
            pltpu.VMEM((layers * C, C), BF),
            pltpu.VMEM((layers, C, cells), BF),
            pltpu.VMEM((layers, C, cells), F4),
            pltpu.VMEM((C, cells), F4),
            pltpu.VMEM((C, cells), F4),
            pltpu.VMEM((layers, C, cells), BF),
            pltpu.VMEM((layers * C, C), F4),
        ],
        name="train",
        compiler_params=pltpu.CompilerParams(vmem_limit_bytes=48 * MIB),
    )(col, h, target, mixing, out_weight)


def adamw(master, gradient, first, second):
    first_next = 0.9 * first + 0.1 * gradient
    second_next = 0.999 * second + 0.001 * gradient * gradient
    ratio = first_next / (1.0 - 0.9**10) / (jnp.sqrt(second_next / (1.0 - 0.999**10)) + 1e-08)
    return (master - 0.01 * (ratio + 0.1 * master), first_next, second_next)


def body(
    populations,
    relaxation,
    send_lists,
    lift_weight,
    norm_gain,
    norm_shift,
    mix_master,
    mix_first,
    mix_second,
    out_weight,
):
    every = ("sec", "row", "col")
    size = lax.axis_size(every)
    swap = [(0, 1), (1, 0)]
    col = lax.axis_index("col")
    up = [(i, (i + 1) % size) for i in range(size)]
    before = lax.ppermute(populations[1:15, 15], every, up)
    behind = lax.ppermute(populations[1:15, 0], every, [(j, i) for i, j in up])
    shard = jnp.broadcast_to(mix_master.astype(BF), (32, 20, C))
    mine = lax.all_to_all(shard, "row", split_axis=0, concat_axis=0, tiled=True)
    other = lax.ppermute(mine, "col", swap)
    pair = [jnp.where(col == 0, mine, other), jnp.where(col == 0, other, mine)]
    mixing = jnp.stack(pair, axis=1).reshape(64 * 20, C)
    after, outgoing = lattice(populations, before, behind, relaxation, send_lists)
    arrived = lax.all_to_all(
        outgoing.reshape(32, 16, 128), "row", split_axis=0, concat_axis=0, tiled=True
    ).reshape(512, 128)
    h, target = lift(arrived, lift_weight, norm_gain[:, None], norm_shift[:, None])
    out_rows = jnp.pad(out_weight, ((3, 10), (0, 0)))
    send, keep = train(col.astype(I4)[None], h, target, mixing, out_rows)
    half = keep + lax.ppermute(send, "col", swap)
    terms = lax.all_to_all(
        half.reshape(32, PIECE, C), "row", split_axis=0, concat_axis=0, tiled=True
    )
    summed = jnp.sum(terms, axis=0)
    summed = jnp.where(col == 0, summed[0:20], summed[4:24])
    gradient = summed + lax.ppermute(summed, "sec", swap)
    new_master, new_first, new_second = adamw(mix_master, gradient, mix_first, mix_second)
    return (after, new_master, new_first, new_second)


def solution(mesh):
    in_specs = (
        P(None, ("sec", "row", "col"), None),
        P(("sec", "row", "col"), None),
        P(("sec", "row", "col"), None),
        P(),
        P(),
        P(),
        P(("row", "col"), None),
        P(("row", "col"), None),
        P(("row", "col"), None),
        P(),
    )
    out_specs = (
        P(None, ("sec", "row", "col"), None),
        P(("row", "col"), None),
        P(("row", "col"), None),
        P(("row", "col"), None),
    )
    return jax.shard_map(body, mesh=mesh, in_specs=in_specs, out_specs=out_specs, check_vma=False)
```

```python
import functools

import jax
import jax.numpy as jnp
from jax import lax
from jax.experimental import pallas as pl
from jax.experimental.pallas import tpu as pltpu
from jax.sharding import PartitionSpec as P

BF = jnp.bfloat16
F4 = jnp.float32
I4 = jnp.int32
C = 320
CELLS = 4096
WEIGHT_ROWS = 56
BLOCK_ROWS = 16 + WEIGHT_ROWS
WIDE = 384
MIB = 1024 * 1024

VELOCITIES = (
    (0, 0, 0),
    (1, 0, 0),
    (-1, 0, 0),
    (0, 1, 0),
    (0, -1, 0),
    (0, 0, 1),
    (0, 0, -1),
    (1, 1, 0),
    (-1, -1, 0),
    (1, -1, 0),
    (-1, 1, 0),
    (1, 0, 1),
    (-1, 0, -1),
    (1, 0, -1),
    (-1, 0, 1),
    (0, 1, 1),
    (0, -1, -1),
    (0, 1, -1),
    (0, -1, 1),
)
LATTICE_WEIGHTS = (1.0 / 3.0,) + (1.0 / 18.0,) * 6 + (1.0 / 36.0,) * 12

TAIL_P = 0.3275911 * 0.7071067811865476
TAIL_A = (
    0.5 * 0.254829592,
    0.5 * -0.284496736,
    0.5 * 1.421413741,
    0.5 * -1.453152027,
    0.5 * 1.061405429,
)
EXP_SCALE = -0.5 * 1.4426950408889634


def iota(shape, dim):
    return lax.broadcasted_iota(I4, shape, dim)


def gelu_parts(z):
    size = jnp.abs(z)
    t = pl.reciprocal(1.0 + TAIL_P * size, approx=True)
    bell = jnp.exp2(z * z * EXP_SCALE)
    poly = (((TAIL_A[4] * t + TAIL_A[3]) * t + TAIL_A[2]) * t + TAIL_A[1]) * t + TAIL_A[0]
    return size, bell, poly * t * bell


def gelu_value(z):
    size, bell, tail = gelu_parts(z)
    return jnp.maximum(z, 0.0) - size * tail


def gelu_both(z):
    size, bell, tail = gelu_parts(z)
    value = jnp.maximum(z, 0.0) - size * tail
    below = tail - (size * 0.3989422804014327) * bell
    return value, jnp.where(z >= 0.0, 1.0 - below, below)


def moments(read):
    density = read[0]
    moment = [None, None, None]
    for index in range(1, 19):
        density = density + read[index]
        for axis in range(3):
            along = VELOCITIES[index][axis]
            if along:
                term = read[index] if along > 0 else -read[index]
                moment[axis] = term if moment[axis] is None else moment[axis] + term
    return density, [moment[axis] / density for axis in range(3)]


def brick_rows(fields):
    stacked = jnp.concatenate(fields, axis=0).astype(BF)
    lane = iota((256, 256), 1)
    source = (lane & 0xC0) | (((lane >> 3) & 3) << 4) | (((lane >> 5) & 1) << 3) | (lane & 7)
    lanes = (iota((256, 256), 0) == source).astype(F4).astype(BF)
    row = iota((128, 96), 0)
    wanted = ((row >> 2) & 7) * 16 + (row & 3) * 4 + (row >> 5)
    rows = (iota((128, 96), 1) == wanted).astype(F4).astype(BF)
    moved = jnp.dot(stacked, lanes, preferred_element_type=F4).astype(BF)
    moved = jnp.dot(rows, moved, preferred_element_type=F4)
    part = iota((32, 128), 1) >> 5
    flag = (iota((32, 128), 0) >> 2) == 6
    groups = []
    for group in range(8):
        tile, place = group // 4, group % 4
        total = None
        for low in range(4):
            piece = moved[low * 32 : (low + 1) * 32, tile * 128 : (tile + 1) * 128]
            turn = (low - place) * 32 % 128
            if turn:
                piece = pltpu.roll(piece, turn, 1)
            total = piece if total is None else jnp.where(part == low, piece, total)
        groups.append(jnp.where(flag, 1.0, total))
    return jnp.concatenate(groups, axis=0).astype(BF)


def route_rows(targets):
    across = jnp.broadcast_to(targets, (32, 32)).astype(F4)
    first, second = iota((32, 32), 0), iota((32, 32), 1)
    down = jnp.sum(jnp.where(first == second, across, 0.0), axis=1, keepdims=True)
    earlier = (down == across) & (first < second)
    rank = jnp.sum(jnp.where(earlier, 1.0, 0.0), axis=0, keepdims=True)
    code = (2.0 * across[0:16] + rank).astype(BF)
    lane = iota((32, 256), 1)
    spread = (iota((32, 256), 0) == 8 * (lane & 3) + (lane >> 5)).astype(F4).astype(BF)
    code = jnp.dot(code, spread, preferred_element_type=F4)[0:1].astype(I4)
    key = code * 8 + ((iota((1, 256), 1) >> 2) & 7)
    return (iota((512, 256), 0) == key).astype(F4).astype(BF)


def own_half(col):
    return (iota((8, 128), 0) < 4) == (col == 0)


def pack_piece(tile, half):
    low = iota((8, 128), 1) < 64
    return [
        tile(0, 0),
        tile(0, 1),
        tile(1, 0),
        tile(1, 1),
        jnp.where(low, tile(0, 2), pltpu.roll(tile(1, 2), 64, 1)),
        jnp.where(half, tile(2, 0), pltpu.roll(tile(2, 1), 4, 0)),
        tile(2, 2),
    ]


def unpack_piece(tiles):
    return (
        (tiles[0], tiles[1], tiles[4]),
        (tiles[2], tiles[3], pltpu.roll(tiles[4], 64, 1)),
        (tiles[5], pltpu.roll(tiles[5], 4, 0), tiles[6]),
    )


def lattice_kernel(
    col_ref,
    pop_ref,
    before_ref,
    behind_ref,
    relax_ref,
    lists_ref,
    mix_ref,
    after_ref,
    out_ref,
    window,
    routed,
):
    row = iota((16, 256), 0)
    depth = iota((16, 256), 1) & 15
    read = []
    for index in range(19):
        along_x, along_y, along_z = VELOCITIES[index]
        plane = pop_ref[index]
        if along_x > 0:
            plane = jnp.where(row == 0, before_ref[index - 1 : index], pltpu.roll(plane, 1, 0))
        elif along_x < 0:
            plane = jnp.where(row == 15, behind_ref[index - 1 : index], pltpu.roll(plane, 15, 0))
        if along_y:
            plane = pltpu.roll(plane, along_y * 16 % 256, 1)
        if along_z > 0:
            plane = jnp.where(depth == 0, pltpu.roll(plane, 241, 1), pltpu.roll(plane, 1, 1))
        elif along_z < 0:
            plane = jnp.where(depth == 15, pltpu.roll(plane, 15, 1), pltpu.roll(plane, 255, 1))
        read.append(plane)
    density, flow = moments(read)
    speed = flow[0] * flow[0] + flow[1] * flow[1] + flow[2] * flow[2]
    relaxation = relax_ref[...]
    for index in range(19):
        project = None
        for axis in range(3):
            along = VELOCITIES[index][axis]
            if along:
                term = flow[axis] if along > 0 else -flow[axis]
                project = term if project is None else project + term
        if project is None:
            shape = 1.0 - 1.5 * speed
        else:
            shape = 1.0 + 3.0 * project + 4.5 * project * project - 1.5 * speed
        balance = LATTICE_WEIGHTS[index] * density * shape
        after_ref[index] = read[index] - relaxation * (read[index] - balance)
    unused, old_flow = moments([pop_ref[index] for index in range(19)])
    bricks = brick_rows(old_flow + flow)
    select = route_rows(lists_ref[...])
    routed[...] = jnp.dot(select, bricks, preferred_element_type=F4)
    col = col_ref[0]
    window[...] = jnp.zeros_like(window)

    @pl.when(col == 0)
    def _():
        window[0:20, 0:C] = mix_ref[...]

    @pl.when(col != 0)
    def _():
        window[4:24, 0:C] = mix_ref[...]

    def tile(index, lanes):
        start = pl.multiple_of((index * 8 + 8 * col) % 24, 8)
        return window[pl.ds(start, 8), lanes * 128 : (lanes + 1) * 128]

    weights = jnp.concatenate(pack_piece(tile, own_half(col)), axis=0)
    for pair in range(16):
        start = pair * 2 * BLOCK_ROWS
        first = routed[pair * 32 : pair * 32 + 16]
        second = routed[pair * 32 + 16 : pair * 32 + 32]
        out_ref[start : start + 2 * BLOCK_ROWS] = jnp.concatenate(
            [first, weights, second, weights], axis=0
        ).astype(BF)


def lattice(col, populations, before, behind, relaxation, lists, master):
    vector = pl.BlockSpec(memory_space=pltpu.VMEM)
    return pl.pallas_call(
        lattice_kernel,
        in_specs=[pl.BlockSpec(memory_space=pltpu.SMEM)] + [vector] * 6,
        out_specs=(vector, vector),
        out_shape=(
            jax.ShapeDtypeStruct((19, 16, 256), F4),
            jax.ShapeDtypeStruct((32 * BLOCK_ROWS, 128), BF),
        ),
        scratch_shapes=[pltpu.VMEM((24, WIDE), F4), pltpu.VMEM((512, 128), F4)],
        name="lattice",
        compiler_params=pltpu.CompilerParams(vmem_limit_bytes=24 * MIB),
    )(col, populations, before, behind, relaxation, lists, master)


def lift_kernel(arrived_ref, lift_ref, gain_ref, shift_ref, h_ref, target_ref, taps, lifted):
    parts = []
    for pair in range(16):
        start = pair * 2 * BLOCK_ROWS
        block = arrived_ref[start : start + 2 * BLOCK_ROWS].astype(F4)
        parts += [block[0:16], block[BLOCK_ROWS : BLOCK_ROWS + 16]]
    arrived = jnp.concatenate(parts, axis=0).astype(BF)
    flags = (iota((32, 512), 1) == iota((32, 512), 0) * 16 + 6).astype(F4).astype(BF)
    flags = jnp.dot(flags, arrived, preferred_element_type=F4).astype(BF)
    source = iota((32, 512), 1) >> 4
    ahead = (iota((32, 512), 0) < source).astype(F4).astype(BF)
    same = (iota((32, 512), 0) == source).astype(F4).astype(BF)
    dims = (((0,), (0,)), ((), ()))
    place = lax.dot_general(flags, ahead, dims, preferred_element_type=F4)[0:1].astype(I4)
    live = lax.dot_general(flags, same, dims, preferred_element_type=F4)[0:1]
    lane = iota((1, 512), 1)
    key = jnp.where(live > 0.5, place * 16 + (lane & 15), -1)
    pick = (iota((256, 512), 0) == key).astype(F4).astype(BF)
    held = jnp.dot(pick, arrived, preferred_element_type=F4)
    for brick in range(32):
        target_ref[0:8, brick * 128 : (brick + 1) * 128] = held[brick * 8 : (brick + 1) * 8]
    target_ref[8:16, :] = jnp.zeros((8, CELLS), F4)
    cell = iota((8, 128), 1)
    cell_x, cell_y, cell_z = cell >> 5, (cell >> 3) & 3, cell & 7
    shifts = [(x, y, z) for x in (-1, 0, 1) for y in (-1, 0, 1) for z in (-1, 0, 1)]
    masks = []
    for x, y, z in shifts:
        inside = (cell_x + x >= 0) & (cell_x + x < 4) & (cell_y + y >= 0) & (cell_y + y < 4)
        masks.append(inside & (cell_z + z >= 0) & (cell_z + z < 8))
    for pair in range(14):
        for brick in range(32):
            own = held[brick * 8 : (brick + 1) * 8]
            halves = []
            for tap in (2 * pair, 2 * pair + 1):
                if tap == 27:
                    halves.append(jnp.zeros((8, 128), F4))
                    continue
                x, y, z = shifts[tap]
                turn = -(x * 32 + y * 8 + z) % 128
                moved = pltpu.roll(own, turn, 1) if turn else own
                halves.append(jnp.where(masks[tap], moved, 0.0))
            taps[pair * 16 : (pair + 1) * 16, brick * 128 : (brick + 1) * 128] = jnp.concatenate(
                halves, axis=0
            ).astype(BF)
    column = iota((81, 224), 1)
    feature = (column & 7) * 27 + (column >> 3)
    valid = ((column & 7) < 3) & (column < 216)
    spread = jnp.where(valid & (iota((81, 224), 0) == feature), 1.0, 0.0).astype(BF)
    weight = jnp.dot(lift_ref[...], spread, preferred_element_type=F4).astype(BF)
    for start in range(0, CELLS, 512):
        part = slice(start, start + 512)
        lifted[:, part] = jnp.dot(weight, taps[:, part], preferred_element_type=F4)

    @pl.loop(0, C // 16)
    def _(block):
        rows = pl.ds(pl.multiple_of(block * 16, 16), 16)
        total = jnp.zeros((16, 128), F4)
        square = jnp.zeros((16, 128), F4)
        for start in range(0, CELLS, 128):
            value = lifted[rows, start : start + 128]
            total = total + value
            square = square + value * value
        mean = jnp.sum(total, axis=1, keepdims=True) / CELLS
        spread = jnp.sum(square, axis=1, keepdims=True) / CELLS - mean * mean
        scale = lax.rsqrt(spread + 1e-05) * gain_ref[rows, :]
        shift = shift_ref[rows, :]
        for start in range(0, CELLS, 256):
            part = slice(start, start + 256)
            normed = (lifted[rows, part] - mean) * scale + shift
            h_ref[rows, part] = gelu_value(normed).astype(BF)


def lift(arrived, lift_weight, gain, shift):
    return pl.pallas_call(
        lift_kernel,
        out_shape=(
            jax.ShapeDtypeStruct((C, CELLS), BF),
            jax.ShapeDtypeStruct((16, CELLS), F4),
        ),
        scratch_shapes=[pltpu.VMEM((224, CELLS), BF), pltpu.VMEM((C, CELLS), F4)],
        name="lift",
        compiler_params=pltpu.CompilerParams(vmem_limit_bytes=40 * MIB),
    )(arrived, lift_weight, gain, shift)


def train_kernel(
    steps,
    layers,
    col_ref,
    h_ref,
    target_ref,
    mine_ref,
    other_ref,
    out_ref,
    send_ref,
    keep_ref,
    mix_ref,
    mix_back,
    states,
    slopes,
    ahead,
    back,
    inner,
    total,
):
    step = pl.program_id(0)
    cells = h_ref.shape[1]
    parts = [slice(start, start + 256) for start in range(0, cells, 256)]

    @pl.when(step == 0)
    def _():
        total[...] = jnp.zeros_like(total)
        even = col_ref[0] == 0
        upper = iota((8, 128), 0) < 4
        for pair in range(16):
            rows = slice(pair * 2 * BLOCK_ROWS, (pair + 1) * 2 * BLOCK_ROWS)
            mine = mine_ref[rows, :].astype(F4)
            other = other_ref[rows, :].astype(F4)
            tiles = []
            for start in (16, BLOCK_ROWS + 16):
                sides = ([], [])
                for index in range(7):
                    at = slice(start + index * 8, start + index * 8 + 8)
                    sides[0].append(jnp.where(even, mine[at], other[at]))
                    sides[1].append(jnp.where(even, other[at], mine[at]))
                left, right = unpack_piece(sides[0]), unpack_piece(sides[1])
                middle = [jnp.where(upper, a, b) for a, b in zip(left[2], right[2])]
                tiles += [left[0], left[1], middle, right[0], right[1]]
            for lanes in range(3):
                width = min(C - lanes * 128, 128)
                column = jnp.concatenate([tile[lanes] for tile in tiles], axis=0).astype(BF)
                mix_ref[pair * 80 : (pair + 1) * 80, lanes * 128 : lanes * 128 + width] = column[
                    :, 0:width
                ]
        same = (iota((C, C), 0) == iota((C, C), 1)).astype(F4).astype(BF)
        for layer in range(1, layers):
            rows = slice(layer * C, (layer + 1) * C)
            mix_back[rows, :] = lax.dot_general(
                mix_ref[rows, :], same, (((0,), (0,)), ((), ())), preferred_element_type=F4
            ).astype(BF)

    def state(layer):
        return h_ref if layer == 0 else states.at[layer - 1]

    for layer in range(layers):
        for part in parts:
            ahead[:, part] = jnp.dot(
                mix_ref[layer * C : (layer + 1) * C, :],
                state(layer)[:, part],
                preferred_element_type=F4,
            )
        for part in parts:
            for start in range(0, C, 16):
                rows = slice(start, start + 16)
                value, slope = gelu_both(ahead[rows, part])
                slopes[layer, rows, part] = slope
                states[layer, rows, part] = (state(layer)[rows, part].astype(F4) + value).astype(BF)
    for part in parts:
        output = jnp.dot(out_ref[...], states[layers - 1, :, part], preferred_element_type=F4)
        delta = ((output - target_ref[:, part]) * (2.0 / 384.0)).astype(BF)
        back[:, part] = lax.dot_general(
            out_ref[...], delta, (((0,), (0,)), ((), ())), preferred_element_type=F4
        )
    for layer in range(layers - 1, -1, -1):
        rows_of = slice(layer * C, (layer + 1) * C)
        for part in parts:
            for start in range(0, C, 16):
                rows = slice(start, start + 16)
                inner[layer, rows, part] = (back[rows, part] * slopes[layer, rows, part]).astype(BF)
        if layer > 0:
            for part in parts:
                back[:, part] += jnp.dot(
                    mix_back[rows_of, :], inner[layer, :, part], preferred_element_type=F4
                )
        total[rows_of, 0:C] += lax.dot_general(
            inner[layer], state(layer)[...], (((1,), (1,)), ((), ())), preferred_element_type=F4
        )

    @pl.when(step == steps - 1)
    def _():
        col = col_ref[0]
        for piece in range(32):
            for ref, side in ((keep_ref, col), (send_ref, 1 - col)):

                def tile(index, lanes):
                    start = piece * 40 + 16
                    if index < 2:
                        start = pl.multiple_of(piece * 40 + 24 * side + 8 * index, 8)
                    return total[pl.ds(start, 8), lanes * 128 : (lanes + 1) * 128]

                packed = pack_piece(tile, own_half(side))
                for index in range(7):
                    start = piece * WEIGHT_ROWS + index * 8
                    ref[start : start + 8, :] = packed[index]


def train(col, h, target, mine, other, out_weight):
    cells = 1024
    steps = CELLS // cells
    layers = 4
    block = pl.BlockSpec((32 * BLOCK_ROWS, 128), lambda i: (0, 0))
    return pl.pallas_call(
        functools.partial(train_kernel, steps, layers),
        grid=(steps,),
        in_specs=[
            pl.BlockSpec(memory_space=pltpu.SMEM),
            pl.BlockSpec((C, cells), lambda i: (0, i)),
            pl.BlockSpec((16, cells), lambda i: (0, i)),
            block,
            block,
            pl.BlockSpec((16, C), lambda i: (0, 0)),
        ],
        out_specs=(
            pl.BlockSpec((32 * WEIGHT_ROWS, 128), lambda i: (0, 0)),
            pl.BlockSpec((32 * WEIGHT_ROWS, 128), lambda i: (0, 0)),
        ),
        out_shape=(
            jax.ShapeDtypeStruct((32 * WEIGHT_ROWS, 128), F4),
            jax.ShapeDtypeStruct((32 * WEIGHT_ROWS, 128), F4),
        ),
        scratch_shapes=[
            pltpu.VMEM((layers * C, C), BF),
            pltpu.VMEM((layers * C, C), BF),
            pltpu.VMEM((layers, C, cells), BF),
            pltpu.VMEM((layers, C, cells), F4),
            pltpu.VMEM((C, cells), F4),
            pltpu.VMEM((C, cells), F4),
            pltpu.VMEM((layers, C, cells), BF),
            pltpu.VMEM((layers * C, WIDE), F4),
        ],
        name="train",
        compiler_params=pltpu.CompilerParams(vmem_limit_bytes=48 * MIB),
    )(col, h, target, mine, other, out_weight)


def update_kernel(
    col_ref, own_ref, other_ref, master_ref, first_ref, second_ref, new_ref, first_out, second_out
):
    packed = own_ref[...] + other_ref[...]
    parts = unpack_piece([packed[index * 8 : index * 8 + 8] for index in range(7)])
    full, rest, half = [jnp.concatenate(part, axis=1) for part in parts]
    even = col_ref[0] == 0
    lower = jnp.concatenate([full, rest, half], axis=0)
    upper = pltpu.roll(jnp.concatenate([half, full, rest], axis=0), 20, 0)
    gradient = jnp.where(even, lower, upper)[0:20, 0:C]
    master = master_ref[...]
    first_next = 0.9 * first_ref[...] + 0.1 * gradient
    second_next = 0.999 * second_ref[...] + 0.001 * gradient * gradient
    ratio = first_next / (1.0 - 0.9**10) / (jnp.sqrt(second_next / (1.0 - 0.999**10)) + 1e-08)
    new_ref[...] = master - 0.01 * (ratio + 0.1 * master)
    first_out[...] = first_next
    second_out[...] = second_next


def update(col, own, other, master, first, second):
    vector = pl.BlockSpec(memory_space=pltpu.VMEM)
    return pl.pallas_call(
        update_kernel,
        in_specs=[pl.BlockSpec(memory_space=pltpu.SMEM)] + [vector] * 5,
        out_specs=(vector,) * 3,
        out_shape=(jax.ShapeDtypeStruct(master.shape, F4),) * 3,
        name="update",
    )(col, own, other, master, first, second)


def body(
    populations,
    relaxation,
    send_lists,
    lift_weight,
    norm_gain,
    norm_shift,
    mix_master,
    mix_first,
    mix_second,
    out_weight,
):
    every = ("sec", "row", "col")
    size = lax.axis_size(every)
    swap = [(0, 1), (1, 0)]
    col = lax.axis_index("col").astype(I4)[None]
    up = [(i, (i + 1) % size) for i in range(size)]
    before = lax.ppermute(populations[1:15, 15], every, up)
    behind = lax.ppermute(populations[1:15, 0], every, [(j, i) for i, j in up])
    after, outgoing = lattice(
        col, populations, before, behind, relaxation, send_lists, mix_master
    )
    arrived = lax.all_to_all(
        outgoing.reshape(32, BLOCK_ROWS, 128), "row", split_axis=0, concat_axis=0, tiled=True
    ).reshape(32 * BLOCK_ROWS, 128)
    other = lax.ppermute(arrived, "col", swap)
    h, target = lift(arrived, lift_weight, norm_gain[:, None], norm_shift[:, None])
    out_rows = jnp.pad(out_weight, ((3, 10), (0, 0)))
    send, keep = train(col, h, target, arrived, other, out_rows)
    half = keep + lax.ppermute(send, "col", swap)
    terms = lax.all_to_all(
        half.reshape(32, WEIGHT_ROWS, 128), "row", split_axis=0, concat_axis=0, tiled=True
    )
    summed = jnp.sum(terms, axis=0)
    across = lax.ppermute(summed, "sec", swap)
    new_master, new_first, new_second = update(
        col, summed, across, mix_master, mix_first, mix_second
    )
    return (after, new_master, new_first, new_second)


def solution(mesh):
    in_specs = (
        P(None, ("sec", "row", "col"), None),
        P(("sec", "row", "col"), None),
        P(("sec", "row", "col"), None),
        P(),
        P(),
        P(),
        P(("row", "col"), None),
        P(("row", "col"), None),
        P(("row", "col"), None),
        P(),
    )
    out_specs = (
        P(None, ("sec", "row", "col"), None),
        P(("row", "col"), None),
        P(("row", "col"), None),
        P(("row", "col"), None),
    )
    return jax.shard_map(body, mesh=mesh, in_specs=in_specs, out_specs=out_specs, check_vma=False)
```

```python
import functools

import jax
import jax.numpy as jnp
from jax import lax
from jax.experimental import pallas as pl
from jax.experimental.pallas import tpu as pltpu
from jax.sharding import PartitionSpec as P

BF = jnp.bfloat16
F4 = jnp.float32
I4 = jnp.int32
C = 320
CELLS = 4096
WEIGHT_ROWS = 56
BLOCK_ROWS = 16 + WEIGHT_ROWS
WIDE = 384
SPAN = 1024
MIB = 1024 * 1024

VELOCITIES = (
    (0, 0, 0),
    (1, 0, 0),
    (-1, 0, 0),
    (0, 1, 0),
    (0, -1, 0),
    (0, 0, 1),
    (0, 0, -1),
    (1, 1, 0),
    (-1, -1, 0),
    (1, -1, 0),
    (-1, 1, 0),
    (1, 0, 1),
    (-1, 0, -1),
    (1, 0, -1),
    (-1, 0, 1),
    (0, 1, 1),
    (0, -1, -1),
    (0, 1, -1),
    (0, -1, 1),
)
LATTICE_WEIGHTS = (1.0 / 3.0,) + (1.0 / 18.0,) * 6 + (1.0 / 36.0,) * 12

ROOT_HALF = 0.7071067811865476
EXP_SCALE = -0.5 * 1.4426950408889634


def iota(shape, dim):
    return lax.broadcasted_iota(I4, shape, dim)


def gelu_value(z):
    return z * (0.5 + 0.5 * lax.erf(z * ROOT_HALF))


def gelu_both(z):
    share = 0.5 + 0.5 * lax.erf(z * ROOT_HALF)
    bell = jnp.exp2(z * z * EXP_SCALE)
    return z * share, share + (z * 0.3989422804014327) * bell


def moments(read):
    density = read[0]
    moment = [None, None, None]
    for index in range(1, 19):
        density = density + read[index]
        for axis in range(3):
            along = VELOCITIES[index][axis]
            if along:
                term = read[index] if along > 0 else -read[index]
                moment[axis] = term if moment[axis] is None else moment[axis] + term
    return density, [moment[axis] / density for axis in range(3)]


def brick_rows(stacked):
    lane = iota((256, 256), 1)
    source = (lane & 0xC0) | (((lane >> 3) & 3) << 4) | (((lane >> 5) & 1) << 3) | (lane & 7)
    lanes = (iota((256, 256), 0) == source).astype(F4).astype(BF)
    row = iota((128, 96), 0)
    wanted = ((row >> 2) & 7) * 16 + (row & 3) * 4 + (row >> 5)
    rows = (iota((128, 96), 1) == wanted).astype(F4).astype(BF)
    moved = jnp.dot(stacked, lanes, preferred_element_type=F4).astype(BF)
    moved = jnp.dot(rows, moved, preferred_element_type=F4)
    part = iota((32, 128), 1) >> 5
    flag = (iota((32, 128), 0) >> 2) == 6
    groups = []
    for group in range(8):
        tile, place = group // 4, group % 4
        total = None
        for low in range(4):
            piece = moved[low * 32 : (low + 1) * 32, tile * 128 : (tile + 1) * 128]
            turn = (low - place) * 32 % 128
            if turn:
                piece = pltpu.roll(piece, turn, 1)
            total = piece if total is None else jnp.where(part == low, piece, total)
        groups.append(jnp.where(flag, 1.0, total))
    return jnp.concatenate(groups, axis=0).astype(BF)


def route_rows(targets):
    across = jnp.broadcast_to(targets, (32, 32)).astype(F4)
    first, second = iota((32, 32), 0), iota((32, 32), 1)
    down = jnp.sum(jnp.where(first == second, across, 0.0), axis=1, keepdims=True)
    earlier = (down == across) & (first < second)
    rank = jnp.sum(jnp.where(earlier, 1.0, 0.0), axis=0, keepdims=True)
    code = (2.0 * across[0:16] + rank).astype(BF)
    lane = iota((32, 256), 1)
    spread = (iota((32, 256), 0) == 8 * (lane & 3) + (lane >> 5)).astype(F4).astype(BF)
    code = jnp.dot(code, spread, preferred_element_type=F4)[0:1].astype(I4)
    key = code * 8 + ((iota((1, 256), 1) >> 2) & 7)
    return (iota((512, 256), 0) == key).astype(F4).astype(BF)


def own_half(col):
    return (iota((8, 128), 0) < 4) == (col == 0)


def pack_piece(tile, half):
    low = iota((8, 128), 1) < 64
    return [
        tile(0, 0),
        tile(0, 1),
        tile(1, 0),
        tile(1, 1),
        jnp.where(low, tile(0, 2), pltpu.roll(tile(1, 2), 64, 1)),
        jnp.where(half, tile(2, 0), pltpu.roll(tile(2, 1), 4, 0)),
        tile(2, 2),
    ]


def unpack_piece(tiles):
    return (
        (tiles[0], tiles[1], tiles[4]),
        (tiles[2], tiles[3], pltpu.roll(tiles[4], 64, 1)),
        (tiles[5], pltpu.roll(tiles[5], 4, 0), tiles[6]),
    )


def prepare_kernel(
    col_ref,
    pop_ref,
    lists_ref,
    mix_ref,
    lift_ref,
    gain_ref,
    shift_ref,
    out_ref,
    old_ref,
    select_ref,
    weights_ref,
    lift_out,
    gain_out,
    shift_out,
    rows_out,
    window,
    rows,
):
    unused, old_flow = moments([pop_ref[index] for index in range(19)])
    old_ref[...] = jnp.concatenate(old_flow, axis=0).astype(BF)
    select_ref[...] = route_rows(lists_ref[...])
    col = col_ref[0]
    window[...] = jnp.zeros_like(window)

    @pl.when(col == 0)
    def _():
        window[0:20, 0:C] = mix_ref[...]

    @pl.when(col != 0)
    def _():
        window[4:24, 0:C] = mix_ref[...]

    def tile(index, lanes):
        start = pl.multiple_of((index * 8 + 8 * col) % 24, 8)
        return window[pl.ds(start, 8), lanes * 128 : (lanes + 1) * 128]

    weights_ref[...] = jnp.concatenate(pack_piece(tile, own_half(col)), axis=0)
    column = iota((81, 224), 1)
    feature = (column & 7) * 27 + (column >> 3)
    valid = ((column & 7) < 3) & (column < 216)
    spread = jnp.where(valid & (iota((81, 224), 0) == feature), 1.0, 0.0).astype(BF)
    lift_out[...] = jnp.dot(lift_ref[...], spread, preferred_element_type=F4).astype(BF)
    same = iota((C, C), 0) == iota((C, C), 1)
    for source, target in ((gain_ref, gain_out), (shift_ref, shift_out)):
        down = jnp.sum(jnp.where(same, source[...], 0.0), axis=1, keepdims=True)
        target[...] = jnp.broadcast_to(down, (C, 128))
    rows[...] = jnp.zeros_like(rows)
    rows[3:6, :] = out_ref[...].astype(F4)
    rows_out[...] = rows[...].astype(BF)


def prepare(col, populations, lists, master, lift_weight, gain, shift, out_weight):
    vector = pl.BlockSpec(memory_space=pltpu.VMEM)
    return pl.pallas_call(
        prepare_kernel,
        in_specs=[pl.BlockSpec(memory_space=pltpu.SMEM)] + [vector] * 7,
        out_specs=(vector,) * 7,
        out_shape=(
            jax.ShapeDtypeStruct((48, 256), BF),
            jax.ShapeDtypeStruct((512, 256), BF),
            jax.ShapeDtypeStruct((WEIGHT_ROWS, 128), F4),
            jax.ShapeDtypeStruct((C, 224), BF),
            jax.ShapeDtypeStruct((C, 128), F4),
            jax.ShapeDtypeStruct((C, 128), F4),
            jax.ShapeDtypeStruct((16, C), BF),
        ),
        scratch_shapes=[pltpu.VMEM((24, WIDE), F4), pltpu.VMEM((16, C), F4)],
        name="prepare",
        cost_estimate=pl.CostEstimate(flops=10**7, bytes_accessed=4 * 10**6, transcendentals=0),
        compiler_params=pltpu.CompilerParams(vmem_limit_bytes=16 * MIB),
    )(col, populations, lists, master, lift_weight, gain, shift, out_weight)


def streamed(pop_ref, before_ref, behind_ref):
    row = iota((16, 256), 0)
    depth = iota((16, 256), 1) & 15
    read = []
    for index in range(19):
        along_x, along_y, along_z = VELOCITIES[index]
        plane = pop_ref[index]
        if along_x > 0:
            plane = jnp.where(row == 0, before_ref[index - 1 : index], pltpu.roll(plane, 1, 0))
        elif along_x < 0:
            plane = jnp.where(row == 15, behind_ref[index - 1 : index], pltpu.roll(plane, 15, 0))
        if along_y:
            plane = pltpu.roll(plane, along_y * 16 % 256, 1)
        if along_z > 0:
            plane = jnp.where(depth == 0, pltpu.roll(plane, 241, 1), pltpu.roll(plane, 1, 1))
        elif along_z < 0:
            plane = jnp.where(depth == 15, pltpu.roll(plane, 15, 1), pltpu.roll(plane, 255, 1))
        read.append(plane)
    return read


def route_kernel(
    pop_ref, before_ref, behind_ref, old_ref, select_ref, weights_ref, out_ref, routed
):
    density, flow = moments(streamed(pop_ref, before_ref, behind_ref))
    fields = jnp.concatenate([old_ref[...]] + [part.astype(BF) for part in flow], axis=0)
    bricks = brick_rows(fields)
    routed[...] = jnp.dot(select_ref[...], bricks, preferred_element_type=F4)
    weights = weights_ref[...]
    for pair in range(16):
        start = pair * 2 * BLOCK_ROWS
        first = routed[pair * 32 : pair * 32 + 16]
        second = routed[pair * 32 + 16 : pair * 32 + 32]
        out_ref[start : start + 2 * BLOCK_ROWS] = jnp.concatenate(
            [first, weights, second, weights], axis=0
        ).astype(BF)


def route(populations, before, behind, old, select, weights):
    return pl.pallas_call(
        route_kernel,
        out_shape=jax.ShapeDtypeStruct((32 * BLOCK_ROWS, 128), BF),
        scratch_shapes=[pltpu.VMEM((512, 128), F4)],
        name="route",
        compiler_params=pltpu.CompilerParams(vmem_limit_bytes=16 * MIB),
    )(populations, before, behind, old, select, weights)


def collide_kernel(pop_ref, before_ref, behind_ref, relax_ref, after_ref):
    read = streamed(pop_ref, before_ref, behind_ref)
    density, flow = moments(read)
    speed = flow[0] * flow[0] + flow[1] * flow[1] + flow[2] * flow[2]
    relaxation = relax_ref[...]
    for index in range(19):
        project = None
        for axis in range(3):
            along = VELOCITIES[index][axis]
            if along:
                term = flow[axis] if along > 0 else -flow[axis]
                project = term if project is None else project + term
        if project is None:
            shape = 1.0 - 1.5 * speed
        else:
            shape = 1.0 + 3.0 * project + 4.5 * project * project - 1.5 * speed
        balance = LATTICE_WEIGHTS[index] * density * shape
        after_ref[index] = read[index] - relaxation * (read[index] - balance)


def collide(populations, before, behind, relaxation):
    return pl.pallas_call(
        collide_kernel,
        out_shape=jax.ShapeDtypeStruct((19, 16, 256), F4),
        name="collide",
        cost_estimate=pl.CostEstimate(flops=10**7, bytes_accessed=4 * 10**6, transcendentals=0),
        compiler_params=pltpu.CompilerParams(vmem_limit_bytes=16 * MIB),
    )(populations, before, behind, relaxation)


def lift_kernel(
    arrived_ref,
    weight_ref,
    gain_ref,
    shift_ref,
    h_ref,
    target_ref,
    taps,
    lifted,
    sums,
    squares,
    means,
    scales,
):
    parts = []
    for pair in range(16):
        start = pair * 2 * BLOCK_ROWS
        block = arrived_ref[start : start + 2 * BLOCK_ROWS].astype(F4)
        parts += [block[0:16], block[BLOCK_ROWS : BLOCK_ROWS + 16]]
    arrived = jnp.concatenate(parts, axis=0).astype(BF)
    flags = (iota((32, 512), 1) == iota((32, 512), 0) * 16 + 6).astype(F4).astype(BF)
    flags = jnp.dot(flags, arrived, preferred_element_type=F4).astype(BF)
    source = iota((32, 512), 1) >> 4
    ahead = (iota((32, 512), 0) < source).astype(F4).astype(BF)
    same = (iota((32, 512), 0) == source).astype(F4).astype(BF)
    dims = (((0,), (0,)), ((), ()))
    place = lax.dot_general(flags, ahead, dims, preferred_element_type=F4)[0:1].astype(I4)
    live = lax.dot_general(flags, same, dims, preferred_element_type=F4)[0:1]
    lane = iota((1, 512), 1)
    key = jnp.where(live > 0.5, place * 16 + (lane & 15), -1)
    pick = (iota((256, 512), 0) == key).astype(F4).astype(BF)
    held = jnp.dot(pick, arrived, preferred_element_type=F4)
    for brick in range(32):
        target_ref[0:8, brick * 128 : (brick + 1) * 128] = held[brick * 8 : (brick + 1) * 8]
    target_ref[8:16, :] = jnp.zeros((8, CELLS), F4)
    cell = iota((8, 128), 1)
    cell_x, cell_y, cell_z = cell >> 5, (cell >> 3) & 3, cell & 7
    shifts = [(x, y, z) for x in (-1, 0, 1) for y in (-1, 0, 1) for z in (-1, 0, 1)]
    masks = []
    for x, y, z in shifts:
        inside = (cell_x + x >= 0) & (cell_x + x < 4) & (cell_y + y >= 0) & (cell_y + y < 4)
        masks.append(inside & (cell_z + z >= 0) & (cell_z + z < 8))
    weight = weight_ref[...]
    for start in range(0, CELLS, SPAN):
        part = slice(start, start + SPAN)
        for brick in range(start // 128, (start + SPAN) // 128):
            own = held[brick * 8 : (brick + 1) * 8]
            for pair in range(14):
                halves = []
                for tap in (2 * pair, 2 * pair + 1):
                    if tap == 27:
                        halves.append(jnp.zeros((8, 128), F4))
                        continue
                    x, y, z = shifts[tap]
                    turn = -(x * 32 + y * 8 + z) % 128
                    moved = pltpu.roll(own, turn, 1) if turn else own
                    halves.append(jnp.where(masks[tap], moved, 0.0))
                taps[pair * 16 : (pair + 1) * 16, brick * 128 : (brick + 1) * 128] = (
                    jnp.concatenate(halves, axis=0).astype(BF)
                )
        lifted[:, part] = jnp.dot(weight, taps[:, part], preferred_element_type=F4)
        for row in range(0, C, 16):
            rows = slice(row, row + 16)
            total = None
            for at in range(start, start + SPAN, 128):
                value = lifted[rows, at : at + 128]
                total = value if total is None else total + value
                square = value * value if at == start else square + value * value
            sums[rows, :] = total if start == 0 else sums[rows, :] + total
            squares[rows, :] = square if start == 0 else squares[rows, :] + square
    mean = jnp.sum(sums[...], axis=1, keepdims=True) / CELLS
    spread = jnp.sum(squares[...], axis=1, keepdims=True) / CELLS - mean * mean
    means[...] = jnp.broadcast_to(mean, (C, 128))
    scales[...] = lax.rsqrt(spread + 1e-05) * gain_ref[...]

    @pl.loop(0, CELLS // SPAN)
    def _(index):
        for row in range(0, C, 16):
            rows = slice(row, row + 16)
            mean, scale, shift = means[rows, :], scales[rows, :], shift_ref[rows, :]
            for at in range(0, SPAN, 128):
                part = pl.ds(pl.multiple_of(index * SPAN + at, 128), 128)
                normed = (lifted[rows, part] - mean) * scale + shift
                h_ref[rows, part] = gelu_value(normed).astype(BF)


def lift(arrived, weight, gain, shift):
    return pl.pallas_call(
        lift_kernel,
        out_shape=(
            jax.ShapeDtypeStruct((C, CELLS), BF),
            jax.ShapeDtypeStruct((16, CELLS), F4),
        ),
        scratch_shapes=[pltpu.VMEM((224, CELLS), BF), pltpu.VMEM((C, CELLS), F4)]
        + [pltpu.VMEM((C, 128), F4)] * 4,
        name="lift",
        compiler_params=pltpu.CompilerParams(vmem_limit_bytes=40 * MIB),
    )(arrived, weight, gain, shift)


def train_kernel(
    steps,
    layers,
    col_ref,
    h_ref,
    target_ref,
    mine_ref,
    other_ref,
    out_ref,
    send_ref,
    keep_ref,
    mix_ref,
    mix_back,
    states,
    slopes,
    ahead,
    back,
    inner,
    total,
):
    step = pl.program_id(0)
    cells = h_ref.shape[1]
    parts = [slice(start, start + 256) for start in range(0, cells, 256)]

    @pl.when(step == 0)
    def _():
        total[...] = jnp.zeros_like(total)
        even = col_ref[0] == 0
        upper = iota((8, 128), 0) < 4
        for pair in range(16):
            rows = slice(pair * 2 * BLOCK_ROWS, (pair + 1) * 2 * BLOCK_ROWS)
            mine = mine_ref[rows, :].astype(F4)
            other = other_ref[rows, :].astype(F4)
            tiles = []
            for start in (16, BLOCK_ROWS + 16):
                sides = ([], [])
                for index in range(7):
                    at = slice(start + index * 8, start + index * 8 + 8)
                    sides[0].append(jnp.where(even, mine[at], other[at]))
                    sides[1].append(jnp.where(even, other[at], mine[at]))
                left, right = unpack_piece(sides[0]), unpack_piece(sides[1])
                middle = [jnp.where(upper, a, b) for a, b in zip(left[2], right[2])]
                tiles += [left[0], left[1], middle, right[0], right[1]]
            for lanes in range(3):
                width = min(C - lanes * 128, 128)
                column = jnp.concatenate([tile[lanes] for tile in tiles], axis=0).astype(BF)
                mix_ref[pair * 80 : (pair + 1) * 80, lanes * 128 : lanes * 128 + width] = column[
                    :, 0:width
                ]
        same = (iota((C, C), 0) == iota((C, C), 1)).astype(F4).astype(BF)
        for layer in range(1, layers):
            rows = slice(layer * C, (layer + 1) * C)
            mix_back[rows, :] = lax.dot_general(
                mix_ref[rows, :], same, (((0,), (0,)), ((), ())), preferred_element_type=F4
            ).astype(BF)

    def state(layer):
        return h_ref if layer == 0 else states.at[layer - 1]

    for layer in range(layers):
        for part in parts:
            ahead[:, part] = jnp.dot(
                mix_ref[layer * C : (layer + 1) * C, :],
                state(layer)[:, part],
                preferred_element_type=F4,
            )
        for part in parts:
            for start in range(0, C, 16):
                rows = slice(start, start + 16)
                value, slope = gelu_both(ahead[rows, part])
                slopes[layer, rows, part] = slope
                states[layer, rows, part] = (state(layer)[rows, part].astype(F4) + value).astype(BF)
    for part in parts:
        output = jnp.dot(out_ref[...], states[layers - 1, :, part], preferred_element_type=F4)
        delta = ((output - target_ref[:, part]) * (2.0 / 384.0)).astype(BF)
        back[:, part] = lax.dot_general(
            out_ref[...], delta, (((0,), (0,)), ((), ())), preferred_element_type=F4
        )
    for layer in range(layers - 1, -1, -1):
        rows_of = slice(layer * C, (layer + 1) * C)
        for part in parts:
            for start in range(0, C, 16):
                rows = slice(start, start + 16)
                inner[layer, rows, part] = (back[rows, part] * slopes[layer, rows, part]).astype(BF)
        if layer > 0:
            for part in parts:
                back[:, part] += jnp.dot(
                    mix_back[rows_of, :], inner[layer, :, part], preferred_element_type=F4
                )
        total[rows_of, 0:C] += lax.dot_general(
            inner[layer], state(layer)[...], (((1,), (1,)), ((), ())), preferred_element_type=F4
        )

    @pl.when(step == steps - 1)
    def _():
        col = col_ref[0]
        for piece in range(32):
            for ref, side in ((keep_ref, col), (send_ref, 1 - col)):

                def tile(index, lanes):
                    start = piece * 40 + 16
                    if index < 2:
                        start = pl.multiple_of(piece * 40 + 24 * side + 8 * index, 8)
                    return total[pl.ds(start, 8), lanes * 128 : (lanes + 1) * 128]

                packed = pack_piece(tile, own_half(side))
                for index in range(7):
                    start = piece * WEIGHT_ROWS + index * 8
                    ref[start : start + 8, :] = packed[index]


def train(col, h, target, mine, other, out_weight):
    cells = 1024
    steps = CELLS // cells
    layers = 4
    block = pl.BlockSpec((32 * BLOCK_ROWS, 128), lambda i: (0, 0))
    return pl.pallas_call(
        functools.partial(train_kernel, steps, layers),
        grid=(steps,),
        in_specs=[
            pl.BlockSpec(memory_space=pltpu.SMEM),
            pl.BlockSpec((C, cells), lambda i: (0, i)),
            pl.BlockSpec((16, cells), lambda i: (0, i)),
            block,
            block,
            pl.BlockSpec((16, C), lambda i: (0, 0)),
        ],
        out_specs=(
            pl.BlockSpec((32 * WEIGHT_ROWS, 128), lambda i: (0, 0)),
            pl.BlockSpec((32 * WEIGHT_ROWS, 128), lambda i: (0, 0)),
        ),
        out_shape=(
            jax.ShapeDtypeStruct((32 * WEIGHT_ROWS, 128), F4),
            jax.ShapeDtypeStruct((32 * WEIGHT_ROWS, 128), F4),
        ),
        scratch_shapes=[
            pltpu.VMEM((layers * C, C), BF),
            pltpu.VMEM((layers * C, C), BF),
            pltpu.VMEM((layers, C, cells), BF),
            pltpu.VMEM((layers, C, cells), F4),
            pltpu.VMEM((C, cells), F4),
            pltpu.VMEM((C, cells), F4),
            pltpu.VMEM((layers, C, cells), BF),
            pltpu.VMEM((layers * C, WIDE), F4),
        ],
        name="train",
        compiler_params=pltpu.CompilerParams(vmem_limit_bytes=48 * MIB),
    )(col, h, target, mine, other, out_weight)


def update_kernel(
    col_ref, own_ref, other_ref, master_ref, first_ref, second_ref, new_ref, first_out, second_out
):
    packed = own_ref[...] + other_ref[...]
    parts = unpack_piece([packed[index * 8 : index * 8 + 8] for index in range(7)])
    full, rest, half = [jnp.concatenate(part, axis=1) for part in parts]
    even = col_ref[0] == 0
    lower = jnp.concatenate([full, rest, half], axis=0)
    upper = pltpu.roll(jnp.concatenate([half, full, rest], axis=0), 20, 0)
    gradient = jnp.where(even, lower, upper)[0:20, 0:C]
    master = master_ref[...]
    first_next = 0.9 * first_ref[...] + 0.1 * gradient
    second_next = 0.999 * second_ref[...] + 0.001 * gradient * gradient
    ratio = first_next / (1.0 - 0.9**10) / (jnp.sqrt(second_next / (1.0 - 0.999**10)) + 1e-08)
    new_ref[...] = master - 0.01 * (ratio + 0.1 * master)
    first_out[...] = first_next
    second_out[...] = second_next


def update(col, own, other, master, first, second):
    vector = pl.BlockSpec(memory_space=pltpu.VMEM)
    return pl.pallas_call(
        update_kernel,
        in_specs=[pl.BlockSpec(memory_space=pltpu.SMEM)] + [vector] * 5,
        out_specs=(vector,) * 3,
        out_shape=(jax.ShapeDtypeStruct(master.shape, F4),) * 3,
        name="update",
    )(col, own, other, master, first, second)


def body(
    populations,
    relaxation,
    send_lists,
    lift_weight,
    norm_gain,
    norm_shift,
    mix_master,
    mix_first,
    mix_second,
    out_weight,
):
    every = ("sec", "row", "col")
    size = lax.axis_size(every)
    swap = [(0, 1), (1, 0)]
    col = lax.axis_index("col").astype(I4)[None]
    up = [(i, (i + 1) % size) for i in range(size)]
    before = lax.ppermute(populations[1:15, 15], every, up)
    behind = lax.ppermute(populations[1:15, 0], every, [(j, i) for i, j in up])
    old, select, weights, lift_rows, gain, shift, out_rows = prepare(
        col,
        populations,
        send_lists,
        mix_master,
        lift_weight,
        norm_gain[None],
        norm_shift[None],
        out_weight,
    )
    outgoing = route(populations, before, behind, old, select, weights)
    arrived = lax.all_to_all(
        outgoing.reshape(32, BLOCK_ROWS, 128), "row", split_axis=0, concat_axis=0, tiled=True
    ).reshape(32 * BLOCK_ROWS, 128)
    after = collide(populations, before, behind, relaxation)
    other = lax.ppermute(arrived, "col", swap)
    h, target = lift(arrived, lift_rows, gain, shift)
    send, keep = train(col, h, target, arrived, other, out_rows)
    half = keep + lax.ppermute(send, "col", swap)
    terms = lax.all_to_all(
        half.reshape(32, WEIGHT_ROWS, 128), "row", split_axis=0, concat_axis=0, tiled=True
    )
    summed = jnp.sum(terms, axis=0)
    across = lax.ppermute(summed, "sec", swap)
    new_master, new_first, new_second = update(
        col, summed, across, mix_master, mix_first, mix_second
    )
    return (after, new_master, new_first, new_second)


def solution(mesh):
    in_specs = (
        P(None, ("sec", "row", "col"), None),
        P(("sec", "row", "col"), None),
        P(("sec", "row", "col"), None),
        P(),
        P(),
        P(),
        P(("row", "col"), None),
        P(("row", "col"), None),
        P(("row", "col"), None),
        P(),
    )
    out_specs = (
        P(None, ("sec", "row", "col"), None),
        P(("row", "col"), None),
        P(("row", "col"), None),
        P(("row", "col"), None),
    )
    return jax.shard_map(body, mesh=mesh, in_specs=in_specs, out_specs=out_specs, check_vma=False)
```

```python
import functools

import jax
import jax.numpy as jnp
from jax import lax
from jax.experimental import pallas as pl
from jax.experimental.pallas import tpu as pltpu
from jax.sharding import PartitionSpec as P

BF = jnp.bfloat16
F4 = jnp.float32
I4 = jnp.int32
C = 320
CELLS = 4096
WEIGHT_ROWS = 56
BLOCK_ROWS = 16 + WEIGHT_ROWS
WIDE = 384
SPAN = 1024
MIB = 1024 * 1024

VELOCITIES = (
    (0, 0, 0),
    (1, 0, 0),
    (-1, 0, 0),
    (0, 1, 0),
    (0, -1, 0),
    (0, 0, 1),
    (0, 0, -1),
    (1, 1, 0),
    (-1, -1, 0),
    (1, -1, 0),
    (-1, 1, 0),
    (1, 0, 1),
    (-1, 0, -1),
    (1, 0, -1),
    (-1, 0, 1),
    (0, 1, 1),
    (0, -1, -1),
    (0, 1, -1),
    (0, -1, 1),
)
LATTICE_WEIGHTS = (1.0 / 3.0,) + (1.0 / 18.0,) * 6 + (1.0 / 36.0,) * 12

ROOT_HALF = 0.7071067811865476
EXP_SCALE = -0.5 * 1.4426950408889634


def iota(shape, dim):
    return lax.broadcasted_iota(I4, shape, dim)


def gelu_value(z):
    return z * (0.5 + 0.5 * lax.erf(z * ROOT_HALF))


def gelu_both(z):
    share = 0.5 + 0.5 * lax.erf(z * ROOT_HALF)
    bell = jnp.exp2(z * z * EXP_SCALE)
    return z * share, share + (z * 0.3989422804014327) * bell


def moments(read):
    density = read[0]
    moment = [None, None, None]
    for index in range(1, 19):
        density = density + read[index]
        for axis in range(3):
            along = VELOCITIES[index][axis]
            if along:
                term = read[index] if along > 0 else -read[index]
                moment[axis] = term if moment[axis] is None else moment[axis] + term
    return density, [moment[axis] / density for axis in range(3)]


def brick_rows(stacked):
    lane = iota((256, 256), 1)
    source = (lane & 0xC0) | (((lane >> 3) & 3) << 4) | (((lane >> 5) & 1) << 3) | (lane & 7)
    lanes = (iota((256, 256), 0) == source).astype(F4).astype(BF)
    row = iota((128, 96), 0)
    wanted = ((row >> 2) & 7) * 16 + (row & 3) * 4 + (row >> 5)
    rows = (iota((128, 96), 1) == wanted).astype(F4).astype(BF)
    moved = jnp.dot(stacked, lanes, preferred_element_type=F4).astype(BF)
    moved = jnp.dot(rows, moved, preferred_element_type=F4)
    part = iota((32, 128), 1) >> 5
    flag = (iota((32, 128), 0) >> 2) == 6
    groups = []
    for group in range(8):
        tile, place = group // 4, group % 4
        total = None
        for low in range(4):
            piece = moved[low * 32 : (low + 1) * 32, tile * 128 : (tile + 1) * 128]
            turn = (low - place) * 32 % 128
            if turn:
                piece = pltpu.roll(piece, turn, 1)
            total = piece if total is None else jnp.where(part == low, piece, total)
        groups.append(jnp.where(flag, 1.0, total))
    return jnp.concatenate(groups, axis=0).astype(BF)


def route_rows(targets):
    across = jnp.broadcast_to(targets, (32, 32)).astype(F4)
    first, second = iota((32, 32), 0), iota((32, 32), 1)
    down = jnp.sum(jnp.where(first == second, across, 0.0), axis=1, keepdims=True)
    earlier = (down == across) & (first < second)
    rank = jnp.sum(jnp.where(earlier, 1.0, 0.0), axis=0, keepdims=True)
    code = (2.0 * across[0:16] + rank).astype(BF)
    lane = iota((32, 256), 1)
    spread = (iota((32, 256), 0) == 8 * (lane & 3) + (lane >> 5)).astype(F4).astype(BF)
    code = jnp.dot(code, spread, preferred_element_type=F4)[0:1].astype(I4)
    key = code * 8 + ((iota((1, 256), 1) >> 2) & 7)
    return (iota((512, 256), 0) == key).astype(F4).astype(BF)


def own_half(col):
    return (iota((8, 128), 0) < 4) == (col == 0)


def pack_piece(tile, half):
    low = iota((8, 128), 1) < 64
    return [
        tile(0, 0),
        tile(0, 1),
        tile(1, 0),
        tile(1, 1),
        jnp.where(low, tile(0, 2), pltpu.roll(tile(1, 2), 64, 1)),
        jnp.where(half, tile(2, 0), pltpu.roll(tile(2, 1), 4, 0)),
        tile(2, 2),
    ]


def unpack_piece(tiles):
    return (
        (tiles[0], tiles[1], tiles[4]),
        (tiles[2], tiles[3], pltpu.roll(tiles[4], 64, 1)),
        (tiles[5], pltpu.roll(tiles[5], 4, 0), tiles[6]),
    )


def planes_kernel(pop_ref, last_ref, initial_ref, own_ref):
    own_ref[...] = pop_ref[...]
    for index in range(1, 15):
        last_ref[index - 1 : index, :] = pop_ref[index, 15:16, :]
        initial_ref[index - 1 : index, :] = pop_ref[index, 0:1, :]


def planes(populations):
    return pl.pallas_call(
        planes_kernel,
        out_shape=(jax.ShapeDtypeStruct((14, 256), F4),) * 2
        + (jax.ShapeDtypeStruct((19, 16, 256), F4),),
        name="planes",
        compiler_params=pltpu.CompilerParams(vmem_limit_bytes=16 * MIB),
    )(populations)


def gathered_rows(gain, shift, lists, out_weight, master, lift_weight):
    def placed(array, start):
        rows, lanes = array.shape
        return jnp.pad(array, ((start, 120 - start - rows), (0, C - lanes))).astype(F4)

    row = iota((120, C), 0)
    total = placed(lists, 2) + placed(out_weight, 3) + placed(master, 8) + placed(lift_weight.T, 32)
    return jnp.where(row == 0, gain, jnp.where(row == 1, shift, total))


def prepare_kernel(
    col_ref,
    pop_ref,
    small_ref,
    old_ref,
    select_ref,
    weights_ref,
    lift_out,
    gain_out,
    shift_out,
    rows_out,
    window,
):
    unused, old_flow = moments([pop_ref[index] for index in range(19)])
    old_ref[...] = jnp.concatenate(old_flow, axis=0).astype(BF)
    select_ref[...] = route_rows(small_ref[2:3, 0:32])
    col = col_ref[0]
    window[...] = jnp.zeros_like(window)

    @pl.when(col == 0)
    def _():
        window[0:20, 0:C] = small_ref[8:28, :]

    @pl.when(col != 0)
    def _():
        window[4:24, 0:C] = small_ref[8:28, :]

    def tile(index, lanes):
        start = pl.multiple_of((index * 8 + 8 * col) % 24, 8)
        return window[pl.ds(start, 8), lanes * 128 : (lanes + 1) * 128]

    weights_ref[...] = jnp.concatenate(pack_piece(tile, own_half(col)), axis=0)
    column = iota((88, 224), 1)
    feature = (column & 7) * 27 + (column >> 3)
    valid = ((column & 7) < 3) & (column < 216)
    spread = jnp.where(valid & (iota((88, 224), 0) == feature), 1.0, 0.0).astype(BF)
    lift_out[...] = lax.dot_general(
        small_ref[32:120, :].astype(BF),
        spread,
        (((0,), (0,)), ((), ())),
        preferred_element_type=F4,
    ).astype(BF)
    same = iota((C, C), 0) == iota((C, C), 1)
    for index, target in ((0, gain_out), (1, shift_out)):
        across = small_ref[index : index + 1, :]
        down = jnp.sum(jnp.where(same, across, 0.0), axis=1, keepdims=True)
        target[...] = jnp.broadcast_to(down, (C, 128))
    row = iota((8, C), 0)
    rows = jnp.where((row >= 3) & (row < 6), small_ref[0:8, :], 0.0)
    rows_out[...] = jnp.concatenate([rows, jnp.zeros_like(rows)], axis=0).astype(BF)


def prepare(col, populations, small):
    vector = pl.BlockSpec(memory_space=pltpu.VMEM)
    return pl.pallas_call(
        prepare_kernel,
        in_specs=[pl.BlockSpec(memory_space=pltpu.SMEM)] + [vector] * 2,
        out_specs=(vector,) * 7,
        out_shape=(
            jax.ShapeDtypeStruct((48, 256), BF),
            jax.ShapeDtypeStruct((512, 256), BF),
            jax.ShapeDtypeStruct((WEIGHT_ROWS, 128), F4),
            jax.ShapeDtypeStruct((C, 224), BF),
            jax.ShapeDtypeStruct((C, 128), F4),
            jax.ShapeDtypeStruct((C, 128), F4),
            jax.ShapeDtypeStruct((16, C), BF),
        ),
        scratch_shapes=[pltpu.VMEM((24, WIDE), F4)],
        name="prepare",
        cost_estimate=pl.CostEstimate(flops=10**7, bytes_accessed=4 * 10**6, transcendentals=0),
        compiler_params=pltpu.CompilerParams(vmem_limit_bytes=16 * MIB),
    )(col, populations, small)


def streamed(pop_ref, before_ref, behind_ref):
    row = iota((16, 256), 0)
    depth = iota((16, 256), 1) & 15
    read = []
    for index in range(19):
        along_x, along_y, along_z = VELOCITIES[index]
        plane = pop_ref[index]
        if along_x > 0:
            plane = jnp.where(row == 0, before_ref[index - 1 : index], pltpu.roll(plane, 1, 0))
        elif along_x < 0:
            plane = jnp.where(row == 15, behind_ref[index - 1 : index], pltpu.roll(plane, 15, 0))
        if along_y:
            plane = pltpu.roll(plane, along_y * 16 % 256, 1)
        if along_z > 0:
            plane = jnp.where(depth == 0, pltpu.roll(plane, 241, 1), pltpu.roll(plane, 1, 1))
        elif along_z < 0:
            plane = jnp.where(depth == 15, pltpu.roll(plane, 15, 1), pltpu.roll(plane, 255, 1))
        read.append(plane)
    return read


def route_kernel(
    pop_ref, before_ref, behind_ref, old_ref, select_ref, weights_ref, out_ref, routed
):
    density, flow = moments(streamed(pop_ref, before_ref, behind_ref))
    fields = jnp.concatenate([old_ref[...]] + [part.astype(BF) for part in flow], axis=0)
    bricks = brick_rows(fields)
    routed[...] = jnp.dot(select_ref[...], bricks, preferred_element_type=F4)
    weights = weights_ref[...]
    for pair in range(16):
        start = pair * 2 * BLOCK_ROWS
        first = routed[pair * 32 : pair * 32 + 16]
        second = routed[pair * 32 + 16 : pair * 32 + 32]
        out_ref[start : start + 2 * BLOCK_ROWS] = jnp.concatenate(
            [first, weights, second, weights], axis=0
        ).astype(BF)


def route(populations, before, behind, old, select, weights):
    return pl.pallas_call(
        route_kernel,
        out_shape=jax.ShapeDtypeStruct((32 * BLOCK_ROWS, 128), BF),
        scratch_shapes=[pltpu.VMEM((512, 128), F4)],
        name="route",
        compiler_params=pltpu.CompilerParams(vmem_limit_bytes=16 * MIB),
    )(populations, before, behind, old, select, weights)


def collide_kernel(
    pop_ref,
    before_ref,
    behind_ref,
    relax_ref,
    master_ref,
    first_ref,
    second_ref,
    after_ref,
    state_ref,
):
    state_ref[0], state_ref[1], state_ref[2] = master_ref[...], first_ref[...], second_ref[...]
    read = streamed(pop_ref, before_ref, behind_ref)
    density, flow = moments(read)
    speed = flow[0] * flow[0] + flow[1] * flow[1] + flow[2] * flow[2]
    relaxation = relax_ref[...]
    for index in range(19):
        project = None
        for axis in range(3):
            along = VELOCITIES[index][axis]
            if along:
                term = flow[axis] if along > 0 else -flow[axis]
                project = term if project is None else project + term
        if project is None:
            shape = 1.0 - 1.5 * speed
        else:
            shape = 1.0 + 3.0 * project + 4.5 * project * project - 1.5 * speed
        balance = LATTICE_WEIGHTS[index] * density * shape
        after_ref[index] = read[index] - relaxation * (read[index] - balance)


def collide(populations, before, behind, relaxation, *state):
    return pl.pallas_call(
        collide_kernel,
        out_shape=(
            jax.ShapeDtypeStruct((19, 16, 256), F4),
            jax.ShapeDtypeStruct((3, 20, C), F4),
        ),
        name="collide",
        cost_estimate=pl.CostEstimate(flops=10**7, bytes_accessed=4 * 10**6, transcendentals=0),
        compiler_params=pltpu.CompilerParams(vmem_limit_bytes=16 * MIB),
    )(populations, before, behind, relaxation, *state)


def lift_kernel(
    arrived_ref,
    weight_ref,
    gain_ref,
    shift_ref,
    h_ref,
    target_ref,
    taps,
    lifted,
    sums,
    squares,
    means,
    scales,
):
    parts = []
    for pair in range(16):
        start = pair * 2 * BLOCK_ROWS
        block = arrived_ref[start : start + 2 * BLOCK_ROWS].astype(F4)
        parts += [block[0:16], block[BLOCK_ROWS : BLOCK_ROWS + 16]]
    arrived = jnp.concatenate(parts, axis=0).astype(BF)
    flags = (iota((32, 512), 1) == iota((32, 512), 0) * 16 + 6).astype(F4).astype(BF)
    flags = jnp.dot(flags, arrived, preferred_element_type=F4).astype(BF)
    source = iota((32, 512), 1) >> 4
    ahead = (iota((32, 512), 0) < source).astype(F4).astype(BF)
    same = (iota((32, 512), 0) == source).astype(F4).astype(BF)
    dims = (((0,), (0,)), ((), ()))
    place = lax.dot_general(flags, ahead, dims, preferred_element_type=F4)[0:1].astype(I4)
    live = lax.dot_general(flags, same, dims, preferred_element_type=F4)[0:1]
    lane = iota((1, 512), 1)
    key = jnp.where(live > 0.5, place * 16 + (lane & 15), -1)
    pick = (iota((256, 512), 0) == key).astype(F4).astype(BF)
    held = jnp.dot(pick, arrived, preferred_element_type=F4)
    for brick in range(32):
        target_ref[0:8, brick * 128 : (brick + 1) * 128] = held[brick * 8 : (brick + 1) * 8]
    target_ref[8:16, :] = jnp.zeros((8, CELLS), F4)
    cell = iota((8, 128), 1)
    cell_x, cell_y, cell_z = cell >> 5, (cell >> 3) & 3, cell & 7
    shifts = [(x, y, z) for x in (-1, 0, 1) for y in (-1, 0, 1) for z in (-1, 0, 1)]
    masks = []
    for x, y, z in shifts:
        inside = (cell_x + x >= 0) & (cell_x + x < 4) & (cell_y + y >= 0) & (cell_y + y < 4)
        masks.append(inside & (cell_z + z >= 0) & (cell_z + z < 8))
    weight = weight_ref[...]
    for start in range(0, CELLS, SPAN):
        part = slice(start, start + SPAN)
        for brick in range(start // 128, (start + SPAN) // 128):
            own = held[brick * 8 : (brick + 1) * 8]
            for pair in range(14):
                halves = []
                for tap in (2 * pair, 2 * pair + 1):
                    if tap == 27:
                        halves.append(jnp.zeros((8, 128), F4))
                        continue
                    x, y, z = shifts[tap]
                    turn = -(x * 32 + y * 8 + z) % 128
                    moved = pltpu.roll(own, turn, 1) if turn else own
                    halves.append(jnp.where(masks[tap], moved, 0.0))
                taps[pair * 16 : (pair + 1) * 16, brick * 128 : (brick + 1) * 128] = (
                    jnp.concatenate(halves, axis=0).astype(BF)
                )
        lifted[:, part] = jnp.dot(weight, taps[:, part], preferred_element_type=F4)
        for row in range(0, C, 16):
            rows = slice(row, row + 16)
            total = None
            for at in range(start, start + SPAN, 128):
                value = lifted[rows, at : at + 128]
                total = value if total is None else total + value
                square = value * value if at == start else square + value * value
            sums[rows, :] = total if start == 0 else sums[rows, :] + total
            squares[rows, :] = square if start == 0 else squares[rows, :] + square
    mean = jnp.sum(sums[...], axis=1, keepdims=True) / CELLS
    spread = jnp.sum(squares[...], axis=1, keepdims=True) / CELLS - mean * mean
    means[...] = jnp.broadcast_to(mean, (C, 128))
    scales[...] = lax.rsqrt(spread + 1e-05) * gain_ref[...]

    @pl.loop(0, CELLS // SPAN)
    def _(index):
        for row in range(0, C, 16):
            rows = slice(row, row + 16)
            mean, scale, shift = means[rows, :], scales[rows, :], shift_ref[rows, :]
            for at in range(0, SPAN, 128):
                part = pl.ds(pl.multiple_of(index * SPAN + at, 128), 128)
                normed = (lifted[rows, part] - mean) * scale + shift
                h_ref[rows, part] = gelu_value(normed).astype(BF)


def lift(arrived, weight, gain, shift):
    return pl.pallas_call(
        lift_kernel,
        out_shape=(
            jax.ShapeDtypeStruct((C, CELLS), BF),
            jax.ShapeDtypeStruct((16, CELLS), F4),
        ),
        scratch_shapes=[pltpu.VMEM((224, CELLS), BF), pltpu.VMEM((C, CELLS), F4)]
        + [pltpu.VMEM((C, 128), F4)] * 4,
        name="lift",
        compiler_params=pltpu.CompilerParams(vmem_limit_bytes=40 * MIB),
    )(arrived, weight, gain, shift)


def train_kernel(
    steps,
    layers,
    col_ref,
    h_ref,
    target_ref,
    mine_ref,
    other_ref,
    out_ref,
    send_ref,
    keep_ref,
    mix_ref,
    mix_back,
    states,
    slopes,
    ahead,
    back,
    inner,
    total,
):
    step = pl.program_id(0)
    cells = h_ref.shape[1]
    parts = [slice(start, start + 256) for start in range(0, cells, 256)]

    @pl.when(step == 0)
    def _():
        total[...] = jnp.zeros_like(total)
        even = col_ref[0] == 0
        upper = iota((8, 128), 0) < 4
        for pair in range(16):
            rows = slice(pair * 2 * BLOCK_ROWS, (pair + 1) * 2 * BLOCK_ROWS)
            mine = mine_ref[rows, :].astype(F4)
            other = other_ref[rows, :].astype(F4)
            tiles = []
            for start in (16, BLOCK_ROWS + 16):
                sides = ([], [])
                for index in range(7):
                    at = slice(start + index * 8, start + index * 8 + 8)
                    sides[0].append(jnp.where(even, mine[at], other[at]))
                    sides[1].append(jnp.where(even, other[at], mine[at]))
                left, right = unpack_piece(sides[0]), unpack_piece(sides[1])
                middle = [jnp.where(upper, a, b) for a, b in zip(left[2], right[2])]
                tiles += [left[0], left[1], middle, right[0], right[1]]
            for lanes in range(3):
                width = min(C - lanes * 128, 128)
                column = jnp.concatenate([tile[lanes] for tile in tiles], axis=0).astype(BF)
                mix_ref[pair * 80 : (pair + 1) * 80, lanes * 128 : lanes * 128 + width] = column[
                    :, 0:width
                ]
        same = (iota((C, C), 0) == iota((C, C), 1)).astype(F4).astype(BF)
        for layer in range(1, layers):
            rows = slice(layer * C, (layer + 1) * C)
            mix_back[rows, :] = lax.dot_general(
                mix_ref[rows, :], same, (((0,), (0,)), ((), ())), preferred_element_type=F4
            ).astype(BF)

    def state(layer):
        return h_ref if layer == 0 else states.at[layer - 1]

    for layer in range(layers):
        for part in parts:
            ahead[:, part] = jnp.dot(
                mix_ref[layer * C : (layer + 1) * C, :],
                state(layer)[:, part],
                preferred_element_type=F4,
            )
        for part in parts:
            for start in range(0, C, 16):
                rows = slice(start, start + 16)
                value, slope = gelu_both(ahead[rows, part])
                slopes[layer, rows, part] = slope
                states[layer, rows, part] = (state(layer)[rows, part].astype(F4) + value).astype(BF)
    for part in parts:
        output = jnp.dot(out_ref[...], states[layers - 1, :, part], preferred_element_type=F4)
        delta = ((output - target_ref[:, part]) * (2.0 / 384.0)).astype(BF)
        back[:, part] = lax.dot_general(
            out_ref[...], delta, (((0,), (0,)), ((), ())), preferred_element_type=F4
        )
    for layer in range(layers - 1, -1, -1):
        rows_of = slice(layer * C, (layer + 1) * C)
        for part in parts:
            for start in range(0, C, 16):
                rows = slice(start, start + 16)
                inner[layer, rows, part] = (back[rows, part] * slopes[layer, rows, part]).astype(BF)
        if layer > 0:
            for part in parts:
                back[:, part] += jnp.dot(
                    mix_back[rows_of, :], inner[layer, :, part], preferred_element_type=F4
                )
        total[rows_of, 0:C] += lax.dot_general(
            inner[layer], state(layer)[...], (((1,), (1,)), ((), ())), preferred_element_type=F4
        )

    @pl.when(step == steps - 1)
    def _():
        col = col_ref[0]
        for piece in range(32):
            for ref, side in ((keep_ref, col), (send_ref, 1 - col)):

                def tile(index, lanes):
                    start = piece * 40 + 16
                    if index < 2:
                        start = pl.multiple_of(piece * 40 + 24 * side + 8 * index, 8)
                    return total[pl.ds(start, 8), lanes * 128 : (lanes + 1) * 128]

                packed = pack_piece(tile, own_half(side))
                for index in range(7):
                    start = piece * WEIGHT_ROWS + index * 8
                    ref[start : start + 8, :] = packed[index]


def train(col, h, target, mine, other, out_weight):
    cells = 1024
    steps = CELLS // cells
    layers = 4
    block = pl.BlockSpec((32 * BLOCK_ROWS, 128), lambda i: (0, 0))
    return pl.pallas_call(
        functools.partial(train_kernel, steps, layers),
        grid=(steps,),
        in_specs=[
            pl.BlockSpec(memory_space=pltpu.SMEM),
            pl.BlockSpec((C, cells), lambda i: (0, i)),
            pl.BlockSpec((16, cells), lambda i: (0, i)),
            block,
            block,
            pl.BlockSpec((16, C), lambda i: (0, 0)),
        ],
        out_specs=(
            pl.BlockSpec((32 * WEIGHT_ROWS, 128), lambda i: (0, 0)),
            pl.BlockSpec((32 * WEIGHT_ROWS, 128), lambda i: (0, 0)),
        ),
        out_shape=(
            jax.ShapeDtypeStruct((32 * WEIGHT_ROWS, 128), F4),
            jax.ShapeDtypeStruct((32 * WEIGHT_ROWS, 128), F4),
        ),
        scratch_shapes=[
            pltpu.VMEM((layers * C, C), BF),
            pltpu.VMEM((layers * C, C), BF),
            pltpu.VMEM((layers, C, cells), BF),
            pltpu.VMEM((layers, C, cells), F4),
            pltpu.VMEM((C, cells), F4),
            pltpu.VMEM((C, cells), F4),
            pltpu.VMEM((layers, C, cells), BF),
            pltpu.VMEM((layers * C, WIDE), F4),
        ],
        name="train",
        compiler_params=pltpu.CompilerParams(vmem_limit_bytes=48 * MIB),
    )(col, h, target, mine, other, out_weight)


def update_kernel(col_ref, own_ref, other_ref, state_ref, new_ref, first_out, second_out):
    packed = own_ref[...] + other_ref[...]
    parts = unpack_piece([packed[index * 8 : index * 8 + 8] for index in range(7)])
    full, rest, half = [jnp.concatenate(part, axis=1) for part in parts]
    even = col_ref[0] == 0
    lower = jnp.concatenate([full, rest, half], axis=0)
    upper = pltpu.roll(jnp.concatenate([half, full, rest], axis=0), 20, 0)
    gradient = jnp.where(even, lower, upper)[0:20, 0:C]
    master = state_ref[0]
    first_next = 0.9 * state_ref[1] + 0.1 * gradient
    second_next = 0.999 * state_ref[2] + 0.001 * gradient * gradient
    ratio = first_next / (1.0 - 0.9**10) / (jnp.sqrt(second_next / (1.0 - 0.999**10)) + 1e-08)
    new_ref[...] = master - 0.01 * (ratio + 0.1 * master)
    first_out[...] = first_next
    second_out[...] = second_next


def update(col, own, other, state):
    vector = pl.BlockSpec(memory_space=pltpu.VMEM)
    return pl.pallas_call(
        update_kernel,
        in_specs=[pl.BlockSpec(memory_space=pltpu.SMEM)] + [vector] * 3,
        out_specs=(vector,) * 3,
        out_shape=(jax.ShapeDtypeStruct((20, C), F4),) * 3,
        name="update",
    )(col, own, other, state)


def body(
    populations,
    relaxation,
    send_lists,
    lift_weight,
    norm_gain,
    norm_shift,
    mix_master,
    mix_first,
    mix_second,
    out_weight,
):
    every = ("sec", "row", "col")
    size = lax.axis_size(every)
    swap = [(0, 1), (1, 0)]
    col = lax.axis_index("col").astype(I4)[None]
    up = [(i, (i + 1) % size) for i in range(size)]
    last, initial, populations = planes(populations)
    before = lax.ppermute(last, every, up)
    behind = lax.ppermute(initial, every, [(j, i) for i, j in up])
    small = gathered_rows(norm_gain, norm_shift, send_lists, out_weight, mix_master, lift_weight)
    old, select, weights, lift_rows, gain, shift, out_rows = prepare(col, populations, small)
    outgoing = route(populations, before, behind, old, select, weights)
    arrived = lax.all_to_all(
        outgoing.reshape(32, BLOCK_ROWS, 128), "row", split_axis=0, concat_axis=0, tiled=True
    ).reshape(32 * BLOCK_ROWS, 128)
    after, state = collide(
        populations, before, behind, relaxation, mix_master, mix_first, mix_second
    )
    other = lax.ppermute(arrived, "col", swap)
    h, target = lift(arrived, lift_rows, gain, shift)
    send, keep = train(col, h, target, arrived, other, out_rows)
    half = keep + lax.ppermute(send, "col", swap)
    terms = lax.all_to_all(
        half.reshape(32, WEIGHT_ROWS, 128), "row", split_axis=0, concat_axis=0, tiled=True
    )
    summed = jnp.sum(terms, axis=0)
    across = lax.ppermute(summed, "sec", swap)
    new_master, new_first, new_second = update(col, summed, across, state)
    return (after, new_master, new_first, new_second)


def solution(mesh):
    in_specs = (
        P(None, ("sec", "row", "col"), None),
        P(("sec", "row", "col"), None),
        P(("sec", "row", "col"), None),
        P(),
        P(),
        P(),
        P(("row", "col"), None),
        P(("row", "col"), None),
        P(("row", "col"), None),
        P(),
    )
    out_specs = (
        P(None, ("sec", "row", "col"), None),
        P(("row", "col"), None),
        P(("row", "col"), None),
        P(("row", "col"), None),
    )
    return jax.shard_map(body, mesh=mesh, in_specs=in_specs, out_specs=out_specs, check_vma=False)
```

```python
import functools

import jax
import jax.numpy as jnp
from jax import lax
from jax.experimental import pallas as pl
from jax.experimental.pallas import tpu as pltpu
from jax.sharding import PartitionSpec as P

BF = jnp.bfloat16
F4 = jnp.float32
I4 = jnp.int32
C = 320
CELLS = 4096
WEIGHT_ROWS = 56
BLOCK_ROWS = 16 + WEIGHT_ROWS
WIDE = 384
SPAN = 1024
MIB = 1024 * 1024

VELOCITIES = (
    (0, 0, 0),
    (1, 0, 0),
    (-1, 0, 0),
    (0, 1, 0),
    (0, -1, 0),
    (0, 0, 1),
    (0, 0, -1),
    (1, 1, 0),
    (-1, -1, 0),
    (1, -1, 0),
    (-1, 1, 0),
    (1, 0, 1),
    (-1, 0, -1),
    (1, 0, -1),
    (-1, 0, 1),
    (0, 1, 1),
    (0, -1, -1),
    (0, 1, -1),
    (0, -1, 1),
)
LATTICE_WEIGHTS = (1.0 / 3.0,) + (1.0 / 18.0,) * 6 + (1.0 / 36.0,) * 12

ROOT_HALF = 0.7071067811865476
EXP_SCALE = -0.5 * 1.4426950408889634


def iota(shape, dim):
    return lax.broadcasted_iota(I4, shape, dim)


def gelu_value(z):
    return z * (0.5 + 0.5 * lax.erf(z * ROOT_HALF))


def gelu_both(z):
    share = 0.5 + 0.5 * lax.erf(z * ROOT_HALF)
    bell = jnp.exp2(z * z * EXP_SCALE)
    return z * share, share + (z * 0.3989422804014327) * bell


def moments(read):
    density = read[0]
    moment = [None, None, None]
    for index in range(1, 19):
        density = density + read[index]
        for axis in range(3):
            along = VELOCITIES[index][axis]
            if along:
                term = read[index] if along > 0 else -read[index]
                moment[axis] = term if moment[axis] is None else moment[axis] + term
    return density, [moment[axis] / density for axis in range(3)]


def brick_rows(stacked):
    lane = iota((256, 256), 1)
    source = (lane & 0xC0) | (((lane >> 3) & 3) << 4) | (((lane >> 5) & 1) << 3) | (lane & 7)
    lanes = (iota((256, 256), 0) == source).astype(F4).astype(BF)
    row = iota((128, 96), 0)
    wanted = ((row >> 2) & 7) * 16 + (row & 3) * 4 + (row >> 5)
    rows = (iota((128, 96), 1) == wanted).astype(F4).astype(BF)
    moved = jnp.dot(stacked, lanes, preferred_element_type=F4).astype(BF)
    moved = jnp.dot(rows, moved, preferred_element_type=F4)
    part = iota((32, 128), 1) >> 5
    flag = (iota((32, 128), 0) >> 2) == 6
    groups = []
    for group in range(8):
        tile, place = group // 4, group % 4
        total = None
        for low in range(4):
            piece = moved[low * 32 : (low + 1) * 32, tile * 128 : (tile + 1) * 128]
            turn = (low - place) * 32 % 128
            if turn:
                piece = pltpu.roll(piece, turn, 1)
            total = piece if total is None else jnp.where(part == low, piece, total)
        groups.append(jnp.where(flag, 1.0, total))
    return jnp.concatenate(groups, axis=0).astype(BF)


def route_rows(targets):
    across = jnp.broadcast_to(targets, (32, 32)).astype(F4)
    first, second = iota((32, 32), 0), iota((32, 32), 1)
    down = jnp.sum(jnp.where(first == second, across, 0.0), axis=1, keepdims=True)
    earlier = (down == across) & (first < second)
    rank = jnp.sum(jnp.where(earlier, 1.0, 0.0), axis=0, keepdims=True)
    code = (2.0 * across[0:16] + rank).astype(BF)
    lane = iota((32, 256), 1)
    spread = (iota((32, 256), 0) == 8 * (lane & 3) + (lane >> 5)).astype(F4).astype(BF)
    code = jnp.dot(code, spread, preferred_element_type=F4)[0:1].astype(I4)
    key = code * 8 + ((iota((1, 256), 1) >> 2) & 7)
    return (iota((512, 256), 0) == key).astype(F4).astype(BF)


def own_half(col):
    return (iota((8, 128), 0) < 4) == (col == 0)


def pack_piece(tile, half):
    low = iota((8, 128), 1) < 64
    return [
        tile(0, 0),
        tile(0, 1),
        tile(1, 0),
        tile(1, 1),
        jnp.where(low, tile(0, 2), pltpu.roll(tile(1, 2), 64, 1)),
        jnp.where(half, tile(2, 0), pltpu.roll(tile(2, 1), 4, 0)),
        tile(2, 2),
    ]


def unpack_piece(tiles):
    return (
        (tiles[0], tiles[1], tiles[4]),
        (tiles[2], tiles[3], pltpu.roll(tiles[4], 64, 1)),
        (tiles[5], pltpu.roll(tiles[5], 4, 0), tiles[6]),
    )


def planes_kernel(pop_ref, last_ref, initial_ref, own_ref):
    own_ref[...] = pop_ref[...]
    for index in range(1, 15):
        last_ref[index - 1 : index, :] = pop_ref[index, 15:16, :]
        initial_ref[index - 1 : index, :] = pop_ref[index, 0:1, :]


def planes(populations):
    return pl.pallas_call(
        planes_kernel,
        out_shape=(jax.ShapeDtypeStruct((14, 256), F4),) * 2
        + (jax.ShapeDtypeStruct((19, 16, 256), F4),),
        name="planes",
        compiler_params=pltpu.CompilerParams(vmem_limit_bytes=16 * MIB),
    )(populations)


def gathered_rows(gain, shift, lists, out_weight, master, lift_weight):
    def placed(array, start):
        rows, lanes = array.shape
        return jnp.pad(array, ((start, 120 - start - rows), (0, C - lanes))).astype(F4)

    row = iota((120, C), 0)
    total = placed(lists, 2) + placed(out_weight, 3) + placed(master, 8) + placed(lift_weight.T, 32)
    return jnp.where(row == 0, gain, jnp.where(row == 1, shift, total))


def prepare_kernel(
    col_ref,
    pop_ref,
    small_ref,
    old_ref,
    select_ref,
    weights_ref,
    lift_out,
    gain_out,
    shift_out,
    rows_out,
    window,
):
    unused, old_flow = moments([pop_ref[index] for index in range(19)])
    old_ref[...] = jnp.concatenate(old_flow, axis=0).astype(BF)
    select_ref[...] = route_rows(small_ref[2:3, 0:32])
    col = col_ref[0]
    window[...] = jnp.zeros_like(window)

    @pl.when(col == 0)
    def _():
        window[0:20, 0:C] = small_ref[8:28, :]

    @pl.when(col != 0)
    def _():
        window[4:24, 0:C] = small_ref[8:28, :]

    def tile(index, lanes):
        start = pl.multiple_of((index * 8 + 8 * col) % 24, 8)
        return window[pl.ds(start, 8), lanes * 128 : (lanes + 1) * 128]

    weights_ref[...] = jnp.concatenate(pack_piece(tile, own_half(col)), axis=0)
    column = iota((88, 224), 1)
    feature = (column & 7) * 27 + (column >> 3)
    valid = ((column & 7) < 3) & (column < 216)
    spread = jnp.where(valid & (iota((88, 224), 0) == feature), 1.0, 0.0).astype(BF)
    lift_out[...] = lax.dot_general(
        small_ref[32:120, :].astype(BF),
        spread,
        (((0,), (0,)), ((), ())),
        preferred_element_type=F4,
    ).astype(BF)
    same = iota((C, C), 0) == iota((C, C), 1)
    for index, target in ((0, gain_out), (1, shift_out)):
        across = small_ref[index : index + 1, :]
        down = jnp.sum(jnp.where(same, across, 0.0), axis=1, keepdims=True)
        target[...] = jnp.broadcast_to(down, (C, 128))
    row = iota((8, C), 0)
    rows = jnp.where((row >= 3) & (row < 6), small_ref[0:8, :], 0.0)
    rows_out[...] = jnp.concatenate([rows, jnp.zeros_like(rows)], axis=0).astype(BF)


def prepare(col, populations, small):
    vector = pl.BlockSpec(memory_space=pltpu.VMEM)
    return pl.pallas_call(
        prepare_kernel,
        in_specs=[pl.BlockSpec(memory_space=pltpu.SMEM)] + [vector] * 2,
        out_specs=(vector,) * 7,
        out_shape=(
            jax.ShapeDtypeStruct((48, 256), BF),
            jax.ShapeDtypeStruct((512, 256), BF),
            jax.ShapeDtypeStruct((WEIGHT_ROWS, 128), F4),
            jax.ShapeDtypeStruct((C, 224), BF),
            jax.ShapeDtypeStruct((C, 128), F4),
            jax.ShapeDtypeStruct((C, 128), F4),
            jax.ShapeDtypeStruct((16, C), BF),
        ),
        scratch_shapes=[pltpu.VMEM((24, WIDE), F4)],
        name="prepare",
        cost_estimate=pl.CostEstimate(flops=10**7, bytes_accessed=4 * 10**6, transcendentals=0),
        compiler_params=pltpu.CompilerParams(vmem_limit_bytes=16 * MIB),
    )(col, populations, small)


def streamed(pop_ref, before_ref, behind_ref):
    row = iota((16, 256), 0)
    depth = iota((16, 256), 1) & 15
    read = []
    for index in range(19):
        along_x, along_y, along_z = VELOCITIES[index]
        plane = pop_ref[index]
        if along_x > 0:
            plane = jnp.where(row == 0, before_ref[index - 1 : index], pltpu.roll(plane, 1, 0))
        elif along_x < 0:
            plane = jnp.where(row == 15, behind_ref[index - 1 : index], pltpu.roll(plane, 15, 0))
        if along_y:
            plane = pltpu.roll(plane, along_y * 16 % 256, 1)
        if along_z > 0:
            plane = jnp.where(depth == 0, pltpu.roll(plane, 241, 1), pltpu.roll(plane, 1, 1))
        elif along_z < 0:
            plane = jnp.where(depth == 15, pltpu.roll(plane, 15, 1), pltpu.roll(plane, 255, 1))
        read.append(plane)
    return read


def route_kernel(
    pop_ref, before_ref, behind_ref, old_ref, select_ref, weights_ref, out_ref, routed
):
    density, flow = moments(streamed(pop_ref, before_ref, behind_ref))
    fields = jnp.concatenate([old_ref[...]] + [part.astype(BF) for part in flow], axis=0)
    bricks = brick_rows(fields)
    routed[...] = jnp.dot(select_ref[...], bricks, preferred_element_type=F4)
    weights = weights_ref[...]
    for pair in range(16):
        start = pair * 2 * BLOCK_ROWS
        first = routed[pair * 32 : pair * 32 + 16]
        second = routed[pair * 32 + 16 : pair * 32 + 32]
        out_ref[start : start + 2 * BLOCK_ROWS] = jnp.concatenate(
            [first, weights, second, weights], axis=0
        ).astype(BF)


def route(populations, before, behind, old, select, weights):
    return pl.pallas_call(
        route_kernel,
        out_shape=jax.ShapeDtypeStruct((32 * BLOCK_ROWS, 128), BF),
        scratch_shapes=[pltpu.VMEM((512, 128), F4)],
        name="route",
        compiler_params=pltpu.CompilerParams(vmem_limit_bytes=16 * MIB),
    )(populations, before, behind, old, select, weights)


def collide_kernel(
    pop_ref,
    before_ref,
    behind_ref,
    relax_ref,
    master_ref,
    first_ref,
    second_ref,
    after_ref,
    state_ref,
):
    state_ref[0], state_ref[1], state_ref[2] = master_ref[...], first_ref[...], second_ref[...]
    read = streamed(pop_ref, before_ref, behind_ref)
    density, flow = moments(read)
    speed = flow[0] * flow[0] + flow[1] * flow[1] + flow[2] * flow[2]
    relaxation = relax_ref[...]
    for index in range(19):
        project = None
        for axis in range(3):
            along = VELOCITIES[index][axis]
            if along:
                term = flow[axis] if along > 0 else -flow[axis]
                project = term if project is None else project + term
        if project is None:
            shape = 1.0 - 1.5 * speed
        else:
            shape = 1.0 + 3.0 * project + 4.5 * project * project - 1.5 * speed
        balance = LATTICE_WEIGHTS[index] * density * shape
        after_ref[index] = read[index] - relaxation * (read[index] - balance)


def collide(populations, before, behind, relaxation, *state):
    return pl.pallas_call(
        collide_kernel,
        out_shape=(
            jax.ShapeDtypeStruct((19, 16, 256), F4),
            jax.ShapeDtypeStruct((3, 20, C), F4),
        ),
        name="collide",
        cost_estimate=pl.CostEstimate(flops=10**7, bytes_accessed=4 * 10**6, transcendentals=0),
        compiler_params=pltpu.CompilerParams(vmem_limit_bytes=16 * MIB),
    )(populations, before, behind, relaxation, *state)


def lift_kernel(
    arrived_ref,
    weight_ref,
    gain_ref,
    shift_ref,
    h_ref,
    target_ref,
    taps,
    lifted,
    sums,
    squares,
    means,
    scales,
):
    parts = []
    for pair in range(16):
        start = pair * 2 * BLOCK_ROWS
        block = arrived_ref[start : start + 2 * BLOCK_ROWS].astype(F4)
        parts += [block[0:16], block[BLOCK_ROWS : BLOCK_ROWS + 16]]
    arrived = jnp.concatenate(parts, axis=0).astype(BF)
    flags = (iota((32, 512), 1) == iota((32, 512), 0) * 16 + 6).astype(F4).astype(BF)
    flags = jnp.dot(flags, arrived, preferred_element_type=F4).astype(BF)
    source = iota((32, 512), 1) >> 4
    ahead = (iota((32, 512), 0) < source).astype(F4).astype(BF)
    same = (iota((32, 512), 0) == source).astype(F4).astype(BF)
    dims = (((0,), (0,)), ((), ()))
    place = lax.dot_general(flags, ahead, dims, preferred_element_type=F4)[0:1].astype(I4)
    live = lax.dot_general(flags, same, dims, preferred_element_type=F4)[0:1]
    lane = iota((1, 512), 1)
    key = jnp.where(live > 0.5, place * 16 + (lane & 15), -1)
    pick = (iota((256, 512), 0) == key).astype(F4).astype(BF)
    held = jnp.dot(pick, arrived, preferred_element_type=F4)
    for brick in range(32):
        target_ref[0:8, brick * 128 : (brick + 1) * 128] = held[brick * 8 : (brick + 1) * 8]
    target_ref[8:16, :] = jnp.zeros((8, CELLS), F4)
    cell = iota((8, 128), 1)
    cell_x, cell_y, cell_z = cell >> 5, (cell >> 3) & 3, cell & 7
    shifts = [(x, y, z) for x in (-1, 0, 1) for y in (-1, 0, 1) for z in (-1, 0, 1)]
    masks = []
    for x, y, z in shifts:
        inside = (cell_x + x >= 0) & (cell_x + x < 4) & (cell_y + y >= 0) & (cell_y + y < 4)
        masks.append(inside & (cell_z + z >= 0) & (cell_z + z < 8))
    weight = weight_ref[...]
    for start in range(0, CELLS, SPAN):
        part = slice(start, start + SPAN)
        for brick in range(start // 128, (start + SPAN) // 128):
            own = held[brick * 8 : (brick + 1) * 8]
            for pair in range(14):
                halves = []
                for tap in (2 * pair, 2 * pair + 1):
                    if tap == 27:
                        halves.append(jnp.zeros((8, 128), F4))
                        continue
                    x, y, z = shifts[tap]
                    turn = -(x * 32 + y * 8 + z) % 128
                    moved = pltpu.roll(own, turn, 1) if turn else own
                    halves.append(jnp.where(masks[tap], moved, 0.0))
                taps[pair * 16 : (pair + 1) * 16, brick * 128 : (brick + 1) * 128] = (
                    jnp.concatenate(halves, axis=0).astype(BF)
                )
        lifted[:, part] = jnp.dot(weight, taps[:, part], preferred_element_type=F4)
        for row in range(0, C, 16):
            rows = slice(row, row + 16)
            total = None
            for at in range(start, start + SPAN, 128):
                value = lifted[rows, at : at + 128]
                total = value if total is None else total + value
                square = value * value if at == start else square + value * value
            sums[rows, :] = total if start == 0 else sums[rows, :] + total
            squares[rows, :] = square if start == 0 else squares[rows, :] + square
    mean = jnp.sum(sums[...], axis=1, keepdims=True) / CELLS
    spread = jnp.sum(squares[...], axis=1, keepdims=True) / CELLS - mean * mean
    means[...] = jnp.broadcast_to(mean, (C, 128))
    scales[...] = lax.rsqrt(spread + 1e-05) * gain_ref[...]

    @pl.loop(0, CELLS // SPAN)
    def _(index):
        for row in range(0, C, 16):
            rows = slice(row, row + 16)
            mean, scale, shift = means[rows, :], scales[rows, :], shift_ref[rows, :]
            for at in range(0, SPAN, 128):
                part = pl.ds(pl.multiple_of(index * SPAN + at, 128), 128)
                normed = (lifted[rows, part] - mean) * scale + shift
                h_ref[rows, part] = gelu_value(normed).astype(BF)


def lift(arrived, weight, gain, shift):
    return pl.pallas_call(
        lift_kernel,
        out_shape=(
            jax.ShapeDtypeStruct((C, CELLS), BF),
            jax.ShapeDtypeStruct((16, CELLS), F4),
        ),
        scratch_shapes=[pltpu.VMEM((224, CELLS), BF), pltpu.VMEM((C, CELLS), F4)]
        + [pltpu.VMEM((C, 128), F4)] * 4,
        name="lift",
        compiler_params=pltpu.CompilerParams(vmem_limit_bytes=40 * MIB),
    )(arrived, weight, gain, shift)


def train_kernel(
    steps,
    layers,
    col_ref,
    h_ref,
    target_ref,
    mine_ref,
    other_ref,
    out_ref,
    send_ref,
    keep_ref,
    mix_ref,
    mix_back,
    states,
    slopes,
    ahead,
    back,
    inner,
    total,
):
    step = pl.program_id(0)
    cells = h_ref.shape[1]
    parts = [slice(start, start + 256) for start in range(0, cells, 256)]

    @pl.when(step == 0)
    def _():
        total[...] = jnp.zeros_like(total)
        even = col_ref[0] == 0
        upper = iota((8, 128), 0) < 4
        for pair in range(16):
            rows = slice(pair * 2 * BLOCK_ROWS, (pair + 1) * 2 * BLOCK_ROWS)
            mine = mine_ref[rows, :].astype(F4)
            other = other_ref[rows, :].astype(F4)
            tiles = []
            for start in (16, BLOCK_ROWS + 16):
                sides = ([], [])
                for index in range(7):
                    at = slice(start + index * 8, start + index * 8 + 8)
                    sides[0].append(jnp.where(even, mine[at], other[at]))
                    sides[1].append(jnp.where(even, other[at], mine[at]))
                left, right = unpack_piece(sides[0]), unpack_piece(sides[1])
                middle = [jnp.where(upper, a, b) for a, b in zip(left[2], right[2])]
                tiles += [left[0], left[1], middle, right[0], right[1]]
            for lanes in range(3):
                width = min(C - lanes * 128, 128)
                column = jnp.concatenate([tile[lanes] for tile in tiles], axis=0).astype(BF)
                mix_ref[pair * 80 : (pair + 1) * 80, lanes * 128 : lanes * 128 + width] = column[
                    :, 0:width
                ]
        same = (iota((C, C), 0) == iota((C, C), 1)).astype(F4).astype(BF)
        for layer in range(1, layers):
            rows = slice(layer * C, (layer + 1) * C)
            mix_back[rows, :] = lax.dot_general(
                mix_ref[rows, :], same, (((0,), (0,)), ((), ())), preferred_element_type=F4
            ).astype(BF)

    def state(layer):
        return h_ref if layer == 0 else states.at[layer - 1]

    for layer in range(layers):
        for part in parts:
            ahead[:, part] = jnp.dot(
                mix_ref[layer * C : (layer + 1) * C, :],
                state(layer)[:, part],
                preferred_element_type=F4,
            )
        for part in parts:
            for start in range(0, C, 16):
                rows = slice(start, start + 16)
                value, slope = gelu_both(ahead[rows, part])
                slopes[layer, rows, part] = slope
                states[layer, rows, part] = (state(layer)[rows, part].astype(F4) + value).astype(BF)
    def descend(layer, part, change, first):
        for start in range(0, C, 16):
            rows = slice(start, start + 16)
            value = change[start : start + 16]
            if not first:
                value = back[rows, part] + value
            if layer > 0:
                back[rows, part] = value
            inner[layer, rows, part] = (value * slopes[layer, rows, part]).astype(BF)

    for part in parts:
        output = jnp.dot(out_ref[...], states[layers - 1, :, part], preferred_element_type=F4)
        delta = ((output - target_ref[:, part]) * (2.0 / 384.0)).astype(BF)
        change = lax.dot_general(
            out_ref[...], delta, (((0,), (0,)), ((), ())), preferred_element_type=F4
        )
        descend(layers - 1, part, change, True)
    for layer in range(layers - 1, -1, -1):
        rows_of = slice(layer * C, (layer + 1) * C)
        total[rows_of, 0:C] += lax.dot_general(
            inner[layer], state(layer)[...], (((1,), (1,)), ((), ())), preferred_element_type=F4
        )
        if layer > 0:
            for part in parts:
                change = jnp.dot(
                    mix_back[rows_of, :], inner[layer, :, part], preferred_element_type=F4
                )
                descend(layer - 1, part, change, False)

    @pl.when(step == steps - 1)
    def _():
        col = col_ref[0]
        for piece in range(32):
            for ref, side in ((keep_ref, col), (send_ref, 1 - col)):

                def tile(index, lanes):
                    start = piece * 40 + 16
                    if index < 2:
                        start = pl.multiple_of(piece * 40 + 24 * side + 8 * index, 8)
                    return total[pl.ds(start, 8), lanes * 128 : (lanes + 1) * 128]

                packed = pack_piece(tile, own_half(side))
                for index in range(7):
                    start = piece * WEIGHT_ROWS + index * 8
                    ref[start : start + 8, :] = packed[index]


def train(col, h, target, mine, other, out_weight):
    cells = 1024
    steps = CELLS // cells
    layers = 4
    block = pl.BlockSpec((32 * BLOCK_ROWS, 128), lambda i: (0, 0))
    return pl.pallas_call(
        functools.partial(train_kernel, steps, layers),
        grid=(steps,),
        in_specs=[
            pl.BlockSpec(memory_space=pltpu.SMEM),
            pl.BlockSpec((C, cells), lambda i: (0, i)),
            pl.BlockSpec((16, cells), lambda i: (0, i)),
            block,
            block,
            pl.BlockSpec((16, C), lambda i: (0, 0)),
        ],
        out_specs=(
            pl.BlockSpec((32 * WEIGHT_ROWS, 128), lambda i: (0, 0)),
            pl.BlockSpec((32 * WEIGHT_ROWS, 128), lambda i: (0, 0)),
        ),
        out_shape=(
            jax.ShapeDtypeStruct((32 * WEIGHT_ROWS, 128), F4),
            jax.ShapeDtypeStruct((32 * WEIGHT_ROWS, 128), F4),
        ),
        scratch_shapes=[
            pltpu.VMEM((layers * C, C), BF),
            pltpu.VMEM((layers * C, C), BF),
            pltpu.VMEM((layers, C, cells), BF),
            pltpu.VMEM((layers, C, cells), F4),
            pltpu.VMEM((C, cells), F4),
            pltpu.VMEM((C, cells), F4),
            pltpu.VMEM((layers, C, cells), BF),
            pltpu.VMEM((layers * C, WIDE), F4),
        ],
        name="train",
        compiler_params=pltpu.CompilerParams(vmem_limit_bytes=48 * MIB),
    )(col, h, target, mine, other, out_weight)


def update_kernel(col_ref, own_ref, other_ref, state_ref, new_ref, first_out, second_out):
    packed = own_ref[...] + other_ref[...]
    parts = unpack_piece([packed[index * 8 : index * 8 + 8] for index in range(7)])
    full, rest, half = [jnp.concatenate(part, axis=1) for part in parts]
    even = col_ref[0] == 0
    lower = jnp.concatenate([full, rest, half], axis=0)
    upper = pltpu.roll(jnp.concatenate([half, full, rest], axis=0), 20, 0)
    gradient = jnp.where(even, lower, upper)[0:20, 0:C]
    master = state_ref[0]
    first_next = 0.9 * state_ref[1] + 0.1 * gradient
    second_next = 0.999 * state_ref[2] + 0.001 * gradient * gradient
    ratio = first_next / (1.0 - 0.9**10) / (jnp.sqrt(second_next / (1.0 - 0.999**10)) + 1e-08)
    new_ref[...] = master - 0.01 * (ratio + 0.1 * master)
    first_out[...] = first_next
    second_out[...] = second_next


def update(col, own, other, state):
    vector = pl.BlockSpec(memory_space=pltpu.VMEM)
    return pl.pallas_call(
        update_kernel,
        in_specs=[pl.BlockSpec(memory_space=pltpu.SMEM)] + [vector] * 3,
        out_specs=(vector,) * 3,
        out_shape=(jax.ShapeDtypeStruct((20, C), F4),) * 3,
        name="update",
        compiler_params=pltpu.CompilerParams(vmem_limit_bytes=16 * MIB),
    )(col, own, other, state)


def body(
    populations,
    relaxation,
    send_lists,
    lift_weight,
    norm_gain,
    norm_shift,
    mix_master,
    mix_first,
    mix_second,
    out_weight,
):
    every = ("sec", "row", "col")
    size = lax.axis_size(every)
    swap = [(0, 1), (1, 0)]
    col = lax.axis_index("col").astype(I4)[None]
    up = [(i, (i + 1) % size) for i in range(size)]
    last, initial, populations = planes(populations)
    before = lax.ppermute(last, every, up)
    behind = lax.ppermute(initial, every, [(j, i) for i, j in up])
    small = gathered_rows(norm_gain, norm_shift, send_lists, out_weight, mix_master, lift_weight)
    old, select, weights, lift_rows, gain, shift, out_rows = prepare(col, populations, small)
    outgoing = route(populations, before, behind, old, select, weights)
    arrived = lax.all_to_all(
        outgoing.reshape(32, BLOCK_ROWS, 128), "row", split_axis=0, concat_axis=0, tiled=True
    ).reshape(32 * BLOCK_ROWS, 128)
    after, state = collide(
        populations, before, behind, relaxation, mix_master, mix_first, mix_second
    )
    other = lax.ppermute(arrived, "col", swap)
    h, target = lift(arrived, lift_rows, gain, shift)
    send, keep = train(col, h, target, arrived, other, out_rows)
    half = keep + lax.ppermute(send, "col", swap)
    terms = lax.all_to_all(
        half.reshape(32, WEIGHT_ROWS, 128), "row", split_axis=0, concat_axis=0, tiled=True
    )
    summed = jnp.sum(terms, axis=0)
    across = lax.ppermute(summed, "sec", swap)
    new_master, new_first, new_second = update(col, summed, across, state)
    return (after, new_master, new_first, new_second)


def solution(mesh):
    in_specs = (
        P(None, ("sec", "row", "col"), None),
        P(("sec", "row", "col"), None),
        P(("sec", "row", "col"), None),
        P(),
        P(),
        P(),
        P(("row", "col"), None),
        P(("row", "col"), None),
        P(("row", "col"), None),
        P(),
    )
    out_specs = (
        P(None, ("sec", "row", "col"), None),
        P(("row", "col"), None),
        P(("row", "col"), None),
        P(("row", "col"), None),
    )
    return jax.shard_map(body, mesh=mesh, in_specs=in_specs, out_specs=out_specs, check_vma=False)
```

```python
import functools

import jax
import jax.numpy as jnp
from jax import lax
from jax.experimental import pallas as pl
from jax.experimental.pallas import tpu as pltpu
from jax.sharding import PartitionSpec as P

BF = jnp.bfloat16
F4 = jnp.float32
I4 = jnp.int32
C = 320
CELLS = 4096
WEIGHT_ROWS = 56
BLOCK_ROWS = 16 + WEIGHT_ROWS
WIDE = 384
SPAN = 1024
MIB = 1024 * 1024

VELOCITIES = (
    (0, 0, 0),
    (1, 0, 0),
    (-1, 0, 0),
    (0, 1, 0),
    (0, -1, 0),
    (0, 0, 1),
    (0, 0, -1),
    (1, 1, 0),
    (-1, -1, 0),
    (1, -1, 0),
    (-1, 1, 0),
    (1, 0, 1),
    (-1, 0, -1),
    (1, 0, -1),
    (-1, 0, 1),
    (0, 1, 1),
    (0, -1, -1),
    (0, 1, -1),
    (0, -1, 1),
)
FORWARD = [index for index in range(19) if VELOCITIES[index][0] > 0]
BACKWARD = [index for index in range(19) if VELOCITIES[index][0] < 0]
LATTICE_WEIGHTS = (1.0 / 3.0,) + (1.0 / 18.0,) * 6 + (1.0 / 36.0,) * 12

ROOT_HALF = 0.7071067811865476
EXP_SCALE = -0.5 * 1.4426950408889634


def iota(shape, dim):
    return lax.broadcasted_iota(I4, shape, dim)


def gelu_value(z):
    return z * (0.5 + 0.5 * lax.erf(z * ROOT_HALF))


def gelu_both(z):
    share = 0.5 + 0.5 * lax.erf(z * ROOT_HALF)
    bell = jnp.exp2(z * z * EXP_SCALE)
    return z * share, share + (z * 0.3989422804014327) * bell


def moments(read):
    density = read[0]
    moment = [None, None, None]
    for index in range(1, 19):
        density = density + read[index]
        for axis in range(3):
            along = VELOCITIES[index][axis]
            if along:
                term = read[index] if along > 0 else -read[index]
                moment[axis] = term if moment[axis] is None else moment[axis] + term
    return density, [moment[axis] / density for axis in range(3)]


def brick_rows(stacked):
    lane = iota((256, 256), 1)
    source = (lane & 0xC0) | (((lane >> 3) & 3) << 4) | (((lane >> 5) & 1) << 3) | (lane & 7)
    lanes = (iota((256, 256), 0) == source).astype(F4).astype(BF)
    row = iota((128, 96), 0)
    wanted = ((row >> 2) & 7) * 16 + (row & 3) * 4 + (row >> 5)
    rows = (iota((128, 96), 1) == wanted).astype(F4).astype(BF)
    moved = jnp.dot(stacked, lanes, preferred_element_type=F4).astype(BF)
    moved = jnp.dot(rows, moved, preferred_element_type=F4)
    part = iota((32, 128), 1) >> 5
    flag = (iota((32, 128), 0) >> 2) == 6
    groups = []
    for group in range(8):
        tile, place = group // 4, group % 4
        total = None
        for low in range(4):
            piece = moved[low * 32 : (low + 1) * 32, tile * 128 : (tile + 1) * 128]
            turn = (low - place) * 32 % 128
            if turn:
                piece = pltpu.roll(piece, turn, 1)
            total = piece if total is None else jnp.where(part == low, piece, total)
        groups.append(jnp.where(flag, 1.0, total))
    return jnp.concatenate(groups, axis=0).astype(BF)


def route_rows(targets):
    across = jnp.broadcast_to(targets, (32, 32)).astype(F4)
    first, second = iota((32, 32), 0), iota((32, 32), 1)
    down = jnp.sum(jnp.where(first == second, across, 0.0), axis=1, keepdims=True)
    earlier = (down == across) & (first < second)
    rank = jnp.sum(jnp.where(earlier, 1.0, 0.0), axis=0, keepdims=True)
    code = (2.0 * across[0:16] + rank).astype(BF)
    lane = iota((32, 256), 1)
    spread = (iota((32, 256), 0) == 8 * (lane & 3) + (lane >> 5)).astype(F4).astype(BF)
    code = jnp.dot(code, spread, preferred_element_type=F4)[0:1].astype(I4)
    key = code * 8 + ((iota((1, 256), 1) >> 2) & 7)
    return (iota((512, 256), 0) == key).astype(F4).astype(BF)


def own_half(col):
    return (iota((8, 128), 0) < 4) == (col == 0)


def pack_piece(tile, half):
    low = iota((8, 128), 1) < 64
    return [
        tile(0, 0),
        tile(0, 1),
        tile(1, 0),
        tile(1, 1),
        jnp.where(low, tile(0, 2), pltpu.roll(tile(1, 2), 64, 1)),
        jnp.where(half, tile(2, 0), pltpu.roll(tile(2, 1), 4, 0)),
        tile(2, 2),
    ]


def unpack_piece(tiles):
    return (
        (tiles[0], tiles[1], tiles[4]),
        (tiles[2], tiles[3], pltpu.roll(tiles[4], 64, 1)),
        (tiles[5], pltpu.roll(tiles[5], 4, 0), tiles[6]),
    )


def planes_kernel(pop_ref, last_ref, initial_ref, own_ref):
    own_ref[...] = pop_ref[...]
    for ref, indices, row in ((last_ref, FORWARD, 15), (initial_ref, BACKWARD, 0)):
        ref[...] = jnp.zeros_like(ref)
        for slot, index in enumerate(indices):
            ref[slot : slot + 1, :] = pop_ref[index, row : row + 1, :]


def planes(populations):
    return pl.pallas_call(
        planes_kernel,
        out_shape=(jax.ShapeDtypeStruct((8, 256), F4),) * 2
        + (jax.ShapeDtypeStruct((19, 16, 256), F4),),
        name="planes",
        compiler_params=pltpu.CompilerParams(vmem_limit_bytes=16 * MIB),
    )(populations)


def gathered_rows(gain, shift, lists, out_weight, master, lift_weight):
    def placed(array, start):
        rows, lanes = array.shape
        return jnp.pad(array, ((start, 120 - start - rows), (0, C - lanes))).astype(F4)

    row = iota((120, C), 0)
    total = placed(lists, 2) + placed(out_weight, 3) + placed(master, 8) + placed(lift_weight.T, 32)
    return jnp.where(row == 0, gain, jnp.where(row == 1, shift, total))


def prepare_kernel(
    col_ref,
    pop_ref,
    small_ref,
    old_ref,
    select_ref,
    weights_ref,
    lift_out,
    gain_out,
    shift_out,
    rows_out,
    window,
):
    unused, old_flow = moments([pop_ref[index] for index in range(19)])
    old_ref[...] = jnp.concatenate(old_flow, axis=0).astype(BF)
    select_ref[...] = route_rows(small_ref[2:3, 0:32])
    col = col_ref[0]
    window[...] = jnp.zeros_like(window)

    @pl.when(col == 0)
    def _():
        window[0:20, 0:C] = small_ref[8:28, :]

    @pl.when(col != 0)
    def _():
        window[4:24, 0:C] = small_ref[8:28, :]

    def tile(index, lanes):
        start = pl.multiple_of((index * 8 + 8 * col) % 24, 8)
        return window[pl.ds(start, 8), lanes * 128 : (lanes + 1) * 128]

    weights_ref[...] = jnp.concatenate(pack_piece(tile, own_half(col)), axis=0)
    column = iota((88, 224), 1)
    feature = (column & 7) * 27 + (column >> 3)
    valid = ((column & 7) < 3) & (column < 216)
    spread = jnp.where(valid & (iota((88, 224), 0) == feature), 1.0, 0.0).astype(BF)
    lift_out[...] = lax.dot_general(
        small_ref[32:120, :].astype(BF),
        spread,
        (((0,), (0,)), ((), ())),
        preferred_element_type=F4,
    ).astype(BF)
    same = iota((C, C), 0) == iota((C, C), 1)
    for index, target in ((0, gain_out), (1, shift_out)):
        across = small_ref[index : index + 1, :]
        down = jnp.sum(jnp.where(same, across, 0.0), axis=1, keepdims=True)
        target[...] = jnp.broadcast_to(down, (C, 128))
    row = iota((8, C), 0)
    rows = jnp.where((row >= 3) & (row < 6), small_ref[0:8, :], 0.0)
    rows_out[...] = jnp.concatenate([rows, jnp.zeros_like(rows)], axis=0).astype(BF)


def prepare(col, populations, small):
    vector = pl.BlockSpec(memory_space=pltpu.VMEM)
    return pl.pallas_call(
        prepare_kernel,
        in_specs=[pl.BlockSpec(memory_space=pltpu.SMEM)] + [vector] * 2,
        out_specs=(vector,) * 7,
        out_shape=(
            jax.ShapeDtypeStruct((48, 256), BF),
            jax.ShapeDtypeStruct((512, 256), BF),
            jax.ShapeDtypeStruct((WEIGHT_ROWS, 128), F4),
            jax.ShapeDtypeStruct((C, 224), BF),
            jax.ShapeDtypeStruct((C, 128), F4),
            jax.ShapeDtypeStruct((C, 128), F4),
            jax.ShapeDtypeStruct((16, C), BF),
        ),
        scratch_shapes=[pltpu.VMEM((24, WIDE), F4)],
        name="prepare",
        cost_estimate=pl.CostEstimate(flops=10**7, bytes_accessed=4 * 10**6, transcendentals=0),
        compiler_params=pltpu.CompilerParams(vmem_limit_bytes=16 * MIB),
    )(col, populations, small)


def streamed(pop_ref, before_ref, behind_ref):
    row = iota((16, 256), 0)
    depth = iota((16, 256), 1) & 15
    read = []
    for index in range(19):
        along_x, along_y, along_z = VELOCITIES[index]
        plane = pop_ref[index]
        if along_x > 0:
            at = FORWARD.index(index)
            plane = jnp.where(row == 0, before_ref[at : at + 1], pltpu.roll(plane, 1, 0))
        elif along_x < 0:
            at = BACKWARD.index(index)
            plane = jnp.where(row == 15, behind_ref[at : at + 1], pltpu.roll(plane, 15, 0))
        if along_y:
            plane = pltpu.roll(plane, along_y * 16 % 256, 1)
        if along_z > 0:
            plane = jnp.where(depth == 0, pltpu.roll(plane, 241, 1), pltpu.roll(plane, 1, 1))
        elif along_z < 0:
            plane = jnp.where(depth == 15, pltpu.roll(plane, 15, 1), pltpu.roll(plane, 255, 1))
        read.append(plane)
    return read


def route_kernel(
    pop_ref, before_ref, behind_ref, old_ref, select_ref, weights_ref, out_ref, routed
):
    density, flow = moments(streamed(pop_ref, before_ref, behind_ref))
    fields = jnp.concatenate([old_ref[...]] + [part.astype(BF) for part in flow], axis=0)
    bricks = brick_rows(fields)
    routed[...] = jnp.dot(select_ref[...], bricks, preferred_element_type=F4)
    weights = weights_ref[...]
    for pair in range(16):
        start = pair * 2 * BLOCK_ROWS
        first = routed[pair * 32 : pair * 32 + 16]
        second = routed[pair * 32 + 16 : pair * 32 + 32]
        out_ref[start : start + 2 * BLOCK_ROWS] = jnp.concatenate(
            [first, weights, second, weights], axis=0
        ).astype(BF)


def route(populations, before, behind, old, select, weights):
    return pl.pallas_call(
        route_kernel,
        out_shape=jax.ShapeDtypeStruct((32 * BLOCK_ROWS, 128), BF),
        scratch_shapes=[pltpu.VMEM((512, 128), F4)],
        name="route",
        compiler_params=pltpu.CompilerParams(vmem_limit_bytes=16 * MIB),
    )(populations, before, behind, old, select, weights)


def collide_kernel(
    pop_ref,
    before_ref,
    behind_ref,
    relax_ref,
    master_ref,
    first_ref,
    second_ref,
    after_ref,
    state_ref,
):
    state_ref[0], state_ref[1], state_ref[2] = master_ref[...], first_ref[...], second_ref[...]
    read = streamed(pop_ref, before_ref, behind_ref)
    density, flow = moments(read)
    speed = flow[0] * flow[0] + flow[1] * flow[1] + flow[2] * flow[2]
    relaxation = relax_ref[...]
    for index in range(19):
        project = None
        for axis in range(3):
            along = VELOCITIES[index][axis]
            if along:
                term = flow[axis] if along > 0 else -flow[axis]
                project = term if project is None else project + term
        if project is None:
            shape = 1.0 - 1.5 * speed
        else:
            shape = 1.0 + 3.0 * project + 4.5 * project * project - 1.5 * speed
        balance = LATTICE_WEIGHTS[index] * density * shape
        after_ref[index] = read[index] - relaxation * (read[index] - balance)


def collide(populations, before, behind, relaxation, *state):
    return pl.pallas_call(
        collide_kernel,
        out_shape=(
            jax.ShapeDtypeStruct((19, 16, 256), F4),
            jax.ShapeDtypeStruct((3, 20, C), F4),
        ),
        name="collide",
        cost_estimate=pl.CostEstimate(flops=10**7, bytes_accessed=4 * 10**6, transcendentals=0),
        compiler_params=pltpu.CompilerParams(vmem_limit_bytes=16 * MIB),
    )(populations, before, behind, relaxation, *state)


def lift_kernel(
    arrived_ref,
    weight_ref,
    gain_ref,
    shift_ref,
    h_ref,
    target_ref,
    taps,
    lifted,
    sums,
    squares,
    means,
    scales,
):
    parts = []
    for pair in range(16):
        start = pair * 2 * BLOCK_ROWS
        block = arrived_ref[start : start + 2 * BLOCK_ROWS].astype(F4)
        parts += [block[0:16], block[BLOCK_ROWS : BLOCK_ROWS + 16]]
    arrived = jnp.concatenate(parts, axis=0).astype(BF)
    flags = (iota((32, 512), 1) == iota((32, 512), 0) * 16 + 6).astype(F4).astype(BF)
    flags = jnp.dot(flags, arrived, preferred_element_type=F4).astype(BF)
    source = iota((32, 512), 1) >> 4
    ahead = (iota((32, 512), 0) < source).astype(F4).astype(BF)
    same = (iota((32, 512), 0) == source).astype(F4).astype(BF)
    dims = (((0,), (0,)), ((), ()))
    place = lax.dot_general(flags, ahead, dims, preferred_element_type=F4)[0:1].astype(I4)
    live = lax.dot_general(flags, same, dims, preferred_element_type=F4)[0:1]
    lane = iota((1, 512), 1)
    key = jnp.where(live > 0.5, place * 16 + (lane & 15), -1)
    pick = (iota((256, 512), 0) == key).astype(F4).astype(BF)
    held = jnp.dot(pick, arrived, preferred_element_type=F4)
    for brick in range(32):
        target_ref[0:8, brick * 128 : (brick + 1) * 128] = held[brick * 8 : (brick + 1) * 8]
    target_ref[8:16, :] = jnp.zeros((8, CELLS), F4)
    cell = iota((8, 128), 1)
    cell_x, cell_y, cell_z = cell >> 5, (cell >> 3) & 3, cell & 7
    shifts = [(x, y, z) for x in (-1, 0, 1) for y in (-1, 0, 1) for z in (-1, 0, 1)]
    masks = []
    for x, y, z in shifts:
        inside = (cell_x + x >= 0) & (cell_x + x < 4) & (cell_y + y >= 0) & (cell_y + y < 4)
        masks.append(inside & (cell_z + z >= 0) & (cell_z + z < 8))
    weight = weight_ref[...]
    for start in range(0, CELLS, SPAN):
        part = slice(start, start + SPAN)
        for brick in range(start // 128, (start + SPAN) // 128):
            own = held[brick * 8 : (brick + 1) * 8]
            for pair in range(14):
                halves = []
                for tap in (2 * pair, 2 * pair + 1):
                    if tap == 27:
                        halves.append(jnp.zeros((8, 128), F4))
                        continue
                    x, y, z = shifts[tap]
                    turn = -(x * 32 + y * 8 + z) % 128
                    moved = pltpu.roll(own, turn, 1) if turn else own
                    halves.append(jnp.where(masks[tap], moved, 0.0))
                taps[pair * 16 : (pair + 1) * 16, brick * 128 : (brick + 1) * 128] = (
                    jnp.concatenate(halves, axis=0).astype(BF)
                )
        lifted[:, part] = jnp.dot(weight, taps[:, part], preferred_element_type=F4)
        for row in range(0, C, 16):
            rows = slice(row, row + 16)
            total = None
            for at in range(start, start + SPAN, 128):
                value = lifted[rows, at : at + 128]
                total = value if total is None else total + value
                square = value * value if at == start else square + value * value
            sums[rows, :] = total if start == 0 else sums[rows, :] + total
            squares[rows, :] = square if start == 0 else squares[rows, :] + square
    mean = jnp.sum(sums[...], axis=1, keepdims=True) / CELLS
    spread = jnp.sum(squares[...], axis=1, keepdims=True) / CELLS - mean * mean
    means[...] = jnp.broadcast_to(mean, (C, 128))
    scales[...] = lax.rsqrt(spread + 1e-05) * gain_ref[...]

    @pl.loop(0, CELLS // SPAN)
    def _(index):
        for row in range(0, C, 16):
            rows = slice(row, row + 16)
            mean, scale, shift = means[rows, :], scales[rows, :], shift_ref[rows, :]
            for at in range(0, SPAN, 128):
                part = pl.ds(pl.multiple_of(index * SPAN + at, 128), 128)
                normed = (lifted[rows, part] - mean) * scale + shift
                h_ref[rows, part] = gelu_value(normed).astype(BF)


def lift(arrived, weight, gain, shift):
    return pl.pallas_call(
        lift_kernel,
        out_shape=(
            jax.ShapeDtypeStruct((C, CELLS), BF),
            jax.ShapeDtypeStruct((16, CELLS), F4),
        ),
        scratch_shapes=[pltpu.VMEM((224, CELLS), BF), pltpu.VMEM((C, CELLS), F4)]
        + [pltpu.VMEM((C, 128), F4)] * 4,
        name="lift",
        compiler_params=pltpu.CompilerParams(vmem_limit_bytes=40 * MIB),
    )(arrived, weight, gain, shift)


def train_kernel(
    steps,
    layers,
    col_ref,
    h_ref,
    target_ref,
    mine_ref,
    other_ref,
    out_ref,
    send_ref,
    keep_ref,
    mix_ref,
    mix_back,
    states,
    slopes,
    ahead,
    back,
    inner,
    total,
):
    step = pl.program_id(0)
    cells = h_ref.shape[1]
    parts = [slice(start, start + 256) for start in range(0, cells, 256)]

    @pl.when(step == 0)
    def _():
        total[...] = jnp.zeros_like(total)
        even = col_ref[0] == 0
        upper = iota((8, 128), 0) < 4
        for pair in range(16):
            rows = slice(pair * 2 * BLOCK_ROWS, (pair + 1) * 2 * BLOCK_ROWS)
            mine = mine_ref[rows, :].astype(F4)
            other = other_ref[rows, :].astype(F4)
            tiles = []
            for start in (16, BLOCK_ROWS + 16):
                sides = ([], [])
                for index in range(7):
                    at = slice(start + index * 8, start + index * 8 + 8)
                    sides[0].append(jnp.where(even, mine[at], other[at]))
                    sides[1].append(jnp.where(even, other[at], mine[at]))
                left, right = unpack_piece(sides[0]), unpack_piece(sides[1])
                middle = [jnp.where(upper, a, b) for a, b in zip(left[2], right[2])]
                tiles += [left[0], left[1], middle, right[0], right[1]]
            for lanes in range(3):
                width = min(C - lanes * 128, 128)
                column = jnp.concatenate([tile[lanes] for tile in tiles], axis=0).astype(BF)
                mix_ref[pair * 80 : (pair + 1) * 80, lanes * 128 : lanes * 128 + width] = column[
                    :, 0:width
                ]
        same = (iota((C, C), 0) == iota((C, C), 1)).astype(F4).astype(BF)
        for layer in range(1, layers):
            rows = slice(layer * C, (layer + 1) * C)
            mix_back[rows, :] = lax.dot_general(
                mix_ref[rows, :], same, (((0,), (0,)), ((), ())), preferred_element_type=F4
            ).astype(BF)

    def state(layer):
        return h_ref if layer == 0 else states.at[layer - 1]

    for layer in range(layers):
        for part in parts:
            ahead[:, part] = jnp.dot(
                mix_ref[layer * C : (layer + 1) * C, :],
                state(layer)[:, part],
                preferred_element_type=F4,
            )
        for part in parts:
            for start in range(0, C, 16):
                rows = slice(start, start + 16)
                value, slope = gelu_both(ahead[rows, part])
                slopes[layer, rows, part] = slope
                states[layer, rows, part] = (state(layer)[rows, part].astype(F4) + value).astype(BF)
    def descend(layer, part, change, first):
        for start in range(0, C, 16):
            rows = slice(start, start + 16)
            value = change[start : start + 16]
            if not first:
                value = back[rows, part] + value
            if layer > 0:
                back[rows, part] = value
            inner[layer, rows, part] = (value * slopes[layer, rows, part]).astype(BF)

    for part in parts:
        output = jnp.dot(out_ref[...], states[layers - 1, :, part], preferred_element_type=F4)
        delta = ((output - target_ref[:, part]) * (2.0 / 384.0)).astype(BF)
        change = lax.dot_general(
            out_ref[...], delta, (((0,), (0,)), ((), ())), preferred_element_type=F4
        )
        descend(layers - 1, part, change, True)
    for layer in range(layers - 1, -1, -1):
        rows_of = slice(layer * C, (layer + 1) * C)
        total[rows_of, 0:C] += lax.dot_general(
            inner[layer], state(layer)[...], (((1,), (1,)), ((), ())), preferred_element_type=F4
        )
        if layer > 0:
            for part in parts:
                change = jnp.dot(
                    mix_back[rows_of, :], inner[layer, :, part], preferred_element_type=F4
                )
                descend(layer - 1, part, change, False)

    @pl.when(step == steps - 1)
    def _():
        col = col_ref[0]
        for piece in range(32):
            for ref, side in ((keep_ref, col), (send_ref, 1 - col)):

                def tile(index, lanes):
                    start = piece * 40 + 16
                    if index < 2:
                        start = pl.multiple_of(piece * 40 + 24 * side + 8 * index, 8)
                    return total[pl.ds(start, 8), lanes * 128 : (lanes + 1) * 128]

                packed = pack_piece(tile, own_half(side))
                for index in range(7):
                    start = piece * WEIGHT_ROWS + index * 8
                    ref[start : start + 8, :] = packed[index]


def train(col, h, target, mine, other, out_weight):
    cells = 1024
    steps = CELLS // cells
    layers = 4
    block = pl.BlockSpec((32 * BLOCK_ROWS, 128), lambda i: (0, 0))
    return pl.pallas_call(
        functools.partial(train_kernel, steps, layers),
        grid=(steps,),
        in_specs=[
            pl.BlockSpec(memory_space=pltpu.SMEM),
            pl.BlockSpec((C, cells), lambda i: (0, i)),
            pl.BlockSpec((16, cells), lambda i: (0, i)),
            block,
            block,
            pl.BlockSpec((16, C), lambda i: (0, 0)),
        ],
        out_specs=(
            pl.BlockSpec((32 * WEIGHT_ROWS, 128), lambda i: (0, 0)),
            pl.BlockSpec((32 * WEIGHT_ROWS, 128), lambda i: (0, 0)),
        ),
        out_shape=(
            jax.ShapeDtypeStruct((32 * WEIGHT_ROWS, 128), F4),
            jax.ShapeDtypeStruct((32 * WEIGHT_ROWS, 128), F4),
        ),
        scratch_shapes=[
            pltpu.VMEM((layers * C, C), BF),
            pltpu.VMEM((layers * C, C), BF),
            pltpu.VMEM((layers, C, cells), BF),
            pltpu.VMEM((layers, C, cells), F4),
            pltpu.VMEM((C, cells), F4),
            pltpu.VMEM((C, cells), F4),
            pltpu.VMEM((layers, C, cells), BF),
            pltpu.VMEM((layers * C, WIDE), F4),
        ],
        name="train",
        compiler_params=pltpu.CompilerParams(vmem_limit_bytes=48 * MIB),
    )(col, h, target, mine, other, out_weight)


def update_kernel(col_ref, own_ref, other_ref, state_ref, new_ref, first_out, second_out):
    packed = own_ref[...] + other_ref[...]
    parts = unpack_piece([packed[index * 8 : index * 8 + 8] for index in range(7)])
    full, rest, half = [jnp.concatenate(part, axis=1) for part in parts]
    even = col_ref[0] == 0
    lower = jnp.concatenate([full, rest, half], axis=0)
    upper = pltpu.roll(jnp.concatenate([half, full, rest], axis=0), 20, 0)
    gradient = jnp.where(even, lower, upper)[0:20, 0:C]
    master = state_ref[0]
    first_next = 0.9 * state_ref[1] + 0.1 * gradient
    second_next = 0.999 * state_ref[2] + 0.001 * gradient * gradient
    ratio = first_next / (1.0 - 0.9**10) / (jnp.sqrt(second_next / (1.0 - 0.999**10)) + 1e-08)
    new_ref[...] = master - 0.01 * (ratio + 0.1 * master)
    first_out[...] = first_next
    second_out[...] = second_next


def update(col, own, other, state):
    vector = pl.BlockSpec(memory_space=pltpu.VMEM)
    return pl.pallas_call(
        update_kernel,
        in_specs=[pl.BlockSpec(memory_space=pltpu.SMEM)] + [vector] * 3,
        out_specs=(vector,) * 3,
        out_shape=(jax.ShapeDtypeStruct((20, C), F4),) * 3,
        name="update",
        compiler_params=pltpu.CompilerParams(vmem_limit_bytes=16 * MIB),
    )(col, own, other, state)


def body(
    populations,
    relaxation,
    send_lists,
    lift_weight,
    norm_gain,
    norm_shift,
    mix_master,
    mix_first,
    mix_second,
    out_weight,
):
    every = ("sec", "row", "col")
    size = lax.axis_size(every)
    swap = [(0, 1), (1, 0)]
    col = lax.axis_index("col").astype(I4)[None]
    up = [(i, (i + 1) % size) for i in range(size)]
    last, initial, populations = planes(populations)
    behind = lax.ppermute(initial, every, [(j, i) for i, j in up])
    before = lax.ppermute(last, every, up)
    small = gathered_rows(norm_gain, norm_shift, send_lists, out_weight, mix_master, lift_weight)
    old, select, weights, lift_rows, gain, shift, out_rows = prepare(col, populations, small)
    outgoing = route(populations, before, behind, old, select, weights)
    arrived = lax.all_to_all(
        outgoing.reshape(32, BLOCK_ROWS, 128), "row", split_axis=0, concat_axis=0, tiled=True
    ).reshape(32 * BLOCK_ROWS, 128)
    after, state = collide(
        populations, before, behind, relaxation, mix_master, mix_first, mix_second
    )
    other = lax.ppermute(arrived, "col", swap)
    h, target = lift(arrived, lift_rows, gain, shift)
    send, keep = train(col, h, target, arrived, other, out_rows)
    half = keep + lax.ppermute(send, "col", swap)
    terms = lax.all_to_all(
        half.reshape(32, WEIGHT_ROWS, 128), "row", split_axis=0, concat_axis=0, tiled=True
    )
    summed = jnp.sum(terms, axis=0)
    across = lax.ppermute(summed, "sec", swap)
    new_master, new_first, new_second = update(col, summed, across, state)
    return (after, new_master, new_first, new_second)


def solution(mesh):
    in_specs = (
        P(None, ("sec", "row", "col"), None),
        P(("sec", "row", "col"), None),
        P(("sec", "row", "col"), None),
        P(),
        P(),
        P(),
        P(("row", "col"), None),
        P(("row", "col"), None),
        P(("row", "col"), None),
        P(),
    )
    out_specs = (
        P(None, ("sec", "row", "col"), None),
        P(("row", "col"), None),
        P(("row", "col"), None),
        P(("row", "col"), None),
    )
    return jax.shard_map(body, mesh=mesh, in_specs=in_specs, out_specs=out_specs, check_vma=False)
```

```python
import functools

import jax
import jax.numpy as jnp
from jax import lax
from jax.experimental import pallas as pl
from jax.experimental.pallas import tpu as pltpu
from jax.sharding import PartitionSpec as P

BF = jnp.bfloat16
F4 = jnp.float32
I4 = jnp.int32
C = 320
CELLS = 4096
WEIGHT_ROWS = 56
BLOCK_ROWS = 16 + WEIGHT_ROWS
WIDE = 384
SPAN = 1024
TOP_POWER = 14.0
MIB = 1024 * 1024

VELOCITIES = (
    (0, 0, 0),
    (1, 0, 0),
    (-1, 0, 0),
    (0, 1, 0),
    (0, -1, 0),
    (0, 0, 1),
    (0, 0, -1),
    (1, 1, 0),
    (-1, -1, 0),
    (1, -1, 0),
    (-1, 1, 0),
    (1, 0, 1),
    (-1, 0, -1),
    (1, 0, -1),
    (-1, 0, 1),
    (0, 1, 1),
    (0, -1, -1),
    (0, 1, -1),
    (0, -1, 1),
)
FORWARD = [index for index in range(19) if VELOCITIES[index][0] > 0]
BACKWARD = [index for index in range(19) if VELOCITIES[index][0] < 0]
LATTICE_WEIGHTS = (1.0 / 3.0,) + (1.0 / 18.0,) * 6 + (1.0 / 36.0,) * 12

ROOT_HALF = 0.7071067811865476
EXP_SCALE = -0.5 * 1.4426950408889634


def iota(shape, dim):
    return lax.broadcasted_iota(I4, shape, dim)


def gelu_value(z):
    return z * (0.5 + 0.5 * lax.erf(z * ROOT_HALF))


def gelu_both(z):
    share = 0.5 + 0.5 * lax.erf(z * ROOT_HALF)
    bell = jnp.exp2(z * z * EXP_SCALE)
    return z * share, share + (z * 0.3989422804014327) * bell


def moments(read):
    density = read[0]
    moment = [None, None, None]
    for index in range(1, 19):
        density = density + read[index]
        for axis in range(3):
            along = VELOCITIES[index][axis]
            if along:
                term = read[index] if along > 0 else -read[index]
                moment[axis] = term if moment[axis] is None else moment[axis] + term
    return density, [moment[axis] / density for axis in range(3)]


def brick_rows(stacked):
    lane = iota((256, 256), 1)
    source = (lane & 0xC0) | (((lane >> 3) & 3) << 4) | (((lane >> 5) & 1) << 3) | (lane & 7)
    lanes = (iota((256, 256), 0) == source).astype(F4).astype(BF)
    row = iota((128, 96), 0)
    wanted = ((row >> 2) & 7) * 16 + (row & 3) * 4 + (row >> 5)
    rows = (iota((128, 96), 1) == wanted).astype(F4).astype(BF)
    moved = jnp.dot(stacked, lanes, preferred_element_type=F4).astype(BF)
    moved = jnp.dot(rows, moved, preferred_element_type=F4)
    part = iota((32, 128), 1) >> 5
    flag = (iota((32, 128), 0) >> 2) == 6
    groups = []
    for group in range(8):
        tile, place = group // 4, group % 4
        total = None
        for low in range(4):
            piece = moved[low * 32 : (low + 1) * 32, tile * 128 : (tile + 1) * 128]
            turn = (low - place) * 32 % 128
            if turn:
                piece = pltpu.roll(piece, turn, 1)
            total = piece if total is None else jnp.where(part == low, piece, total)
        groups.append(jnp.where(flag, 1.0, total))
    return jnp.concatenate(groups, axis=0).astype(BF)


def route_rows(targets):
    across = jnp.broadcast_to(targets, (32, 32)).astype(F4)
    first, second = iota((32, 32), 0), iota((32, 32), 1)
    down = jnp.sum(jnp.where(first == second, across, 0.0), axis=1, keepdims=True)
    earlier = (down == across) & (first < second)
    rank = jnp.sum(jnp.where(earlier, 1.0, 0.0), axis=0, keepdims=True)
    code = (2.0 * across[0:16] + rank).astype(BF)
    lane = iota((32, 256), 1)
    spread = (iota((32, 256), 0) == 8 * (lane & 3) + (lane >> 5)).astype(F4).astype(BF)
    code = jnp.dot(code, spread, preferred_element_type=F4)[0:1].astype(I4)
    key = code * 8 + ((iota((1, 256), 1) >> 2) & 7)
    return (iota((512, 256), 0) == key).astype(F4).astype(BF)


def own_half(col):
    return (iota((8, 128), 0) < 4) == (col == 0)


def pack_piece(tile, half):
    low = iota((8, 128), 1) < 64
    return [
        tile(0, 0),
        tile(0, 1),
        tile(1, 0),
        tile(1, 1),
        jnp.where(low, tile(0, 2), pltpu.roll(tile(1, 2), 64, 1)),
        jnp.where(half, tile(2, 0), pltpu.roll(tile(2, 1), 4, 0)),
        tile(2, 2),
    ]


def unpack_piece(tiles):
    return (
        (tiles[0], tiles[1], tiles[4]),
        (tiles[2], tiles[3], pltpu.roll(tiles[4], 64, 1)),
        (tiles[5], pltpu.roll(tiles[5], 4, 0), tiles[6]),
    )


def planes_kernel(pop_ref, last_ref, initial_ref, own_ref):
    own_ref[...] = pop_ref[...]
    for ref, indices, row in ((last_ref, FORWARD, 15), (initial_ref, BACKWARD, 0)):
        ref[...] = jnp.zeros_like(ref)
        for slot, index in enumerate(indices):
            ref[slot : slot + 1, :] = pop_ref[index, row : row + 1, :]


def planes(populations):
    return pl.pallas_call(
        planes_kernel,
        out_shape=(jax.ShapeDtypeStruct((8, 256), F4),) * 2
        + (jax.ShapeDtypeStruct((19, 16, 256), F4),),
        name="planes",
        compiler_params=pltpu.CompilerParams(vmem_limit_bytes=16 * MIB),
    )(populations)


def gathered_rows(gain, shift, lists, out_weight, master, lift_weight):
    def placed(array, start):
        rows, lanes = array.shape
        return jnp.pad(array, ((start, 120 - start - rows), (0, C - lanes))).astype(F4)

    row = iota((120, C), 0)
    total = placed(lists, 2) + placed(out_weight, 3) + placed(master, 8) + placed(lift_weight.T, 32)
    return jnp.where(row == 0, gain, jnp.where(row == 1, shift, total))


def prepare_kernel(
    col_ref,
    pop_ref,
    small_ref,
    old_ref,
    select_ref,
    weights_ref,
    lift_out,
    gain_out,
    shift_out,
    rows_out,
    window,
):
    unused, old_flow = moments([pop_ref[index] for index in range(19)])
    old_ref[...] = jnp.concatenate(old_flow, axis=0).astype(BF)
    select_ref[...] = route_rows(small_ref[2:3, 0:32])
    col = col_ref[0]
    window[...] = jnp.zeros_like(window)

    @pl.when(col == 0)
    def _():
        window[0:20, 0:C] = small_ref[8:28, :]

    @pl.when(col != 0)
    def _():
        window[4:24, 0:C] = small_ref[8:28, :]

    def tile(index, lanes):
        start = pl.multiple_of((index * 8 + 8 * col) % 24, 8)
        return window[pl.ds(start, 8), lanes * 128 : (lanes + 1) * 128]

    weights_ref[...] = jnp.concatenate(pack_piece(tile, own_half(col)), axis=0)
    column = iota((88, 224), 1)
    feature = (column & 7) * 27 + (column >> 3)
    valid = ((column & 7) < 3) & (column < 216)
    spread = jnp.where(valid & (iota((88, 224), 0) == feature), 1.0, 0.0).astype(BF)
    lift_out[...] = lax.dot_general(
        small_ref[32:120, :].astype(BF),
        spread,
        (((0,), (0,)), ((), ())),
        preferred_element_type=F4,
    ).astype(BF)
    same = iota((C, C), 0) == iota((C, C), 1)
    for index, target in ((0, gain_out), (1, shift_out)):
        across = small_ref[index : index + 1, :]
        down = jnp.sum(jnp.where(same, across, 0.0), axis=1, keepdims=True)
        target[...] = jnp.broadcast_to(down, (C, 128))
    row = iota((8, C), 0)
    rows = jnp.where((row >= 3) & (row < 6), small_ref[0:8, :], 0.0)
    rows_out[...] = jnp.concatenate([rows, jnp.zeros_like(rows)], axis=0).astype(BF)


def prepare(col, populations, small):
    vector = pl.BlockSpec(memory_space=pltpu.VMEM)
    return pl.pallas_call(
        prepare_kernel,
        in_specs=[pl.BlockSpec(memory_space=pltpu.SMEM)] + [vector] * 2,
        out_specs=(vector,) * 7,
        out_shape=(
            jax.ShapeDtypeStruct((48, 256), BF),
            jax.ShapeDtypeStruct((512, 256), BF),
            jax.ShapeDtypeStruct((WEIGHT_ROWS, 128), F4),
            jax.ShapeDtypeStruct((C, 224), BF),
            jax.ShapeDtypeStruct((C, 128), F4),
            jax.ShapeDtypeStruct((C, 128), F4),
            jax.ShapeDtypeStruct((16, C), BF),
        ),
        scratch_shapes=[pltpu.VMEM((24, WIDE), F4)],
        name="prepare",
        cost_estimate=pl.CostEstimate(flops=10**7, bytes_accessed=4 * 10**6, transcendentals=0),
        compiler_params=pltpu.CompilerParams(vmem_limit_bytes=16 * MIB),
    )(col, populations, small)


def streamed(pop_ref, before_ref, behind_ref):
    row = iota((16, 256), 0)
    depth = iota((16, 256), 1) & 15
    read = []
    for index in range(19):
        along_x, along_y, along_z = VELOCITIES[index]
        plane = pop_ref[index]
        if along_x > 0:
            at = FORWARD.index(index)
            plane = jnp.where(row == 0, before_ref[at : at + 1], pltpu.roll(plane, 1, 0))
        elif along_x < 0:
            at = BACKWARD.index(index)
            plane = jnp.where(row == 15, behind_ref[at : at + 1], pltpu.roll(plane, 15, 0))
        if along_y:
            plane = pltpu.roll(plane, along_y * 16 % 256, 1)
        if along_z > 0:
            plane = jnp.where(depth == 0, pltpu.roll(plane, 241, 1), pltpu.roll(plane, 1, 1))
        elif along_z < 0:
            plane = jnp.where(depth == 15, pltpu.roll(plane, 15, 1), pltpu.roll(plane, 255, 1))
        read.append(plane)
    return read


def route_kernel(
    pop_ref, before_ref, behind_ref, old_ref, select_ref, weights_ref, out_ref, routed
):
    density, flow = moments(streamed(pop_ref, before_ref, behind_ref))
    fields = jnp.concatenate([old_ref[...]] + [part.astype(BF) for part in flow], axis=0)
    bricks = brick_rows(fields)
    routed[...] = jnp.dot(select_ref[...], bricks, preferred_element_type=F4)
    weights = weights_ref[...]
    for pair in range(16):
        start = pair * 2 * BLOCK_ROWS
        first = routed[pair * 32 : pair * 32 + 16]
        second = routed[pair * 32 + 16 : pair * 32 + 32]
        out_ref[start : start + 2 * BLOCK_ROWS] = jnp.concatenate(
            [first, weights, second, weights], axis=0
        ).astype(BF)


def route(populations, before, behind, old, select, weights):
    return pl.pallas_call(
        route_kernel,
        out_shape=jax.ShapeDtypeStruct((32 * BLOCK_ROWS, 128), BF),
        scratch_shapes=[pltpu.VMEM((512, 128), F4)],
        name="route",
        compiler_params=pltpu.CompilerParams(vmem_limit_bytes=16 * MIB),
    )(populations, before, behind, old, select, weights)


def collide_kernel(
    pop_ref,
    before_ref,
    behind_ref,
    relax_ref,
    master_ref,
    first_ref,
    second_ref,
    after_ref,
    state_ref,
):
    state_ref[0], state_ref[1], state_ref[2] = master_ref[...], first_ref[...], second_ref[...]
    read = streamed(pop_ref, before_ref, behind_ref)
    density, flow = moments(read)
    speed = flow[0] * flow[0] + flow[1] * flow[1] + flow[2] * flow[2]
    relaxation = relax_ref[...]
    for index in range(19):
        project = None
        for axis in range(3):
            along = VELOCITIES[index][axis]
            if along:
                term = flow[axis] if along > 0 else -flow[axis]
                project = term if project is None else project + term
        if project is None:
            shape = 1.0 - 1.5 * speed
        else:
            shape = 1.0 + 3.0 * project + 4.5 * project * project - 1.5 * speed
        balance = LATTICE_WEIGHTS[index] * density * shape
        after_ref[index] = read[index] - relaxation * (read[index] - balance)


def collide(populations, before, behind, relaxation, *state):
    return pl.pallas_call(
        collide_kernel,
        out_shape=(
            jax.ShapeDtypeStruct((19, 16, 256), F4),
            jax.ShapeDtypeStruct((3, 20, C), F4),
        ),
        name="collide",
        cost_estimate=pl.CostEstimate(flops=10**7, bytes_accessed=4 * 10**6, transcendentals=0),
        compiler_params=pltpu.CompilerParams(vmem_limit_bytes=16 * MIB),
    )(populations, before, behind, relaxation, *state)


def lift_kernel(
    arrived_ref,
    weight_ref,
    gain_ref,
    shift_ref,
    h_ref,
    target_ref,
    taps,
    lifted,
    sums,
    squares,
    means,
    scales,
):
    parts = []
    for pair in range(16):
        start = pair * 2 * BLOCK_ROWS
        block = arrived_ref[start : start + 2 * BLOCK_ROWS].astype(F4)
        parts += [block[0:16], block[BLOCK_ROWS : BLOCK_ROWS + 16]]
    arrived = jnp.concatenate(parts, axis=0).astype(BF)
    flags = (iota((32, 512), 1) == iota((32, 512), 0) * 16 + 6).astype(F4).astype(BF)
    flags = jnp.dot(flags, arrived, preferred_element_type=F4).astype(BF)
    source = iota((32, 512), 1) >> 4
    ahead = (iota((32, 512), 0) < source).astype(F4).astype(BF)
    same = (iota((32, 512), 0) == source).astype(F4).astype(BF)
    dims = (((0,), (0,)), ((), ()))
    place = lax.dot_general(flags, ahead, dims, preferred_element_type=F4)[0:1].astype(I4)
    live = lax.dot_general(flags, same, dims, preferred_element_type=F4)[0:1]
    lane = iota((1, 512), 1)
    key = jnp.where(live > 0.5, place * 16 + (lane & 15), -1)
    pick = (iota((256, 512), 0) == key).astype(F4).astype(BF)
    held = jnp.dot(pick, arrived, preferred_element_type=F4)
    for brick in range(32):
        target_ref[0:8, brick * 128 : (brick + 1) * 128] = held[brick * 8 : (brick + 1) * 8]
    target_ref[8:16, :] = jnp.zeros((8, CELLS), F4)
    cell = iota((8, 128), 1)
    cell_x, cell_y, cell_z = cell >> 5, (cell >> 3) & 3, cell & 7
    shifts = [(x, y, z) for x in (-1, 0, 1) for y in (-1, 0, 1) for z in (-1, 0, 1)]
    masks = []
    for x, y, z in shifts:
        inside = (cell_x + x >= 0) & (cell_x + x < 4) & (cell_y + y >= 0) & (cell_y + y < 4)
        masks.append(inside & (cell_z + z >= 0) & (cell_z + z < 8))
    weight = weight_ref[...]
    for start in range(0, CELLS, SPAN):
        part = slice(start, start + SPAN)
        for brick in range(start // 128, (start + SPAN) // 128):
            own = held[brick * 8 : (brick + 1) * 8]
            for pair in range(14):
                halves = []
                for tap in (2 * pair, 2 * pair + 1):
                    if tap == 27:
                        halves.append(jnp.zeros((8, 128), F4))
                        continue
                    x, y, z = shifts[tap]
                    turn = -(x * 32 + y * 8 + z) % 128
                    moved = pltpu.roll(own, turn, 1) if turn else own
                    halves.append(jnp.where(masks[tap], moved, 0.0))
                taps[pair * 16 : (pair + 1) * 16, brick * 128 : (brick + 1) * 128] = (
                    jnp.concatenate(halves, axis=0).astype(BF)
                )
        lifted[:, part] = jnp.dot(weight, taps[:, part], preferred_element_type=F4)
        for row in range(0, C, 16):
            rows = slice(row, row + 16)
            total = None
            for at in range(start, start + SPAN, 128):
                value = lifted[rows, at : at + 128]
                total = value if total is None else total + value
                square = value * value if at == start else square + value * value
            sums[rows, :] = total if start == 0 else sums[rows, :] + total
            squares[rows, :] = square if start == 0 else squares[rows, :] + square
    mean = jnp.sum(sums[...], axis=1, keepdims=True) / CELLS
    spread = jnp.sum(squares[...], axis=1, keepdims=True) / CELLS - mean * mean
    means[...] = jnp.broadcast_to(mean, (C, 128))
    scales[...] = lax.rsqrt(spread + 1e-05) * gain_ref[...]

    @pl.loop(0, CELLS // SPAN)
    def _(index):
        for row in range(0, C, 16):
            rows = slice(row, row + 16)
            mean, scale, shift = means[rows, :], scales[rows, :], shift_ref[rows, :]
            for at in range(0, SPAN, 128):
                part = pl.ds(pl.multiple_of(index * SPAN + at, 128), 128)
                normed = (lifted[rows, part] - mean) * scale + shift
                h_ref[rows, part] = gelu_value(normed).astype(BF)


def lift(arrived, weight, gain, shift):
    return pl.pallas_call(
        lift_kernel,
        out_shape=(
            jax.ShapeDtypeStruct((C, CELLS), BF),
            jax.ShapeDtypeStruct((16, CELLS), F4),
        ),
        scratch_shapes=[pltpu.VMEM((224, CELLS), BF), pltpu.VMEM((C, CELLS), F4)]
        + [pltpu.VMEM((C, 128), F4)] * 4,
        name="lift",
        compiler_params=pltpu.CompilerParams(vmem_limit_bytes=40 * MIB),
    )(arrived, weight, gain, shift)


def train_kernel(
    steps,
    layers,
    col_ref,
    h_ref,
    target_ref,
    mine_ref,
    other_ref,
    out_ref,
    send_ref,
    keep_ref,
    mix_ref,
    mix_back,
    states,
    slopes,
    ahead,
    back,
    inner,
    total,
):
    step = pl.program_id(0)
    cells = h_ref.shape[1]
    parts = [slice(start, start + 256) for start in range(0, cells, 256)]

    @pl.when(step == 0)
    def _():
        total[...] = jnp.zeros_like(total)
        even = col_ref[0] == 0
        upper = iota((8, 128), 0) < 4
        for pair in range(16):
            rows = slice(pair * 2 * BLOCK_ROWS, (pair + 1) * 2 * BLOCK_ROWS)
            mine = mine_ref[rows, :].astype(F4)
            other = other_ref[rows, :].astype(F4)
            tiles = []
            for start in (16, BLOCK_ROWS + 16):
                sides = ([], [])
                for index in range(7):
                    at = slice(start + index * 8, start + index * 8 + 8)
                    sides[0].append(jnp.where(even, mine[at], other[at]))
                    sides[1].append(jnp.where(even, other[at], mine[at]))
                left, right = unpack_piece(sides[0]), unpack_piece(sides[1])
                middle = [jnp.where(upper, a, b) for a, b in zip(left[2], right[2])]
                tiles += [left[0], left[1], middle, right[0], right[1]]
            for lanes in range(3):
                width = min(C - lanes * 128, 128)
                column = jnp.concatenate([tile[lanes] for tile in tiles], axis=0).astype(BF)
                mix_ref[pair * 80 : (pair + 1) * 80, lanes * 128 : lanes * 128 + width] = column[
                    :, 0:width
                ]
        same = (iota((C, C), 0) == iota((C, C), 1)).astype(F4).astype(BF)
        for layer in range(1, layers):
            rows = slice(layer * C, (layer + 1) * C)
            mix_back[rows, :] = lax.dot_general(
                mix_ref[rows, :], same, (((0,), (0,)), ((), ())), preferred_element_type=F4
            ).astype(BF)

    def state(layer):
        return h_ref if layer == 0 else states.at[layer - 1]

    for layer in range(layers):
        for part in parts:
            ahead[:, part] = jnp.dot(
                mix_ref[layer * C : (layer + 1) * C, :],
                state(layer)[:, part],
                preferred_element_type=F4,
            )
        for part in parts:
            for start in range(0, C, 16):
                rows = slice(start, start + 16)
                value, slope = gelu_both(ahead[rows, part])
                slopes[layer, rows, part] = slope
                states[layer, rows, part] = (state(layer)[rows, part].astype(F4) + value).astype(BF)
    def descend(layer, part, change, first):
        for start in range(0, C, 16):
            rows = slice(start, start + 16)
            value = change[start : start + 16]
            if not first:
                value = back[rows, part] + value
            if layer > 0:
                back[rows, part] = value
            inner[layer, rows, part] = (value * slopes[layer, rows, part]).astype(BF)

    for part in parts:
        output = jnp.dot(out_ref[...], states[layers - 1, :, part], preferred_element_type=F4)
        delta = ((output - target_ref[:, part]) * (2.0 / 384.0)).astype(BF)
        change = lax.dot_general(
            out_ref[...], delta, (((0,), (0,)), ((), ())), preferred_element_type=F4
        )
        descend(layers - 1, part, change, True)
    for layer in range(layers - 1, -1, -1):
        rows_of = slice(layer * C, (layer + 1) * C)
        total[rows_of, 0:C] += lax.dot_general(
            inner[layer], state(layer)[...], (((1,), (1,)), ((), ())), preferred_element_type=F4
        )
        if layer > 0:
            for part in parts:
                change = jnp.dot(
                    mix_back[rows_of, :], inner[layer, :, part], preferred_element_type=F4
                )
                descend(layer - 1, part, change, False)

    @pl.when(step == steps - 1)
    def _():
        col = col_ref[0]
        for piece in range(32):
            for ref, side in ((keep_ref, col), (send_ref, 1 - col)):

                def tile(index, lanes):
                    start = piece * 40 + 16
                    if index < 2:
                        start = pl.multiple_of(piece * 40 + 24 * side + 8 * index, 8)
                    return total[pl.ds(start, 8), lanes * 128 : (lanes + 1) * 128]

                packed = pack_piece(tile, own_half(side))
                for index in range(7):
                    start = piece * WEIGHT_ROWS + index * 8
                    ref[start : start + 8, :] = packed[index]


def train(col, h, target, mine, other, out_weight):
    cells = 1024
    steps = CELLS // cells
    layers = 4
    block = pl.BlockSpec((32 * BLOCK_ROWS, 128), lambda i: (0, 0))
    return pl.pallas_call(
        functools.partial(train_kernel, steps, layers),
        grid=(steps,),
        in_specs=[
            pl.BlockSpec(memory_space=pltpu.SMEM),
            pl.BlockSpec((C, cells), lambda i: (0, i)),
            pl.BlockSpec((16, cells), lambda i: (0, i)),
            block,
            block,
            pl.BlockSpec((16, C), lambda i: (0, 0)),
        ],
        out_specs=(
            pl.BlockSpec((32 * WEIGHT_ROWS, 128), lambda i: (0, 0)),
            pl.BlockSpec((32 * WEIGHT_ROWS, 128), lambda i: (0, 0)),
        ),
        out_shape=(
            jax.ShapeDtypeStruct((32 * WEIGHT_ROWS, 128), F4),
            jax.ShapeDtypeStruct((32 * WEIGHT_ROWS, 128), F4),
        ),
        scratch_shapes=[
            pltpu.VMEM((layers * C, C), BF),
            pltpu.VMEM((layers * C, C), BF),
            pltpu.VMEM((layers, C, cells), BF),
            pltpu.VMEM((layers, C, cells), F4),
            pltpu.VMEM((C, cells), F4),
            pltpu.VMEM((C, cells), F4),
            pltpu.VMEM((layers, C, cells), BF),
            pltpu.VMEM((layers * C, WIDE), F4),
        ],
        name="train",
        compiler_params=pltpu.CompilerParams(vmem_limit_bytes=48 * MIB),
    )(col, h, target, mine, other, out_weight)


def scale_kernel(keep_ref, other_ref, out_ref):
    peak = jnp.zeros((8, 128), F4)
    for start in range(0, 32 * WEIGHT_ROWS, 8):
        value = keep_ref[start : start + 8, :] + other_ref[start : start + 8, :]
        out_ref[start : start + 8, :] = value
        peak = jnp.maximum(peak, jnp.abs(value))
    peak = jnp.max(jnp.max(peak, axis=1, keepdims=True), axis=0, keepdims=True)
    power = jnp.ceil(jnp.log2(jnp.maximum(peak, 1e-30)))
    scale = jnp.broadcast_to(jnp.exp2(TOP_POWER - power), (8, 128))
    power = jnp.broadcast_to(power, (8, 128))
    free = iota((8, 128), 1) == 127
    for start in range(0, 32 * WEIGHT_ROWS, 8):
        value = out_ref[start : start + 8, :] * scale
        if start % WEIGHT_ROWS == 48:
            value = jnp.where(free, power, value)
        out_ref[start : start + 8, :] = value


def scaled(keep, other):
    return pl.pallas_call(
        scale_kernel,
        out_shape=jax.ShapeDtypeStruct((32 * WEIGHT_ROWS, 128), F4),
        name="scaled",
        compiler_params=pltpu.CompilerParams(vmem_limit_bytes=16 * MIB),
    )(keep, other)


def update_kernel(col_ref, own_ref, other_ref, state_ref, new_ref, first_out, second_out):
    packed = own_ref[...] + other_ref[...]
    parts = unpack_piece([packed[index * 8 : index * 8 + 8] for index in range(7)])
    full, rest, half = [jnp.concatenate(part, axis=1) for part in parts]
    even = col_ref[0] == 0
    lower = jnp.concatenate([full, rest, half], axis=0)
    upper = pltpu.roll(jnp.concatenate([half, full, rest], axis=0), 20, 0)
    gradient = jnp.where(even, lower, upper)[0:20, 0:C]
    master = state_ref[0]
    first_next = 0.9 * state_ref[1] + 0.1 * gradient
    second_next = 0.999 * state_ref[2] + 0.001 * gradient * gradient
    ratio = first_next / (1.0 - 0.9**10) / (jnp.sqrt(second_next / (1.0 - 0.999**10)) + 1e-08)
    new_ref[...] = master - 0.01 * (ratio + 0.1 * master)
    first_out[...] = first_next
    second_out[...] = second_next


def update(col, own, other, state):
    vector = pl.BlockSpec(memory_space=pltpu.VMEM)
    return pl.pallas_call(
        update_kernel,
        in_specs=[pl.BlockSpec(memory_space=pltpu.SMEM)] + [vector] * 3,
        out_specs=(vector,) * 3,
        out_shape=(jax.ShapeDtypeStruct((20, C), F4),) * 3,
        name="update",
        compiler_params=pltpu.CompilerParams(vmem_limit_bytes=16 * MIB),
    )(col, own, other, state)


def body(
    populations,
    relaxation,
    send_lists,
    lift_weight,
    norm_gain,
    norm_shift,
    mix_master,
    mix_first,
    mix_second,
    out_weight,
):
    every = ("sec", "row", "col")
    size = lax.axis_size(every)
    swap = [(0, 1), (1, 0)]
    col = lax.axis_index("col").astype(I4)[None]
    up = [(i, (i + 1) % size) for i in range(size)]
    last, initial, populations = planes(populations)
    behind = lax.ppermute(initial, every, [(j, i) for i, j in up])
    before = lax.ppermute(last, every, up)
    small = gathered_rows(norm_gain, norm_shift, send_lists, out_weight, mix_master, lift_weight)
    old, select, weights, lift_rows, gain, shift, out_rows = prepare(col, populations, small)
    outgoing = route(populations, before, behind, old, select, weights)
    arrived = lax.all_to_all(
        outgoing.reshape(32, BLOCK_ROWS, 128), "row", split_axis=0, concat_axis=0, tiled=True
    ).reshape(32 * BLOCK_ROWS, 128)
    after, state = collide(
        populations, before, behind, relaxation, mix_master, mix_first, mix_second
    )
    other = lax.ppermute(arrived, "col", swap)
    h, target = lift(arrived, lift_rows, gain, shift)
    send, keep = train(col, h, target, arrived, other, out_rows)
    half = scaled(keep, lax.ppermute(send, "col", swap)).reshape(32, WEIGHT_ROWS, 128)
    terms = lax.all_to_all(
        half.astype(jnp.float16), "row", split_axis=0, concat_axis=0, tiled=True
    ).astype(F4)
    summed = jnp.sum(terms * jnp.exp2(terms[:, 48:49, 127:128] - TOP_POWER), axis=0)
    across = lax.ppermute(summed, "sec", swap)
    new_master, new_first, new_second = update(col, summed, across, state)
    return (after, new_master, new_first, new_second)


def solution(mesh):
    in_specs = (
        P(None, ("sec", "row", "col"), None),
        P(("sec", "row", "col"), None),
        P(("sec", "row", "col"), None),
        P(),
        P(),
        P(),
        P(("row", "col"), None),
        P(("row", "col"), None),
        P(("row", "col"), None),
        P(),
    )
    out_specs = (
        P(None, ("sec", "row", "col"), None),
        P(("row", "col"), None),
        P(("row", "col"), None),
        P(("row", "col"), None),
    )
    return jax.shard_map(body, mesh=mesh, in_specs=in_specs, out_specs=out_specs, check_vma=False)
```

```python
import functools

import jax
import jax.numpy as jnp
from jax import lax
from jax.experimental import pallas as pl
from jax.experimental.pallas import tpu as pltpu
from jax.sharding import PartitionSpec as P

BF = jnp.bfloat16
F4 = jnp.float32
I4 = jnp.int32
C = 320
CELLS = 4096
WEIGHT_ROWS = 56
BLOCK_ROWS = 16 + WEIGHT_ROWS
WIDE = 384
SPAN = 1024
TOP_POWER = 14.0
MIB = 1024 * 1024

VELOCITIES = (
    (0, 0, 0),
    (1, 0, 0),
    (-1, 0, 0),
    (0, 1, 0),
    (0, -1, 0),
    (0, 0, 1),
    (0, 0, -1),
    (1, 1, 0),
    (-1, -1, 0),
    (1, -1, 0),
    (-1, 1, 0),
    (1, 0, 1),
    (-1, 0, -1),
    (1, 0, -1),
    (-1, 0, 1),
    (0, 1, 1),
    (0, -1, -1),
    (0, 1, -1),
    (0, -1, 1),
)
FORWARD = [index for index in range(19) if VELOCITIES[index][0] > 0]
BACKWARD = [index for index in range(19) if VELOCITIES[index][0] < 0]
LATTICE_WEIGHTS = (1.0 / 3.0,) + (1.0 / 18.0,) * 6 + (1.0 / 36.0,) * 12

ROOT_HALF = 0.7071067811865476
EXP_SCALE = -0.5 * 1.4426950408889634


def iota(shape, dim):
    return lax.broadcasted_iota(I4, shape, dim)


def gelu_value(z):
    return z * (0.5 + 0.5 * lax.erf(z * ROOT_HALF))


def gelu_both(z):
    share = 0.5 + 0.5 * lax.erf(z * ROOT_HALF)
    bell = jnp.exp2(z * z * EXP_SCALE)
    return z * share, share + (z * 0.3989422804014327) * bell


def moments(read):
    density = read[0]
    moment = [None, None, None]
    for index in range(1, 19):
        density = density + read[index]
        for axis in range(3):
            along = VELOCITIES[index][axis]
            if along:
                term = read[index] if along > 0 else -read[index]
                moment[axis] = term if moment[axis] is None else moment[axis] + term
    return density, [moment[axis] / density for axis in range(3)]


def brick_rows(stacked):
    lane = iota((256, 256), 1)
    source = (lane & 0xC0) | (((lane >> 3) & 3) << 4) | (((lane >> 5) & 1) << 3) | (lane & 7)
    lanes = (iota((256, 256), 0) == source).astype(F4).astype(BF)
    row = iota((128, 96), 0)
    wanted = ((row >> 2) & 7) * 16 + (row & 3) * 4 + (row >> 5)
    rows = (iota((128, 96), 1) == wanted).astype(F4).astype(BF)
    moved = jnp.dot(stacked, lanes, preferred_element_type=F4).astype(BF)
    moved = jnp.dot(rows, moved, preferred_element_type=F4)
    part = iota((32, 128), 1) >> 5
    flag = (iota((32, 128), 0) >> 2) == 6
    groups = []
    for group in range(8):
        tile, place = group // 4, group % 4
        total = None
        for low in range(4):
            piece = moved[low * 32 : (low + 1) * 32, tile * 128 : (tile + 1) * 128]
            turn = (low - place) * 32 % 128
            if turn:
                piece = pltpu.roll(piece, turn, 1)
            total = piece if total is None else jnp.where(part == low, piece, total)
        groups.append(jnp.where(flag, 1.0, total))
    return jnp.concatenate(groups, axis=0).astype(BF)


def route_rows(targets):
    across = jnp.broadcast_to(targets, (32, 32)).astype(F4)
    first, second = iota((32, 32), 0), iota((32, 32), 1)
    down = jnp.sum(jnp.where(first == second, across, 0.0), axis=1, keepdims=True)
    earlier = (down == across) & (first < second)
    rank = jnp.sum(jnp.where(earlier, 1.0, 0.0), axis=0, keepdims=True)
    code = (2.0 * across[0:16] + rank).astype(BF)
    lane = iota((32, 256), 1)
    spread = (iota((32, 256), 0) == 8 * (lane & 3) + (lane >> 5)).astype(F4).astype(BF)
    code = jnp.dot(code, spread, preferred_element_type=F4)[0:1].astype(I4)
    key = code * 8 + ((iota((1, 256), 1) >> 2) & 7)
    return (iota((512, 256), 0) == key).astype(F4).astype(BF)


def own_half(col):
    return (iota((8, 128), 0) < 4) == (col == 0)


def pack_piece(tile, half):
    low = iota((8, 128), 1) < 64
    return [
        tile(0, 0),
        tile(0, 1),
        tile(1, 0),
        tile(1, 1),
        jnp.where(low, tile(0, 2), pltpu.roll(tile(1, 2), 64, 1)),
        jnp.where(half, tile(2, 0), pltpu.roll(tile(2, 1), 4, 0)),
        tile(2, 2),
    ]


def unpack_piece(tiles):
    return (
        (tiles[0], tiles[1], tiles[4]),
        (tiles[2], tiles[3], pltpu.roll(tiles[4], 64, 1)),
        (tiles[5], pltpu.roll(tiles[5], 4, 0), tiles[6]),
    )


def planes_kernel(pop_ref, last_ref, initial_ref, own_ref):
    own_ref[...] = pop_ref[...]
    for ref, indices, row in ((last_ref, FORWARD, 15), (initial_ref, BACKWARD, 0)):
        ref[...] = jnp.zeros_like(ref)
        for slot, index in enumerate(indices):
            ref[slot : slot + 1, :] = pop_ref[index, row : row + 1, :]


def planes(populations):
    return pl.pallas_call(
        planes_kernel,
        out_shape=(jax.ShapeDtypeStruct((8, 256), F4),) * 2
        + (jax.ShapeDtypeStruct((19, 16, 256), F4),),
        name="planes",
        compiler_params=pltpu.CompilerParams(vmem_limit_bytes=16 * MIB),
    )(populations)


def gathered_rows(gain, shift, lists, out_weight, master, lift_weight):
    def placed(array, start):
        rows, lanes = array.shape
        return jnp.pad(array, ((start, 120 - start - rows), (0, C - lanes))).astype(F4)

    row = iota((120, C), 0)
    total = placed(lists, 2) + placed(out_weight, 3) + placed(master, 8) + placed(lift_weight.T, 32)
    return jnp.where(row == 0, gain, jnp.where(row == 1, shift, total))


def prepare_kernel(
    col_ref,
    pop_ref,
    small_ref,
    old_ref,
    select_ref,
    weights_ref,
    lift_out,
    gain_out,
    shift_out,
    rows_out,
    window,
):
    unused, old_flow = moments([pop_ref[index] for index in range(19)])
    old_ref[...] = jnp.concatenate(old_flow, axis=0).astype(BF)
    select_ref[...] = route_rows(small_ref[2:3, 0:32])
    col = col_ref[0]
    window[...] = jnp.zeros_like(window)

    @pl.when(col == 0)
    def _():
        window[0:20, 0:C] = small_ref[8:28, :]

    @pl.when(col != 0)
    def _():
        window[4:24, 0:C] = small_ref[8:28, :]

    def tile(index, lanes):
        start = pl.multiple_of((index * 8 + 8 * col) % 24, 8)
        return window[pl.ds(start, 8), lanes * 128 : (lanes + 1) * 128]

    weights_ref[...] = jnp.concatenate(pack_piece(tile, own_half(col)), axis=0)
    column = iota((88, 224), 1)
    feature = (column & 7) * 27 + (column >> 3)
    valid = ((column & 7) < 3) & (column < 216)
    spread = jnp.where(valid & (iota((88, 224), 0) == feature), 1.0, 0.0).astype(BF)
    lift_out[...] = lax.dot_general(
        small_ref[32:120, :].astype(BF),
        spread,
        (((0,), (0,)), ((), ())),
        preferred_element_type=F4,
    ).astype(BF)
    same = iota((C, C), 0) == iota((C, C), 1)
    for index, target in ((0, gain_out), (1, shift_out)):
        across = small_ref[index : index + 1, :]
        down = jnp.sum(jnp.where(same, across, 0.0), axis=1, keepdims=True)
        target[...] = jnp.broadcast_to(down, (C, 128))
    row = iota((8, C), 0)
    rows = jnp.where((row >= 3) & (row < 6), small_ref[0:8, :], 0.0)
    rows_out[...] = jnp.concatenate([rows, jnp.zeros_like(rows)], axis=0).astype(BF)


def prepare(col, populations, small):
    vector = pl.BlockSpec(memory_space=pltpu.VMEM)
    return pl.pallas_call(
        prepare_kernel,
        in_specs=[pl.BlockSpec(memory_space=pltpu.SMEM)] + [vector] * 2,
        out_specs=(vector,) * 7,
        out_shape=(
            jax.ShapeDtypeStruct((48, 256), BF),
            jax.ShapeDtypeStruct((512, 256), BF),
            jax.ShapeDtypeStruct((WEIGHT_ROWS, 128), F4),
            jax.ShapeDtypeStruct((C, 224), BF),
            jax.ShapeDtypeStruct((C, 128), F4),
            jax.ShapeDtypeStruct((C, 128), F4),
            jax.ShapeDtypeStruct((16, C), BF),
        ),
        scratch_shapes=[pltpu.VMEM((24, WIDE), F4)],
        name="prepare",
        cost_estimate=pl.CostEstimate(flops=10**7, bytes_accessed=4 * 10**6, transcendentals=0),
        compiler_params=pltpu.CompilerParams(vmem_limit_bytes=16 * MIB),
    )(col, populations, small)


def streamed(pop_ref, before_ref, behind_ref):
    row = iota((16, 256), 0)
    depth = iota((16, 256), 1) & 15
    read = []
    for index in range(19):
        along_x, along_y, along_z = VELOCITIES[index]
        plane = pop_ref[index]
        if along_x > 0:
            at = FORWARD.index(index)
            plane = jnp.where(row == 0, before_ref[at : at + 1], pltpu.roll(plane, 1, 0))
        elif along_x < 0:
            at = BACKWARD.index(index)
            plane = jnp.where(row == 15, behind_ref[at : at + 1], pltpu.roll(plane, 15, 0))
        if along_y:
            plane = pltpu.roll(plane, along_y * 16 % 256, 1)
        if along_z > 0:
            plane = jnp.where(depth == 0, pltpu.roll(plane, 241, 1), pltpu.roll(plane, 1, 1))
        elif along_z < 0:
            plane = jnp.where(depth == 15, pltpu.roll(plane, 15, 1), pltpu.roll(plane, 255, 1))
        read.append(plane)
    return read


def route_kernel(
    pop_ref, behind_ref, before_ref, old_ref, select_ref, weights_ref, out_ref, routed
):
    density, flow = moments(streamed(pop_ref, before_ref, behind_ref))
    fields = jnp.concatenate([old_ref[...]] + [part.astype(BF) for part in flow], axis=0)
    bricks = brick_rows(fields)
    routed[...] = jnp.dot(select_ref[...], bricks, preferred_element_type=F4)
    weights = weights_ref[...]
    for pair in range(16):
        start = pair * 2 * BLOCK_ROWS
        first = routed[pair * 32 : pair * 32 + 16]
        second = routed[pair * 32 + 16 : pair * 32 + 32]
        out_ref[start : start + 2 * BLOCK_ROWS] = jnp.concatenate(
            [first, weights, second, weights], axis=0
        ).astype(BF)


def route(populations, before, behind, old, select, weights):
    return pl.pallas_call(
        route_kernel,
        out_shape=jax.ShapeDtypeStruct((32 * BLOCK_ROWS, 128), BF),
        scratch_shapes=[pltpu.VMEM((512, 128), F4)],
        name="route",
        compiler_params=pltpu.CompilerParams(vmem_limit_bytes=16 * MIB),
    )(populations, behind, before, old, select, weights)


def collide_kernel(
    pop_ref,
    behind_ref,
    before_ref,
    relax_ref,
    master_ref,
    first_ref,
    second_ref,
    after_ref,
    state_ref,
):
    state_ref[0], state_ref[1], state_ref[2] = master_ref[...], first_ref[...], second_ref[...]
    read = streamed(pop_ref, before_ref, behind_ref)
    density, flow = moments(read)
    speed = flow[0] * flow[0] + flow[1] * flow[1] + flow[2] * flow[2]
    relaxation = relax_ref[...]
    for index in range(19):
        project = None
        for axis in range(3):
            along = VELOCITIES[index][axis]
            if along:
                term = flow[axis] if along > 0 else -flow[axis]
                project = term if project is None else project + term
        if project is None:
            shape = 1.0 - 1.5 * speed
        else:
            shape = 1.0 + 3.0 * project + 4.5 * project * project - 1.5 * speed
        balance = LATTICE_WEIGHTS[index] * density * shape
        after_ref[index] = read[index] - relaxation * (read[index] - balance)


def collide(populations, before, behind, relaxation, *state):
    return pl.pallas_call(
        collide_kernel,
        out_shape=(
            jax.ShapeDtypeStruct((19, 16, 256), F4),
            jax.ShapeDtypeStruct((3, 20, C), F4),
        ),
        name="collide",
        cost_estimate=pl.CostEstimate(flops=10**7, bytes_accessed=4 * 10**6, transcendentals=0),
        compiler_params=pltpu.CompilerParams(vmem_limit_bytes=16 * MIB),
    )(populations, behind, before, relaxation, *state)


def lift_kernel(
    arrived_ref,
    weight_ref,
    gain_ref,
    shift_ref,
    h_ref,
    target_ref,
    taps,
    lifted,
    sums,
    squares,
    means,
    scales,
):
    parts = []
    for pair in range(16):
        start = pair * 2 * BLOCK_ROWS
        block = arrived_ref[start : start + 2 * BLOCK_ROWS].astype(F4)
        parts += [block[0:16], block[BLOCK_ROWS : BLOCK_ROWS + 16]]
    arrived = jnp.concatenate(parts, axis=0).astype(BF)
    flags = (iota((32, 512), 1) == iota((32, 512), 0) * 16 + 6).astype(F4).astype(BF)
    flags = jnp.dot(flags, arrived, preferred_element_type=F4).astype(BF)
    source = iota((32, 512), 1) >> 4
    ahead = (iota((32, 512), 0) < source).astype(F4).astype(BF)
    same = (iota((32, 512), 0) == source).astype(F4).astype(BF)
    dims = (((0,), (0,)), ((), ()))
    place = lax.dot_general(flags, ahead, dims, preferred_element_type=F4)[0:1].astype(I4)
    live = lax.dot_general(flags, same, dims, preferred_element_type=F4)[0:1]
    lane = iota((1, 512), 1)
    key = jnp.where(live > 0.5, place * 16 + (lane & 15), -1)
    pick = (iota((256, 512), 0) == key).astype(F4).astype(BF)
    held = jnp.dot(pick, arrived, preferred_element_type=F4)
    for brick in range(32):
        target_ref[0:8, brick * 128 : (brick + 1) * 128] = held[brick * 8 : (brick + 1) * 8]
    target_ref[8:16, :] = jnp.zeros((8, CELLS), F4)
    cell = iota((8, 128), 1)
    cell_x, cell_y, cell_z = cell >> 5, (cell >> 3) & 3, cell & 7
    shifts = [(x, y, z) for x in (-1, 0, 1) for y in (-1, 0, 1) for z in (-1, 0, 1)]
    masks = []
    for x, y, z in shifts:
        inside = (cell_x + x >= 0) & (cell_x + x < 4) & (cell_y + y >= 0) & (cell_y + y < 4)
        masks.append(inside & (cell_z + z >= 0) & (cell_z + z < 8))
    weight = weight_ref[...]
    for start in range(0, CELLS, SPAN):
        part = slice(start, start + SPAN)
        for brick in range(start // 128, (start + SPAN) // 128):
            own = held[brick * 8 : (brick + 1) * 8]
            for pair in range(14):
                halves = []
                for tap in (2 * pair, 2 * pair + 1):
                    if tap == 27:
                        halves.append(jnp.zeros((8, 128), F4))
                        continue
                    x, y, z = shifts[tap]
                    turn = -(x * 32 + y * 8 + z) % 128
                    moved = pltpu.roll(own, turn, 1) if turn else own
                    halves.append(jnp.where(masks[tap], moved, 0.0))
                taps[pair * 16 : (pair + 1) * 16, brick * 128 : (brick + 1) * 128] = (
                    jnp.concatenate(halves, axis=0).astype(BF)
                )
        lifted[:, part] = jnp.dot(weight, taps[:, part], preferred_element_type=F4)
        for row in range(0, C, 16):
            rows = slice(row, row + 16)
            total = None
            for at in range(start, start + SPAN, 128):
                value = lifted[rows, at : at + 128]
                total = value if total is None else total + value
                square = value * value if at == start else square + value * value
            sums[rows, :] = total if start == 0 else sums[rows, :] + total
            squares[rows, :] = square if start == 0 else squares[rows, :] + square
    mean = jnp.sum(sums[...], axis=1, keepdims=True) / CELLS
    spread = jnp.sum(squares[...], axis=1, keepdims=True) / CELLS - mean * mean
    means[...] = jnp.broadcast_to(mean, (C, 128))
    scales[...] = lax.rsqrt(spread + 1e-05) * gain_ref[...]

    @pl.loop(0, CELLS // SPAN)
    def _(index):
        for row in range(0, C, 16):
            rows = slice(row, row + 16)
            mean, scale, shift = means[rows, :], scales[rows, :], shift_ref[rows, :]
            for at in range(0, SPAN, 128):
                part = pl.ds(pl.multiple_of(index * SPAN + at, 128), 128)
                normed = (lifted[rows, part] - mean) * scale + shift
                h_ref[rows, part] = gelu_value(normed).astype(BF)


def lift(arrived, weight, gain, shift):
    return pl.pallas_call(
        lift_kernel,
        out_shape=(
            jax.ShapeDtypeStruct((C, CELLS), BF),
            jax.ShapeDtypeStruct((16, CELLS), F4),
        ),
        scratch_shapes=[pltpu.VMEM((224, CELLS), BF), pltpu.VMEM((C, CELLS), F4)]
        + [pltpu.VMEM((C, 128), F4)] * 4,
        name="lift",
        compiler_params=pltpu.CompilerParams(vmem_limit_bytes=40 * MIB),
    )(arrived, weight, gain, shift)


def train_kernel(
    steps,
    layers,
    col_ref,
    h_ref,
    target_ref,
    mine_ref,
    other_ref,
    out_ref,
    send_ref,
    keep_ref,
    mix_ref,
    mix_back,
    states,
    slopes,
    ahead,
    back,
    inner,
    total,
):
    step = pl.program_id(0)
    cells = h_ref.shape[1]
    parts = [slice(start, start + 256) for start in range(0, cells, 256)]

    @pl.when(step == 0)
    def _():
        total[...] = jnp.zeros_like(total)
        even = col_ref[0] == 0
        upper = iota((8, 128), 0) < 4
        for pair in range(16):
            rows = slice(pair * 2 * BLOCK_ROWS, (pair + 1) * 2 * BLOCK_ROWS)
            mine = mine_ref[rows, :].astype(F4)
            other = other_ref[rows, :].astype(F4)
            tiles = []
            for start in (16, BLOCK_ROWS + 16):
                sides = ([], [])
                for index in range(7):
                    at = slice(start + index * 8, start + index * 8 + 8)
                    sides[0].append(jnp.where(even, mine[at], other[at]))
                    sides[1].append(jnp.where(even, other[at], mine[at]))
                left, right = unpack_piece(sides[0]), unpack_piece(sides[1])
                middle = [jnp.where(upper, a, b) for a, b in zip(left[2], right[2])]
                tiles += [left[0], left[1], middle, right[0], right[1]]
            for lanes in range(3):
                width = min(C - lanes * 128, 128)
                column = jnp.concatenate([tile[lanes] for tile in tiles], axis=0).astype(BF)
                mix_ref[pair * 80 : (pair + 1) * 80, lanes * 128 : lanes * 128 + width] = column[
                    :, 0:width
                ]
        same = (iota((C, C), 0) == iota((C, C), 1)).astype(F4).astype(BF)
        for layer in range(1, layers):
            rows = slice(layer * C, (layer + 1) * C)
            mix_back[rows, :] = lax.dot_general(
                mix_ref[rows, :], same, (((0,), (0,)), ((), ())), preferred_element_type=F4
            ).astype(BF)

    def state(layer):
        return h_ref if layer == 0 else states.at[layer - 1]

    for layer in range(layers):
        for part in parts:
            ahead[:, part] = jnp.dot(
                mix_ref[layer * C : (layer + 1) * C, :],
                state(layer)[:, part],
                preferred_element_type=F4,
            )
        for part in parts:
            for start in range(0, C, 16):
                rows = slice(start, start + 16)
                value, slope = gelu_both(ahead[rows, part])
                slopes[layer, rows, part] = slope
                states[layer, rows, part] = (state(layer)[rows, part].astype(F4) + value).astype(BF)
    def descend(layer, part, change, first):
        for start in range(0, C, 16):
            rows = slice(start, start + 16)
            value = change[start : start + 16]
            if not first:
                value = back[rows, part] + value
            if layer > 0:
                back[rows, part] = value
            inner[layer, rows, part] = (value * slopes[layer, rows, part]).astype(BF)

    for part in parts:
        output = jnp.dot(out_ref[...], states[layers - 1, :, part], preferred_element_type=F4)
        delta = ((output - target_ref[:, part]) * (2.0 / 384.0)).astype(BF)
        change = lax.dot_general(
            out_ref[...], delta, (((0,), (0,)), ((), ())), preferred_element_type=F4
        )
        descend(layers - 1, part, change, True)
    for layer in range(layers - 1, -1, -1):
        rows_of = slice(layer * C, (layer + 1) * C)
        total[rows_of, 0:C] += lax.dot_general(
            inner[layer], state(layer)[...], (((1,), (1,)), ((), ())), preferred_element_type=F4
        )
        if layer > 0:
            for part in parts:
                change = jnp.dot(
                    mix_back[rows_of, :], inner[layer, :, part], preferred_element_type=F4
                )
                descend(layer - 1, part, change, False)

    @pl.when(step == steps - 1)
    def _():
        col = col_ref[0]
        for piece in range(32):
            for ref, side in ((keep_ref, col), (send_ref, 1 - col)):

                def tile(index, lanes):
                    start = piece * 40 + 16
                    if index < 2:
                        start = pl.multiple_of(piece * 40 + 24 * side + 8 * index, 8)
                    return total[pl.ds(start, 8), lanes * 128 : (lanes + 1) * 128]

                packed = pack_piece(tile, own_half(side))
                for index in range(7):
                    start = piece * WEIGHT_ROWS + index * 8
                    ref[start : start + 8, :] = packed[index]


def train(col, h, target, mine, other, out_weight):
    cells = 1024
    steps = CELLS // cells
    layers = 4
    block = pl.BlockSpec((32 * BLOCK_ROWS, 128), lambda i: (0, 0))
    return pl.pallas_call(
        functools.partial(train_kernel, steps, layers),
        grid=(steps,),
        in_specs=[
            pl.BlockSpec(memory_space=pltpu.SMEM),
            pl.BlockSpec((C, cells), lambda i: (0, i)),
            pl.BlockSpec((16, cells), lambda i: (0, i)),
            block,
            block,
            pl.BlockSpec((16, C), lambda i: (0, 0)),
        ],
        out_specs=(
            pl.BlockSpec((32 * WEIGHT_ROWS, 128), lambda i: (0, 0)),
            pl.BlockSpec((32 * WEIGHT_ROWS, 128), lambda i: (0, 0)),
        ),
        out_shape=(
            jax.ShapeDtypeStruct((32 * WEIGHT_ROWS, 128), F4),
            jax.ShapeDtypeStruct((32 * WEIGHT_ROWS, 128), F4),
        ),
        scratch_shapes=[
            pltpu.VMEM((layers * C, C), BF),
            pltpu.VMEM((layers * C, C), BF),
            pltpu.VMEM((layers, C, cells), BF),
            pltpu.VMEM((layers, C, cells), F4),
            pltpu.VMEM((C, cells), F4),
            pltpu.VMEM((C, cells), F4),
            pltpu.VMEM((layers, C, cells), BF),
            pltpu.VMEM((layers * C, WIDE), F4),
        ],
        name="train",
        compiler_params=pltpu.CompilerParams(vmem_limit_bytes=48 * MIB),
    )(col, h, target, mine, other, out_weight)


def scale_kernel(keep_ref, other_ref, out_ref):
    peak = jnp.zeros((8, 128), F4)
    for start in range(0, 32 * WEIGHT_ROWS, 8):
        value = keep_ref[start : start + 8, :] + other_ref[start : start + 8, :]
        out_ref[start : start + 8, :] = value
        peak = jnp.maximum(peak, jnp.abs(value))
    peak = jnp.max(jnp.max(peak, axis=1, keepdims=True), axis=0, keepdims=True)
    power = jnp.ceil(jnp.log2(jnp.maximum(peak, 1e-30)))
    scale = jnp.broadcast_to(jnp.exp2(TOP_POWER - power), (8, 128))
    power = jnp.broadcast_to(power, (8, 128))
    free = iota((8, 128), 1) == 127
    for start in range(0, 32 * WEIGHT_ROWS, 8):
        value = out_ref[start : start + 8, :] * scale
        if start % WEIGHT_ROWS == 48:
            value = jnp.where(free, power, value)
        out_ref[start : start + 8, :] = value


def scaled(keep, other):
    return pl.pallas_call(
        scale_kernel,
        out_shape=jax.ShapeDtypeStruct((32 * WEIGHT_ROWS, 128), F4),
        name="scaled",
        compiler_params=pltpu.CompilerParams(vmem_limit_bytes=16 * MIB),
    )(keep, other)


def update_kernel(col_ref, own_ref, other_ref, state_ref, new_ref, first_out, second_out):
    packed = own_ref[...] + other_ref[...]
    parts = unpack_piece([packed[index * 8 : index * 8 + 8] for index in range(7)])
    full, rest, half = [jnp.concatenate(part, axis=1) for part in parts]
    even = col_ref[0] == 0
    lower = jnp.concatenate([full, rest, half], axis=0)
    upper = pltpu.roll(jnp.concatenate([half, full, rest], axis=0), 20, 0)
    gradient = jnp.where(even, lower, upper)[0:20, 0:C]
    master = state_ref[0]
    first_next = 0.9 * state_ref[1] + 0.1 * gradient
    second_next = 0.999 * state_ref[2] + 0.001 * gradient * gradient
    ratio = first_next / (1.0 - 0.9**10) / (jnp.sqrt(second_next / (1.0 - 0.999**10)) + 1e-08)
    new_ref[...] = master - 0.01 * (ratio + 0.1 * master)
    first_out[...] = first_next
    second_out[...] = second_next


def update(col, own, other, state):
    vector = pl.BlockSpec(memory_space=pltpu.VMEM)
    return pl.pallas_call(
        update_kernel,
        in_specs=[pl.BlockSpec(memory_space=pltpu.SMEM)] + [vector] * 3,
        out_specs=(vector,) * 3,
        out_shape=(jax.ShapeDtypeStruct((20, C), F4),) * 3,
        name="update",
        compiler_params=pltpu.CompilerParams(vmem_limit_bytes=16 * MIB),
    )(col, own, other, state)


def body(
    populations,
    relaxation,
    send_lists,
    lift_weight,
    norm_gain,
    norm_shift,
    mix_master,
    mix_first,
    mix_second,
    out_weight,
):
    every = ("sec", "row", "col")
    size = lax.axis_size(every)
    swap = [(0, 1), (1, 0)]
    col = lax.axis_index("col").astype(I4)[None]
    up = [(i, (i + 1) % size) for i in range(size)]
    last, initial, populations = planes(populations)
    behind = lax.ppermute(initial, every, [(j, i) for i, j in up])
    before = lax.ppermute(last, every, up)
    small = gathered_rows(norm_gain, norm_shift, send_lists, out_weight, mix_master, lift_weight)
    old, select, weights, lift_rows, gain, shift, out_rows = prepare(col, populations, small)
    outgoing = route(populations, before, behind, old, select, weights)
    arrived = lax.all_to_all(
        outgoing.reshape(32, BLOCK_ROWS, 128), "row", split_axis=0, concat_axis=0, tiled=True
    ).reshape(32 * BLOCK_ROWS, 128)
    after, state = collide(
        populations, before, behind, relaxation, mix_master, mix_first, mix_second
    )
    other = lax.ppermute(arrived, "col", swap)
    h, target = lift(arrived, lift_rows, gain, shift)
    send, keep = train(col, h, target, arrived, other, out_rows)
    half = scaled(keep, lax.ppermute(send, "col", swap)).reshape(32, WEIGHT_ROWS, 128)
    terms = lax.all_to_all(
        half.astype(jnp.float16), "row", split_axis=0, concat_axis=0, tiled=True
    ).astype(F4)
    summed = jnp.sum(terms * jnp.exp2(terms[:, 48:49, 127:128] - TOP_POWER), axis=0)
    across = lax.ppermute(summed, "sec", swap)
    new_master, new_first, new_second = update(col, summed, across, state)
    return (after, new_master, new_first, new_second)


def solution(mesh):
    in_specs = (
        P(None, ("sec", "row", "col"), None),
        P(("sec", "row", "col"), None),
        P(("sec", "row", "col"), None),
        P(),
        P(),
        P(),
        P(("row", "col"), None),
        P(("row", "col"), None),
        P(("row", "col"), None),
        P(),
    )
    out_specs = (
        P(None, ("sec", "row", "col"), None),
        P(("row", "col"), None),
        P(("row", "col"), None),
        P(("row", "col"), None),
    )
    return jax.shard_map(body, mesh=mesh, in_specs=in_specs, out_specs=out_specs, check_vma=False)
```
